32 devices in a mesh: dp: 8 (over y, x, core), head: 4 (over z).
Axes of the slice: x: 2, y: 2, z: 4, core: 2. Of those that a mesh axis runs over, the one named last changes fastest.
Arguments:
- tokens: bfloat16 [512, 32, 768], P('head', 'dp'), may hold values from -6 to 6
- lengths: int32 [32], P('dp'), may hold values from 20 to 512, as said below
- ranges: int32 [4], replicated, may hold values from 32 to 96
- qkv_weight: bfloat16 [3, 768, 768], replicated, may hold values from -0.21875 to 0.21875
- qv_bias: bfloat16 [2, 768], replicated, may hold values from -1.796875 to 1.796875
- out_weight: bfloat16 [768, 768], replicated, may hold values from -1.75 to 1.75
- out_bias: bfloat16 [768], replicated, may hold values from -1.796875 to 1.796875
- norm_gains: bfloat16 [2, 768], replicated, may hold values from 0.5 to 1.5
- norm_shifts: bfloat16 [2, 768], replicated, may hold values from -1.796875 to 1.796875
- ffn_in: bfloat16 [768, 3072], replicated, may hold values from -0.21875 to 0.21875
- ffn_in_bias: bfloat16 [3072], replicated, may hold values from -1.796875 to 1.796875
- ffn_out: bfloat16 [3072, 768], replicated, may hold values from -0.109375 to 0.109375
- ffn_out_bias: bfloat16 [768], replicated, may hold values from -1.796875 to 1.796875
- cotangent: bfloat16 [512, 32, 768], P('head', 'dp'), may hold values from -6 to 6
Outputs:
- output: bfloat16 [512, 32, 768], P('head', 'dp')
- grad_tokens: float32 [512, 32, 768], P('head', 'dp')
- grad_qkv_weight: float32 [3, 768, 768], P(None, 'dp')
- grad_qv_bias: float32 [2, 768], P(None, 'dp')
- grad_out_weight: float32 [768, 768], P('dp')
- grad_out_bias: float32 [768], P('dp')
- grad_norm_gains: float32 [2, 768], P(None, 'dp')
- grad_norm_shifts: float32 [2, 768], P(None, 'dp')
- grad_ffn_in: float32 [768, 3072], P('dp')
- grad_ffn_in_bias: float32 [3072], P('dp')
- grad_ffn_out: float32 [3072, 768], P('dp')
- grad_ffn_out_bias: float32 [768], P('dp')
The draws below stay inside these ranges and needn't reach their ends.
Inputs may be any that keep to these rules, and one draw needn't show every extreme that they name: `lengths`: in every group of 4 consecutive sequences one has exactly 512 tokens.
All inputs are finite; a program needn't handle non-finite values.
Results may differ from the reference program's by a relative error of at most 0.017.
Values may be sent and summed in bfloat16 or wider, within the bound.
A program may use at most 192 MiB of HBM per device.

```python
from functools import partial
import jax
import jax.numpy as jnp
from jax import lax

D = 768
HEADS = 12
HEAD_DIM = 64
FF = 3072
LEN = 512
MIN_LEN = 20
SEQ_GRP = 4
SEQS = 32
N_DP = 8


def draw_lengths(key, part):
    key = jax.random.fold_in(key, 7)
    cap_key, share_key, full_key = jax.random.split(key, 3)
    groups = SEQS // SEQ_GRP
    caps = jax.random.randint(cap_key, (groups, 1), LEN // 2, LEN + 1)
    shares = jax.random.randint(share_key, (groups, SEQ_GRP), 0, 1025)
    drawn = MIN_LEN + (caps - MIN_LEN) * shares // 1024
    chosen = jax.random.randint(full_key, (groups, 1), 0, SEQ_GRP)
    slots = jnp.arange(SEQ_GRP)[None, :]
    return jnp.where(slots == chosen, LEN, drawn).reshape(SEQS).astype(jnp.int32)


def set_ends(result, rng, smallest, top_value):
    longest = result.shape.index(max(result.shape))
    spots = []
    for shift in (0, 1):
        where = [jax.random.randint(jax.random.fold_in(rng, axis), (), 0, length) for axis, length in enumerate(result.shape)]
        where[longest] = (where[longest] + shift) % result.shape[longest]
        spots.append(tuple(where))
    return result.at[spots[0]].set(smallest).at[spots[1]].set(top_value)


def block_levels(stream_key, dims, cuts, least, largest):
    loudness = 1.0
    for dim, parts in cuts:
        steps = jax.random.uniform(jax.random.fold_in(jax.random.fold_in(stream_key, 6), dim), (parts,), jnp.float32, least / len(cuts), largest / len(cuts))
        loudness = loudness * jnp.repeat(jnp.exp(steps), dims[dim] // parts).reshape((-1,) + (1,) * (len(dims) - 1 - dim))
    return loudness


def scatter_about(key, dims, deviation, limit, shards=(), held_as=jnp.bfloat16):
    loudness = block_levels(key, dims, shards, -0.22, 0.18) if shards else 1.0
    entries = jax.random.normal(key, dims, jnp.float32) * deviation * loudness
    return jnp.minimum(jnp.maximum(entries, -limit), limit).astype(held_as)


def setup_inputs(seed: int = 0) -> dict:
    key_list = jax.random.split(jax.random.key(seed), 15)
    return {
        "tokens": scatter_about(key_list[0], (LEN, SEQS, D), 1.0, 6.0, ((0, 4), (1, 8))),
        "lengths": draw_lengths(jax.random.fold_in(key_list[14], 71), 0),
        "ranges": set_ends(jax.random.randint(key_list[2], (4,), 32, 97), jax.random.fold_in(key_list[2], 1), 32, 96).astype(jnp.int32),
        "qkv_weight": scatter_about(key_list[3], (3, D, D), D ** -0.5, 0.21875),
        "qv_bias": scatter_about(key_list[4], (2, D), 0.3, 1.796875),
        "out_weight": scatter_about(key_list[5], (D, D), (max(D // 64, 1)) ** -0.5, 1.75),
        "out_bias": scatter_about(key_list[6], (D,), 0.3, 1.796875),
        "norm_gains": jnp.clip(1.0 + 0.1 * jax.random.normal(key_list[7], (2, D), jnp.float32), 0.5, 1.5).astype(jnp.bfloat16),
        "norm_shifts": scatter_about(key_list[8], (2, D), 0.3, 1.796875),
        "ffn_in": scatter_about(key_list[9], (D, FF), D ** -0.5, 0.21875),
        "ffn_in_bias": scatter_about(key_list[10], (FF,), 0.3, 1.796875),
        "ffn_out": scatter_about(key_list[11], (FF, D), FF ** -0.5, 0.109375),
        "ffn_out_bias": scatter_about(key_list[12], (D,), 0.3, 1.796875),
        "cotangent": scatter_about(key_list[13], (LEN, SEQS, D), 1.0, 6.0, ((0, 4), (1, 8))),
    }


@jax.custom_vjp
def low(v):
    return lax.optimization_barrier(v.astype(jnp.bfloat16)).astype(jnp.float32)

@jax.custom_vjp
def low_back(v):
    return v

def low_keep(v):
    return (low(v), None)

def low_pass(kept, grad):
    return (grad,)

def back_keep(v):
    return (v, None)

def back_low(kept, grad):
    return (low(grad),)
low.defvjp(low_keep, low_pass)
low_back.defvjp(back_keep, back_low)
HIGH = lax.Precision.HIGHEST

def matmul(left, right):
    return jnp.dot(left, right, precision=HIGH)

def soft_clip(value, bound):
    return bound * jnp.tanh(value / bound)

def layer_norm(value, gain, shift):
    center = value - lax.optimization_barrier(jnp.mean(value, axis=-1, keepdims=True))
    spread = lax.optimization_barrier(jnp.mean(center * center, axis=-1, keepdims=True))
    return center * lax.rsqrt(spread + 1e-05) * gain + shift

def attend(queries, key_rows, values, length):
    scores = jnp.einsum('ihe,jhe->hij', queries, key_rows, precision=HIGH) * HEAD_DIM ** (-0.5)
    scores = low_back(scores)
    live = jnp.arange(LEN) < length
    masked = jnp.where(live[None, None, :], scores, -1000000000.0)
    probs = low(jax.nn.softmax(masked, axis=-1))
    return jnp.einsum('hij,jhe->ihe', probs, values, precision=HIGH)

def group_layer(params, bounds, pieces):
    qkv_w, qv_b, out_w, out_b, gains, shifts, w_in, b_in, w_out, b_out = params
    block_tokens, block_lengths = pieces
    token_rows = block_tokens.reshape(LEN * SEQ_GRP, D)
    quant_in = low(soft_clip(token_rows, bounds[0]))
    queries = low_back(low(matmul(quant_in, qkv_w[0]) + qv_b[0]))
    key_rows = low_back(low(matmul(quant_in, qkv_w[1])))
    values = low_back(low(matmul(quant_in, qkv_w[2]) + qv_b[1]))
    shape_four = (LEN, SEQ_GRP, HEADS, HEAD_DIM)
    context = jax.vmap(attend, in_axes=(1, 1, 1, 0), out_axes=1)(queries.reshape(shape_four), key_rows.reshape(shape_four), values.reshape(shape_four), block_lengths)
    context = low_back(low(context.reshape(LEN * SEQ_GRP, D)))
    quant_ctx = low(soft_clip(context, bounds[1]))
    attn_out = low_back(matmul(quant_ctx, out_w) + out_b)
    hidden = layer_norm(token_rows + attn_out, gains[0], shifts[0])
    quant_h = low(soft_clip(hidden, bounds[2]))
    pre = low_back(matmul(quant_h, w_in) + b_in)
    act = low(soft_clip(jax.nn.gelu(pre, approximate=True), bounds[3]))
    branch = low_back(matmul(act, w_out) + b_out)
    normed = layer_norm(hidden + branch, gains[1], shifts[1])
    return normed.reshape(LEN, SEQ_GRP, D)

def reference(tokens, lengths, ranges, qkv_weight, qv_bias, out_weight, out_bias, norm_gains, norm_shifts, ffn_in, ffn_in_bias, ffn_out, ffn_out_bias, cotangent):
    bounds = ranges.astype(jnp.float32) / 16.0
    group_lengths = lengths.reshape(N_DP, SEQ_GRP)

    def forward(inputs, *params):
        blocks = jnp.moveaxis(inputs.reshape(LEN, N_DP, SEQ_GRP, D), 1, 0)
        mapped = lax.map(jax.checkpoint(partial(group_layer, params, bounds)), (blocks, group_lengths))
        return jnp.moveaxis(mapped, 0, 1).reshape(LEN, N_DP * SEQ_GRP, D)
    floats = [a.astype(jnp.float32) for a in (tokens, qkv_weight, qv_bias, out_weight, out_bias, norm_gains, norm_shifts, ffn_in, ffn_in_bias, ffn_out, ffn_out_bias)]
    normed, pullback = jax.vjp(forward, *floats)
    grads = pullback(cotangent.astype(jnp.float32))
    return (normed.astype(jnp.bfloat16), grads[0], grads[1], grads[2], grads[3], grads[4], grads[5], grads[6], grads[7], grads[8], grads[9], grads[10])
```

```python
import functools
import jax
import jax.numpy as jnp
from jax import lax
from jax.experimental import pallas as pl
from jax.experimental.pallas import tpu as pltpu
from jax.sharding import PartitionSpec as P

F32, BF = jnp.float32, jnp.bfloat16
L, D, F, NP = 512, 768, 3072, 6
GC0, GC1 = 0.7978845608028654, 0.044715

def nn(a, b):
    return lax.dot_general(a, b, (((1,), (0,)), ((), ())), preferred_element_type=F32)
def nt(a, b):
    return lax.dot_general(a, b, (((1,), (1,)), ((), ())), preferred_element_type=F32)
def tn(a, b):
    return lax.dot_general(a, b, (((0,), (0,)), ((), ())), preferred_element_type=F32)

def rows_loop(n, step, f):
    def it(r, c):
        f(pl.multiple_of(r * step, step))
        return c
    lax.fori_loop(0, n // step, it, 0)

def mean(v):
    return jnp.sum(v, axis=-1, keepdims=True) * (1.0 / D)

def qkv(x_ref, qi_ref, w_ref, qvb_ref, q_ref, k_ref, v_ref, qt_ref, kt_ref, vt_ref, b0, r0, rows):
    xb = x_ref[rows, :].astype(F32)
    qi = (b0 * jnp.tanh(xb * r0)).astype(BF)
    qi_ref[rows, :] = qi
    for m, (dst, tdst) in enumerate(((q_ref, qt_ref), (k_ref, kt_ref), (v_ref, vt_ref))):
        y = nn(qi, w_ref[m])
        if m == 0:
            y = (y + qvb_ref[0:1, :].astype(F32)).astype(BF).astype(F32) * 0.125
        if m == 2:
            y = y + qvb_ref[1:2, :].astype(F32)
        for p in range(NP):
            yp = y[:, p * 128:(p + 1) * 128].astype(BF)
            dst[p, rows, :] = yp
            tdst[p, :, rows] = yp.T

def attn_fwd(q_t, k_ref, v_t, p_ref, ctxt_ref, length):
    live = lax.broadcasted_iota(jnp.int32, (L, L), 0) < length
    low = lax.broadcasted_iota(jnp.int32, (128, L), 0) < 64
    def pair(p, c):
        kp = k_ref[p]
        qt = q_t[p]
        vt = v_t[p]
        for t in range(2):
            qm = jnp.where(low if t == 0 else ~low, qt, jnp.zeros_like(qt))
            s = nn(kp, qm)
            s = jnp.where(live, s, -1e9)
            e = jnp.exp(s - jnp.max(s, axis=0, keepdims=True))
            pr = (e * (1.0 / jnp.sum(e, axis=0, keepdims=True))).astype(BF)
            p_ref[2 * p + t] = pr
            ctxt_ref[p, 64 * t:64 * t + 64, :] = nn(vt[64 * t:64 * t + 64, :], pr).astype(BF)
        return c
    lax.fori_loop(0, NP, pair, 0)

def out_proj(ctxt_ref, x_ref, wo_ref, ob_ref, nv_ref, qct_ref, slc_ref, n1_ref, r1_ref, hid_ref, slh_ref, qh_ref, b1, i1, b2, i2):
    for p in range(NP):
        ct = ctxt_ref[p].astype(F32)
        th = jnp.tanh(ct * i1)
        qct_ref[p * 128:(p + 1) * 128, :] = (b1 * th).astype(BF)
        slc_ref[:, p * 128:(p + 1) * 128] = (1.0 - th * th).T
    g1, s1 = nv_ref[0:1, :].astype(F32), nv_ref[2:3, :].astype(F32)
    ob = ob_ref[...].astype(F32)
    hid_ref[...] = tn(qct_ref[...], wo_ref[...])
    def f(r):
        rows = pl.ds(r, 64)
        v = hid_ref[rows, :] + ob + x_ref[rows, :].astype(F32)
        c = v - mean(v)
        rr = lax.rsqrt(mean(c * c) + 1e-5)
        n = c * rr
        n1_ref[rows, :] = n
        r1_ref[rows, :] = jnp.broadcast_to(rr, (64, 128))
        h = n * g1 + s1
        hid_ref[rows, :] = h
        th = jnp.tanh(h * i2)
        qh_ref[rows, :] = (b2 * th).astype(BF)
        slh_ref[rows, :] = 1.0 - th * th
    rows_loop(L, 64, f)

def ffn_fwd(qh_ref, win_ref, wout_ref, fib_ref, act_ref, dfac_ref, acc_ref, b3, i3):
    acc_ref[...] = jnp.zeros_like(acc_ref)
    RB = 256
    def chunk(c, _):
        bias = fib_ref[c].astype(F32)
        for r in range(0, L, RB):
            rows = slice(r, r + RB)
            t = nn(qh_ref[rows, :], win_ref[c]) + bias
            t2 = t * t
            th = jnp.tanh(t * (GC0 + (GC0 * GC1) * t2))
            hp = 0.5 + 0.5 * th
            u = t * hp
            cl = jnp.tanh(u * i3)
            act = (b3 * cl).astype(BF)
            d = hp + u * (1.0 - th) * (GC0 + (3 * GC0 * GC1) * t2)
            act_ref[c, rows, :] = act
            dfac_ref[c, rows, :] = (d * (1.0 - cl * cl)).astype(BF)
            acc_ref[rows, :] += nn(act, wout_ref[c])
        return _
    lax.fori_loop(0, 4, chunk, 0)

def colsum_acc(vec_ref, row, val):
    vec_ref[row:row + 1, :] += jnp.sum(val, axis=0, keepdims=True)

def ln2(acc_ref, hid_ref, ct_ref, fob_ref, nv_ref, out_ref, gs_ref, gb_ref, gbt, vec_ref):
    g2, s2 = nv_ref[1:2, :].astype(F32), nv_ref[3:4, :].astype(F32)
    fob = fob_ref[...].astype(F32)
    def f(r):
        rows = pl.ds(r, 64)
        v = acc_ref[rows, :] + fob + hid_ref[rows, :]
        c = v - mean(v)
        rr = lax.rsqrt(mean(c * c) + 1e-5)
        n = c * rr
        out_ref[rows, :] = (n * g2 + s2).astype(BF)
        ct = ct_ref[rows, :].astype(F32)
        cn = ct * n
        colsum_acc(vec_ref, 4, cn)
        colsum_acc(vec_ref, 6, ct)
        q = ct * g2
        gs = rr * (q - mean(q) - n * mean(q * n))
        gs_ref[rows, :] = gs
        gb = gs.astype(BF)
        gb_ref[rows, :] = gb
        colsum_acc(vec_ref, 7, gb.astype(F32))
    rows_loop(L, 64, f)

def ffn_bwd(gb_ref, qh_ref, win_ref, wout_ref, act_ref, dfac_ref, acc_ref, qht_ref, gfo, gfi, vec_ref):
    for p in range(NP):
        qht_ref[p * 128:(p + 1) * 128, :] = qh_ref[:, p * 128:(p + 1) * 128].T
    acc_ref[...] = jnp.zeros_like(acc_ref)
    def chunk(c, _):
        gfo(c, tn(act_ref[c], gb_ref[...]))
        return _
    lax.fori_loop(0, 4, chunk, 0)
    def chunk2(c, _):
        for r in range(0, L, 256):
            rows = slice(r, r + 256)
            ga = nt(gb_ref[rows, :], wout_ref[c])
            gp = (ga * dfac_ref[c, rows, :].astype(F32)).astype(BF)
            dfac_ref[c, rows, :] = gp
            vec_ref[pl.ds(8 + c, 1), :] += jnp.sum(gp.astype(F32), axis=0, keepdims=True)
            acc_ref[rows, :] += nt(gp, win_ref[c])
        gfi(c, nn(qht_ref[...], dfac_ref[c]))
        return _
    lax.fori_loop(0, 4, chunk2, 0)

def ln1_bwd(acc_ref, gs_ref, slh_ref, n1_ref, r1_ref, nv_ref, gat_ref, vec_ref):
    g1 = nv_ref[0:1, :].astype(F32)
    def f(r):
        rows = pl.ds(r, 64)
        gh = gs_ref[rows, :] + acc_ref[rows, :] * slh_ref[rows, :]
        n = n1_ref[rows, :]
        colsum_acc(vec_ref, 3, gh * n)
        colsum_acc(vec_ref, 5, gh)
        q = gh * g1
        gs = r1_ref[rows, 0:1] * (q - mean(q) - n * mean(q * n))
        gs_ref[rows, :] = gs
        gat = gs.astype(BF)
        gat_ref[rows, :] = gat
        colsum_acc(vec_ref, 2, gat.astype(F32))
    rows_loop(L, 64, f)

def out_bwd(gat_ref, wo_ref, qct_ref, slc_ref, dc_ref, dct_ref, go):
    go(nn(qct_ref[...], gat_ref[...]))
    g = nt(gat_ref[...], wo_ref[...])
    for p in range(NP):
        cols = slice(p * 128, (p + 1) * 128)
        d = (g[:, cols] * slc_ref[:, cols]).astype(BF)
        dc_ref[p] = d
        dct_ref[p] = d.T

def attn_bwd(q_ref, k_t, v_ref, dc_ref, dc_t, p_ref, dq_ref, dk_ref, dv_ref):
    low = lax.broadcasted_iota(jnp.int32, (128, L), 0) < 64
    lane_low = lax.broadcasted_iota(jnp.int32, (L, 128), 1) < 64
    def pair(p, c):
        qp, kt, vp, dc, dct = q_ref[p], k_t[p], v_ref[p], dc_ref[p], dc_t[p]
        res = []
        for t in range(2):
            dm = jnp.where(low if t == 0 else ~low, dct, jnp.zeros_like(dct))
            dp = nn(vp, dm)
            pr = p_ref[2 * p + t]
            prf = pr.astype(F32)
            delta = jnp.sum(dp * prf, axis=0, keepdims=True)
            ds = (prf * (dp - delta)).astype(BF)
            dv = nn(pr, dc)
            dk = nn(ds, qp)
            dqt = nn(kt[64 * t:64 * t + 64, :], ds) * 0.125
            res.append((dv, dk, dqt))
        dv_ref[p] = jnp.where(lane_low, res[0][0], res[1][0]).astype(BF)
        dk_ref[p] = jnp.where(lane_low, res[0][1], res[1][1]).astype(BF)
        dq_ref[p] = jnp.concatenate([res[0][2], res[1][2]], axis=0).astype(BF).T
        return c
    lax.fori_loop(0, NP, pair, 0)

def qkv_bwd(qi_ref, qit_ref, x_ref, w_ref, dq_ref, dk_ref, dv_ref, gs_ref, acc_ref, gq, gx_ref, vec_ref, b0, i0):
    for p in range(NP):
        qit_ref[p * 128:(p + 1) * 128, :] = qi_ref[:, p * 128:(p + 1) * 128].T
    for m, ref in enumerate((dq_ref, dk_ref, dv_ref)):
        d = jnp.concatenate([ref[p] for p in range(NP)], axis=1)
        gq(m, nn(qit_ref[...], d))
        if m != 1:
            colsum_acc(vec_ref, 0 if m == 0 else 1, d.astype(F32))
        if m == 0:
            acc_ref[...] = nt(d, w_ref[m])
        else:
            acc_ref[...] += nt(d, w_ref[m])
    def f(r):
        rows = pl.ds(r, 64)
        th = jnp.tanh(x_ref[rows, :].astype(F32) * i0)
        gx_ref[rows, :] = (gs_ref[rows, :] + acc_ref[rows, :] * (1.0 - th * th)).astype(BF)
    rows_loop(L, 64, f)


class LaneSlots:
    def __init__(self, ref):
        self.ref = ref

    def __getitem__(self, p):
        return self.ref[0, :, pl.ds(pl.multiple_of(p * 128, 128), 128)]

    def __setitem__(self, p, value):
        self.ref[0, :, pl.ds(pl.multiple_of(p * 128, 128), 128)] = value


def kernel(x_ref, len_ref, rng_ref, wqkv_ref, qvb_ref, wo_ref, ob_ref, nv_ref, win_ref, fib_ref, wout_ref, fob_ref, ct_ref,
           out_ref, gx_ref, g_ref, vec_ref,
           qi_ref, q_ref, k_ref, v_ref, qt_ref, kt_ref, vt_ref, p_ref, ctxt_ref, qct_ref, slc_ref, n1_ref, r1_ref, hid_ref, slh_ref,
           qh_ref, act_ref, dfac_ref, acc_ref, gs_ref, gb_ref):
    b = [jnp.full((1, 1), rng_ref[i], jnp.int32).astype(F32) * (1 / 16.0) for i in range(4)]
    iv = [1.0 / t for t in b]
    vec_ref[...] = jnp.zeros_like(vec_ref)
    for r in range(0, L, 256):
        qkv(x_ref, qi_ref, wqkv_ref, qvb_ref, q_ref, k_ref, v_ref, qt_ref, kt_ref, vt_ref, b[0], iv[0], slice(r, r + 256))
    attn_fwd(qt_ref, k_ref, vt_ref, p_ref, ctxt_ref, len_ref[0])
    out_proj(ctxt_ref, x_ref, wo_ref, ob_ref, nv_ref, qct_ref, slc_ref, n1_ref, r1_ref, hid_ref, slh_ref, qh_ref, b[1], iv[1], b[2], iv[2])
    ffn_fwd(qh_ref, win_ref, wout_ref, fib_ref, act_ref, dfac_ref, acc_ref, b[3], iv[3])
    ln2(acc_ref, hid_ref, ct_ref, fob_ref, nv_ref, out_ref, gs_ref, gb_ref, None, vec_ref)

    def put(i):
        def f(c, v):
            g_ref[i + c] = v.astype(BF)
        return f

    ffn_bwd(gb_ref, qh_ref, win_ref, wout_ref, act_ref, dfac_ref, acc_ref, vt_ref.reshape(D, L), put(4), put(0), vec_ref)
    ln1_bwd(acc_ref, gs_ref, slh_ref, n1_ref, r1_ref, nv_ref, gb_ref, vec_ref)
    dc = LaneSlots(act_ref)
    out_bwd(gb_ref, wo_ref, qct_ref, slc_ref, dc, vt_ref, functools.partial(put(8), 0))
    attn_bwd(q_ref, kt_ref, v_ref, dc, vt_ref, p_ref, q_ref, k_ref, v_ref)
    qkv_bwd(qi_ref, qct_ref, x_ref, wqkv_ref, q_ref, k_ref, v_ref, gs_ref, acc_ref, put(9), gx_ref, vec_ref, b[0], iv[0])


def layer(*args):
    def vm(*s, d=BF):
        return pltpu.VMEM(s, d)
    scratch = [vm(L, D), vm(6, L, 128), vm(6, L, 128), vm(6, L, 128), vm(6, 128, L), vm(6, 128, L), vm(6, 128, L), vm(12, L, L),
               vm(6, 128, L), vm(D, L), vm(L, D, d=F32), vm(L, D, d=F32), vm(L, 128, d=F32), vm(L, D, d=F32), vm(L, D, d=F32),
               vm(L, D), vm(4, L, D), vm(4, L, D), vm(L, D, d=F32), vm(L, D, d=F32), vm(L, D)]
    outs = [jax.ShapeDtypeStruct((L, D), BF), jax.ShapeDtypeStruct((L, D), BF), jax.ShapeDtypeStruct((12, D, D), BF),
            jax.ShapeDtypeStruct((16, D), F32)]
    v, s = pl.BlockSpec(memory_space=pltpu.VMEM), pl.BlockSpec(memory_space=pltpu.SMEM)
    return pl.pallas_call(
        kernel, out_shape=outs, in_specs=[v, s, s] + [v] * 10, out_specs=[v] * 4, scratch_shapes=scratch,
        compiler_params=pltpu.CompilerParams(vmem_limit_bytes=64 * 1024 * 1024 - 65536))(*args)


def on_device(n_dp, tokens, lengths, ranges, qkv_weight, qv_bias, out_weight, out_bias, norm_gains, norm_shifts, ffn_in, ffn_in_bias,
              ffn_out, ffn_out_bias, cotangent):
    def to_seq(a):
        return lax.all_to_all(a.transpose(1, 0, 2), "head", split_axis=0, concat_axis=1, tiled=True)[0]

    def to_pos(a):
        return lax.all_to_all(a[None], "head", split_axis=1, concat_axis=0, tiled=True).transpose(1, 0, 2)

    length = lax.dynamic_slice(lengths, (lax.axis_index("head"),), (1,))
    out, gx, g, vec = layer(
        to_seq(tokens), length, ranges, qkv_weight, qv_bias, out_weight, out_bias[None], jnp.concatenate([norm_gains, norm_shifts]),
        ffn_in.reshape(D, 4, D).transpose(1, 0, 2), ffn_in_bias.reshape(4, 1, D), ffn_out.reshape(4, D, D), ffn_out_bias[None],
        to_seq(cotangent))
    rs = D // n_dp
    wout = lax.psum_scatter(g[4:8].reshape(4 * D, D), "dp", scatter_dimension=0, tiled=True)
    rest = lax.psum_scatter(jnp.concatenate([g[0:4], g[8:12]]), "dp", scatter_dimension=1, tiled=True)
    both = lax.psum(jnp.concatenate([wout, rest.reshape(8 * rs, D)]), "head").astype(F32)
    wout, rest = both[:4 * rs], both[4 * rs:].reshape(8, rs, D)
    vec = lax.psum(vec, ("dp", "head"))
    i = lax.axis_index("dp")

    def mine(v):
        return lax.dynamic_slice_in_dim(v, i * rs, rs, axis=-1)
    fib = lax.dynamic_slice(vec[8:12].reshape(-1), (i * 4 * rs,), (4 * rs,))
    return (to_pos(out), to_pos(gx).astype(F32), rest[5:8], mine(vec[0:2]), rest[4], mine(vec[2]), mine(vec[3:5]), mine(vec[5:7]),
            rest[0:4].transpose(1, 0, 2).reshape(rs, F), fib, wout, mine(vec[7]))


def solution(mesh):
    tok = P("head", "dp", None)
    return jax.shard_map(
        functools.partial(on_device, mesh.shape["dp"]),
        mesh=mesh,
        in_specs=(tok, P("dp")) + (P(),) * 11 + (tok,),
        out_specs=(tok, tok, P(None, "dp", None), P(None, "dp"), P("dp", None), P("dp"), P(None, "dp"), P(None, "dp"),
                   P("dp", None), P("dp"), P("dp", None), P("dp")),
        check_vma=False,
    )
```

```python
import functools
import jax
import jax.numpy as jnp
from jax import lax
from jax.experimental import pallas as pl
from jax.experimental.pallas import tpu as pltpu
from jax.sharding import PartitionSpec as P

F32, BF = jnp.float32, jnp.bfloat16
L, D, F, NP = 512, 768, 3072, 6
GC0, GC1 = 0.7978845608028654, 0.044715


def nn(a, b):
    return lax.dot_general(a, b, (((1,), (0,)), ((), ())), preferred_element_type=F32)


def nt(a, b):
    return lax.dot_general(a, b, (((1,), (1,)), ((), ())), preferred_element_type=F32)


def tn(a, b):
    return lax.dot_general(a, b, (((0,), (0,)), ((), ())), preferred_element_type=F32)


def rows_loop(n, step, f):
    def it(r, c):
        f(pl.multiple_of(r * step, step))
        return c
    lax.fori_loop(0, n // step, it, 0)


def mean(v):
    return jnp.sum(v, axis=-1, keepdims=True) * (1.0 / D)


class LaneSlots:
    def __init__(self, ref):
        self.ref = ref

    def __getitem__(self, p):
        return self.ref[0, :, pl.ds(pl.multiple_of(p * 128, 128), 128)]

    def __setitem__(self, p, value):
        self.ref[0, :, pl.ds(pl.multiple_of(p * 128, 128), 128)] = value


def qkv(x_ref, qi_ref, w_ref, sm, q_ref, k_ref, v_ref, qt_ref, kt_ref, vt_ref, b0, r0, rows):
    xb = x_ref[rows, :].astype(F32)
    qi = (b0 * jnp.tanh(xb * r0)).astype(BF)
    qi_ref[rows, :] = qi
    for m, (dst, tdst) in enumerate(((q_ref, qt_ref), (k_ref, kt_ref), (v_ref, vt_ref))):
        y = nn(qi, w_ref[m])
        if m == 0:
            y = (y + sm[0:1, :]).astype(BF).astype(F32) * 0.125
        if m == 2:
            y = y + sm[1:2, :]
        for p in range(NP):
            yp = y[:, p * 128:(p + 1) * 128].astype(BF)
            dst[p, rows, :] = yp
            tdst[p, :, rows] = yp.T


def attn_fwd(q_t, k_ref, v_t, p_ref, ctxt_ref, length):
    live = lax.broadcasted_iota(jnp.int32, (L, L), 0) < length
    low = lax.broadcasted_iota(jnp.int32, (128, L), 0) < 64

    def pair(p, c):
        kp, qt, vt = k_ref[p], q_t[p], v_t[p]
        for t in range(2):
            qm = jnp.where(low if t == 0 else ~low, qt, jnp.zeros_like(qt))
            s = jnp.where(live, nn(kp, qm), -1e9)
            e = jnp.exp(s - jnp.max(s, axis=0, keepdims=True))
            pr = (e * (1.0 / jnp.sum(e, axis=0, keepdims=True))).astype(BF)
            p_ref[2 * p + t] = pr
            ctxt_ref[p, 64 * t:64 * t + 64, :] = nn(vt[64 * t:64 * t + 64, :], pr).astype(BF)
        return c
    lax.fori_loop(0, NP, pair, 0)


def out_proj(ctxt_ref, x_ref, wo_ref, sm, qct_ref, slc_ref, n1_ref, r1_ref, hid_ref, slh_ref, qh_ref, acc_ref, b1, i1, b2, i2):
    for p in range(NP):
        th = jnp.tanh(ctxt_ref[p].astype(F32) * i1)
        qct_ref[p * 128:(p + 1) * 128, :] = (b1 * th).astype(BF)
        slc_ref[:, p * 128:(p + 1) * 128] = (1.0 - th * th).astype(BF).T
    hid_ref[...] = tn(qct_ref[...], wo_ref[...])

    def f(r):
        rows = pl.ds(r, 64)
        v = hid_ref[rows, :] + sm[2:3, :] + x_ref[rows, :].astype(F32)
        c = v - mean(v)
        rr = lax.rsqrt(mean(c * c) + 1e-5)
        n = c * rr
        n1_ref[rows, :] = n
        r1_ref[rows, :] = jnp.broadcast_to(rr, (64, 128))
        h = n * sm[3:4, :] + sm[5:6, :]
        hid_ref[rows, :] = h
        th = jnp.tanh(h * i2)
        qh_ref[rows, :] = (b2 * th).astype(BF)
        slh_ref[rows, :] = (1.0 - th * th).astype(BF)
    rows_loop(L, 64, f)
    acc_ref[...] = jnp.zeros_like(acc_ref)


def ffn_fwd(qh_ref, w, sm, act_ref, dfac_ref, acc_ref, b3, i3, before, after):
    def chunk(c, _):
        s = before(c)
        bias = sm[pl.ds(8 + c, 1), :]
        for r in range(0, L, 256):
            rows = slice(r, r + 256)
            t = nn(qh_ref[rows, :], w[s]) + bias
            t2 = t * t
            th = jnp.tanh(t * (GC0 + (GC0 * GC1) * t2))
            hp = 0.5 + 0.5 * th
            u = t * hp
            cl = jnp.tanh(u * i3)
            act = (b3 * cl).astype(BF)
            d = hp + u * (1.0 - th) * (GC0 + (3 * GC0 * GC1) * t2)
            act_ref[c, rows, :] = act
            dfac_ref[c, rows, :] = (d * (1.0 - cl * cl)).astype(BF)
            acc_ref[rows, :] += nn(act, w[s + 1])
        after(c)
        return _
    lax.fori_loop(0, 4, chunk, 0)


def colsum(vec, row, val):
    vec[row:row + 1, :] += jnp.sum(val, axis=0, keepdims=True)


def ln2(acc_ref, hid_ref, ct_ref, sm, gb_ref, vec):
    def f(r):
        rows = pl.ds(r, 64)
        v = acc_ref[rows, :] + sm[7:8, :] + hid_ref[rows, :]
        c = v - mean(v)
        rr = lax.rsqrt(mean(c * c) + 1e-5)
        n = c * rr
        ct = ct_ref[rows, :].astype(F32)
        ct_ref[rows, :] = (n * sm[4:5, :] + sm[6:7, :]).astype(BF)
        colsum(vec, 4, ct * n)
        colsum(vec, 6, ct)
        q = ct * sm[4:5, :]
        gs = rr * (q - mean(q) - n * mean(q * n))
        hid_ref[rows, :] = gs
        gb = gs.astype(BF)
        gb_ref[rows, :] = gb
        colsum(vec, 7, gb.astype(F32))
    rows_loop(L, 64, f)


def ffn_bwd_out(gb_ref, qh_ref, act_ref, qht_ref, put):
    for p in range(NP):
        qht_ref[p * 128:(p + 1) * 128, :] = qh_ref[:, p * 128:(p + 1) * 128].T

    def chunk(c, _):
        put(c, tn(act_ref[c], gb_ref[...]))
        return _
    lax.fori_loop(0, 4, chunk, 0)


def ffn_bwd_in(c, gb_ref, win, wout, dfac_ref, acc_ref, qht_ref, put, vec):
    for r in range(0, L, 256):
        rows = slice(r, r + 256)
        gp = (nt(gb_ref[rows, :], wout[...]) * dfac_ref[c, rows, :].astype(F32)).astype(BF)
        dfac_ref[c, rows, :] = gp
        vec[pl.ds(8 + c, 1), :] += jnp.sum(gp.astype(F32), axis=0, keepdims=True)
        acc_ref[rows, :] += nt(gp, win[...])
    put(nn(qht_ref[...], dfac_ref[c]))


def ln1_bwd(acc_ref, gs_ref, slh_ref, n1_ref, r1_ref, sm, gat_ref, vec):
    def f(r):
        rows = pl.ds(r, 64)
        gh = gs_ref[rows, :] + acc_ref[rows, :] * slh_ref[rows, :].astype(F32)
        n = n1_ref[rows, :]
        colsum(vec, 3, gh * n)
        colsum(vec, 5, gh)
        q = gh * sm[3:4, :]
        gs = r1_ref[rows, 0:1] * (q - mean(q) - n * mean(q * n))
        gs_ref[rows, :] = gs
        gat = gs.astype(BF)
        gat_ref[rows, :] = gat
        colsum(vec, 2, gat.astype(F32))
    rows_loop(L, 64, f)


def out_bwd(gat_ref, wo_ref, qct_ref, slc_ref, dc_ref, dct_ref, put):
    put(nn(qct_ref[...], gat_ref[...]))
    g = nt(gat_ref[...], wo_ref[...])
    for p in range(NP):
        cols = slice(p * 128, (p + 1) * 128)
        d = (g[:, cols] * slc_ref[:, cols].astype(F32)).astype(BF)
        dc_ref[p] = d
        dct_ref[p] = d.T


def attn_bwd(q_ref, k_t, v_ref, dc_ref, dc_t, p_ref, dq_ref, dk_ref, dv_ref, service):
    low = lax.broadcasted_iota(jnp.int32, (128, L), 0) < 64
    lane_low = lax.broadcasted_iota(jnp.int32, (L, 128), 1) < 64

    def pair(p, c):
        qp, kt, vp, dc, dct = q_ref[p], k_t[p], v_ref[p], dc_ref[p], dc_t[p]
        res = []
        for t in range(2):
            dm = jnp.where(low if t == 0 else ~low, dct, jnp.zeros_like(dct))
            dp = nn(vp, dm)
            pr = p_ref[2 * p + t]
            prf = pr.astype(F32)
            delta = jnp.sum(dp * prf, axis=0, keepdims=True)
            ds = (prf * (dp - delta)).astype(BF)
            res.append((nn(pr, dc), nn(ds, qp), nn(kt[64 * t:64 * t + 64, :], ds) * 0.125))
        dv_ref[p] = jnp.where(lane_low, res[0][0], res[1][0]).astype(BF)
        dk_ref[p] = jnp.where(lane_low, res[0][1], res[1][1]).astype(BF)
        dq_ref[p] = jnp.concatenate([res[0][2], res[1][2]], axis=0).astype(BF).T
        service(p)
        return c
    lax.fori_loop(0, NP, pair, 0)


def qkv_bwd(qi_ref, qit_ref, x_ref, w_ref, dq_ref, dk_ref, dv_ref, gs_ref, acc_ref, put, vec, b0, i0):
    for p in range(NP):
        qit_ref[p * 128:(p + 1) * 128, :] = qi_ref[:, p * 128:(p + 1) * 128].T
    for m, ref in enumerate((dq_ref, dk_ref, dv_ref)):
        d = jnp.concatenate([ref[p] for p in range(NP)], axis=1)
        put(m, nn(qit_ref[...], d))
        if m != 1:
            colsum(vec, 0 if m == 0 else 1, d.astype(F32))
        if m == 0:
            acc_ref[...] = nt(d, w_ref[m])
        else:
            acc_ref[...] += nt(d, w_ref[m])

    def f(r):
        rows = pl.ds(r, 64)
        th = jnp.tanh(x_ref[rows, :].astype(F32) * i0)
        x_ref[rows, :] = (gs_ref[rows, :] + acc_ref[rows, :] * (1.0 - th * th)).astype(BF)
    rows_loop(L, 64, f)


MESH = pl.DeviceIdType.MESH


def fused_kernel(n_dp, tok, cot, len_ref, rng_ref, wqkv, wo, win, wout, sm,
                 outp, gxp, gw, vout,
                 w, g, x_ref, ct_ref, qi_ref, q_ref, k_ref, v_ref, qt_ref, kt_ref, vt_ref, p_ref, ctxt_ref, qct_ref, slc_ref,
                 n1_ref, r1_ref, hid_ref, slh_ref, qh_ref, act_ref, dfac_ref, acc_ref, gb_ref, za, vec, vrecv, *rest):
    nb = n_dp.bit_length() - 1
    bufs, (wsem, locsem, a2s, a2r, gs_sem, gr_sem, zs_sem, zr_sem, vs_sem, vr_sem) = rest[:nb], rest[nb:]
    rs, nz, SEG = D // n_dp, 4, L // 4
    dp, z = lax.axis_index("dp"), lax.axis_index("head")
    bit = [(dp // (1 << b)) % 2 for b in range(nb)]
    buddy = [dp + (1 - 2 * bit[b]) * (1 << b) for b in range(nb)]
    z_near, z_cross, z_far = z + 1 - 2 * (z % 2), 3 - z, (z + 2) % 4
    peers = (z_near, z_far, z_cross)
    inner = (z + 1) // 2 == 1

    def at(dpi, zi):
        return {"dp": dpi, "head": zi}

    def load_w(slot, src):
        return pltpu.make_async_copy(src, w.at[slot], wsem.at[slot])

    def win_c(c):
        return win.at[:, pl.ds(pl.multiple_of(c * D, D), D)]

    def wout_c(c):
        return wout.at[pl.ds(pl.multiple_of(c * D, D), D), :]

    def seg(i):
        return pl.ds(pl.multiple_of(i * SEG, SEG), SEG)

    def to_seq(n, src, dst, j):
        return pltpu.make_async_remote_copy(src.at[peers[j]], dst.at[seg(z), :], a2s.at[n, j], a2r.at[n, j], device_id=at(dp, peers[j]),
                                            device_id_type=MESH)

    def to_seq_in(n, src, dst, j):
        return pltpu.make_async_remote_copy(src.at[peers[j]], dst.at[seg(peers[j]), :], a2s.at[n, j], a2r.at[n, j],
                                            device_id=at(dp, peers[j]), device_id_type=MESH)

    def to_pos(n, src, dst, j):
        return pltpu.make_async_remote_copy(src.at[seg(peers[j]), :], dst.at[z], a2s.at[n, j], a2r.at[n, j], device_id=at(dp, peers[j]),
                                            device_id_type=MESH)

    def to_pos_in(n, src, dst, j):
        return pltpu.make_async_remote_copy(src.at[seg(peers[j]), :], dst.at[peers[j]], a2s.at[n, j], a2r.at[n, j],
                                            device_id=at(dp, peers[j]), device_id_type=MESH)

    full = [g.reshape(*((8,) + (2,) * nb + (rs, D)))] + list(bufs)

    def order(i):
        up = list(range(1, nb))
        return [0] + (up if i % 2 == 0 else up[::-1])

    def slot(i, k):
        return i % 8 if k < 1 else i

    def pick(i, k, **vals):
        left = sorted(set(range(nb)) - set(order(i)[:k]), reverse=True)
        return (slot(i, k),) + tuple(vals.get(f"b{b}", slice(None)) for b in left)

    def red(i, k):
        b = order(i)[k]
        return pltpu.make_async_remote_copy(full[k].at[pick(i, k, **{f"b{b}": 1 - bit[b]})], full[k + 1].at[slot(i, k + 1)], gs_sem.at[k, i],
                                            gr_sem.at[k, i], device_id=at(buddy[b], z), device_id_type=MESH)

    def red_add(i, k):
        b = order(i)[k]
        red(i, k).wait_recv()
        if k + 1 < nb:
            n = order(i)[k + 1]
            for val in (1 - bit[n], bit[n]):
                d = pick(i, k + 1, **{f"b{n}": val})
                s = pick(i, k, **{f"b{b}": bit[b], f"b{n}": val})
                full[k + 1][d] = full[k + 1][d] + full[k][s]
                if val is not bit[n]:
                    red(i, k + 1).start()
        else:
            full[nb][i] = full[nb][i] + full[k][pick(i, k, **{f"b{b}": bit[b]})]
            pl.when(jnp.logical_not(inner))(zcopy(i, 0).start)

    def zcopy(i, k):
        src, dst, to = ((bufs[nb - 1], za, z_near), (za, gw, z_cross), (gw, gw, z_near))[k]
        return pltpu.make_async_remote_copy(src.at[i], dst.at[i], zs_sem.at[k, i], zr_sem.at[k, i], device_id=at(dp, to), device_id_type=MESH)

    def z_add(i, k):
        @pl.when(inner)
        def _():
            zcopy(i, k).wait_recv()
            if k == 0:
                za[i] = za[i] + bufs[nb - 1][i]
                zcopy(i, 1).start()
            else:
                gw[i] = gw[i] + za[i]
                zcopy(i, 2).start()

    def z_end(i):
        @pl.when(inner)
        def _():
            zcopy(i, 1).wait_send()
            zcopy(i, 2).wait_send()

        @pl.when(jnp.logical_not(inner))
        def _():
            zcopy(i, 2).wait_recv()
            zcopy(i, 0).wait_send()

    def vcopy(k):
        if k < nb:
            src, dst, to = vec.at[k], vrecv.at[k], at(buddy[k], z)
        else:
            src, dst, to = ((vec.at[nb], vrecv.at[nb], at(dp, z_near)), (vec.at[nb + 1], vrecv.at[nb + 1], at(dp, z_cross)),
                            (vout, vout, at(dp, z_near)))[k - nb]
        return pltpu.make_async_remote_copy(src, dst, vs_sem.at[k], vr_sem.at[k], device_id=to, device_id_type=MESH)

    def v_add(k):
        if k < nb:
            vcopy(k).wait_recv()
            vec[k + 1] = vec[k] + vrecv[k]
            if k + 1 < nb:
                vcopy(k + 1).start()
            else:
                pl.when(jnp.logical_not(inner))(vcopy(nb).start)
        else:
            @pl.when(inner)
            def _():
                vcopy(k).wait_recv()
                if k == nb:
                    vec[nb + 1] = vec[nb] + vrecv[nb]
                    vcopy(nb + 1).start()
                else:
                    vout[...] = vec[nb + 1] + vrecv[nb + 1]
                    vcopy(nb + 2).start()

    def v_end():
        for k in range(nb):
            vcopy(k).wait_send()

        @pl.when(inner)
        def _():
            vcopy(nb + 1).wait_send()
            vcopy(nb + 2).wait_send()

        @pl.when(jnp.logical_not(inner))
        def _():
            vcopy(nb).wait_send()
            vcopy(nb + 2).wait_recv()

    for m in range(3):
        load_w(m, wqkv.at[m]).start()
    own_tok = pltpu.make_async_copy(tok.at[z], x_ref.at[seg(z), :], locsem.at[0])
    own_tok.start()
    load_w(3, wo).start()
    load_w(4, win_c(0)).start()
    load_w(5, wout_c(0)).start()
    barrier = pltpu.get_barrier_semaphore()
    others = [at(buddy[b], z) for b in range(nb)] + [at(dp, p) for p in peers]
    for o in others:
        pl.semaphore_signal(barrier, inc=1, device_id=o, device_id_type=MESH)
    pl.semaphore_wait(barrier, len(others))
    for j in (1, 2, 0):
        to_seq(0, tok, x_ref, j).start()
    b = [jnp.full((1, 1), rng_ref[i], jnp.int32).astype(F32) * (1 / 16.0) for i in range(4)]
    iv = [1.0 / t for t in b]
    vec[0] = jnp.zeros_like(vec[0])
    v0 = vec.at[0]

    own_tok.wait()
    for m in range(3):
        load_w(m, wqkv.at[m]).wait()
    for j in range(4):
        if j:
            to_seq_in(0, tok, x_ref, j - 1).wait_recv()
        qkv(x_ref, qi_ref, w, sm, q_ref, k_ref, v_ref, qt_ref, kt_ref, vt_ref, b[0], iv[0], seg(peers[j - 1] if j else z))
    own_cot = pltpu.make_async_copy(cot.at[z], ct_ref.at[seg(z), :], locsem.at[1])
    own_cot.start()
    for j in (1, 2, 0):
        to_seq(1, cot, ct_ref, j).start()
    load_w(0, win_c(1)).start()
    load_w(1, wout_c(1)).start()
    attn_fwd(qt_ref, k_ref, vt_ref, p_ref, ctxt_ref, len_ref[z])
    load_w(3, wo).wait()
    out_proj(ctxt_ref, x_ref, w.at[3], sm, qct_ref, slc_ref, n1_ref, r1_ref, hid_ref, slh_ref, qh_ref, acc_ref, b[1], iv[1], b[2], iv[2])

    def w_slot(c):
        return 4 * (1 - c % 2)

    def fwd_wait(c):
        load_w(w_slot(c), win_c(c)).wait()
        load_w(w_slot(c) + 1, wout_c(c)).wait()
        return w_slot(c)

    def fwd_done(c):
        @pl.when(c < 2)
        def _():
            load_w(w_slot(c), win_c(c + 2)).start()
            load_w(w_slot(c) + 1, wout_c(c + 2)).start()

    ffn_fwd(qh_ref, w, sm, act_ref, dfac_ref, acc_ref, b[3], iv[3], fwd_wait, fwd_done)
    own_cot.wait()
    for j in range(3):
        to_seq_in(1, cot, ct_ref, j).wait_recv()
    ln2(acc_ref, hid_ref, ct_ref, sm, gb_ref, v0)
    own_out = pltpu.make_async_copy(ct_ref.at[seg(z), :], outp.at[z], locsem.at[2])
    own_out.start()
    for j in (1, 2, 0):
        to_pos(2, ct_ref, outp, j).start()

    def put_out(c, v):
        fr = 4 * rs
        for h in range(D // fr):
            for j in range(4):
                g[j, c * (D // fr) + h] = v[h * fr + j * rs:h * fr + (j + 1) * rs].astype(BF)

    def put(i, v):
        g[i % 8] = v.astype(BF).reshape(n_dp, rs, D)

    ffn_bwd_out(gb_ref, qh_ref, act_ref, vt_ref.reshape(D, L), put_out)
    for i in range(4):
        red(i, 0).start()
    acc_ref[...] = jnp.zeros_like(acc_ref)
    qht = vt_ref.reshape(D, L)
    for j in range(4):
        c = 3 - j
        s = w_slot(c)
        if j >= 2:
            fwd_wait(c)
        ffn_bwd_in(c, gb_ref, w.at[s], w.at[s + 1], dfac_ref, acc_ref, qht, functools.partial(put, 4 + j), v0)
        red(4 + j, 0).start()
        if j < 2:
            load_w(s, win_c(c - 2)).start()
            load_w(s + 1, wout_c(c - 2)).start()
        if j == 2:
            load_w(0, wqkv.at[0]).start()
            load_w(1, wqkv.at[1]).start()
        red_add(j, 0)
    ln1_bwd(acc_ref, hid_ref, slh_ref, n1_ref, r1_ref, sm, gb_ref, v0)
    red_add(4, 0)
    red_add(5, 0)
    dc = LaneSlots(act_ref)
    red(0, 0).wait_send()
    out_bwd(gb_ref, w.at[3], qct_ref, slc_ref, dc, vt_ref, functools.partial(put, 8))
    red(8, 0).start()
    red_add(6, 0)
    red_add(7, 0)
    steps = {1: [(0, 1), (1, 1)], 2: [(8, 0)], 3: [(0, 2), (1, 2)], 5: [(2, 1), (3, 1)]}

    def service(p):
        for at_p, todo in steps.items():
            @pl.when(p == at_p)
            def _():
                for i, k in todo:
                    red_add(i, k)

    attn_bwd(q_ref, kt_ref, v_ref, dc, vt_ref, p_ref, q_ref, k_ref, v_ref, service)
    for i in (1, 2, 3):
        red(i, 0).wait_send()
    for m in (0, 1):
        load_w(m, wqkv.at[m]).wait()

    def put_q(m, v):
        put(9 + m, v)
        red(9 + m, 0).start()
        if m == 0:
            red_add(2, 2)
            red_add(3, 2)
            z_add(0, 0)
            z_add(1, 0)
        if m == 1:
            red_add(9, 0)
            z_add(0, 1)
            z_add(1, 1)
        if m == 2:
            red_add(10, 0)

    qkv_bwd(qi_ref, qct_ref, x_ref, w, q_ref, k_ref, v_ref, hid_ref, acc_ref, put_q, v0, b[0], iv[0])
    vcopy(0).start()
    own_gx = pltpu.make_async_copy(x_ref.at[seg(z), :], gxp.at[z], locsem.at[3])
    own_gx.start()
    for j in (1, 2, 0):
        to_pos(3, x_ref, gxp, j).start()

    red_add(11, 0)
    v_add(0)
    for pr in range(2, 7):
        for i in (2 * pr, 2 * pr + 1):
            if i < 12:
                red_add(i, 1)
        if pr == 2:
            z_add(2, 0)
            z_add(3, 0)
        for i in (2 * pr, 2 * pr + 1):
            if i < 12:
                red_add(i, 2)
        if pr == 2:
            z_add(2, 1)
            z_add(3, 1)
        if pr > 2:
            for i in (2 * pr - 2, 2 * pr - 1):
                z_add(i, 0)
            for i in (2 * pr - 4, 2 * pr - 3):
                if i >= 4:
                    z_add(i, 1)
        if pr - 1 < nb + 2:
            v_add(pr - 1)
    z_add(10, 1)
    z_add(11, 1)
    for i in range(12):
        z_end(i)
        for k in range(nb):
            if (k, i) not in ((0, 0), (0, 1), (0, 2), (0, 3)):
                red(i, k).wait_send()
    v_end()
    own_out.wait()
    own_gx.wait()
    for j in range(3):
        to_seq(0, tok, x_ref, j).wait_send()
        to_seq(1, cot, ct_ref, j).wait_send()
        to_pos(2, ct_ref, outp, j).wait_send()
        to_pos_in(2, ct_ref, outp, j).wait_recv()
        to_pos(3, x_ref, gxp, j).wait_send()
        to_pos_in(3, x_ref, gxp, j).wait_recv()


def fused(n_dp, *args):
    nb, rs = n_dp.bit_length() - 1, D // n_dp

    def vm(*s, d=BF):
        return pltpu.VMEM(s, d)
    dma = pltpu.SemaphoreType.DMA
    scratch = [vm(6, D, D), vm(8, n_dp, rs, D), vm(L, D), vm(L, D), vm(L, D), vm(6, L, 128), vm(6, L, 128), vm(6, L, 128), vm(6, 128, L),
               vm(6, 128, L), vm(6, 128, L), vm(12, L, L), vm(6, 128, L), vm(D, L), vm(L, D),
               vm(L, D, d=F32), vm(L, 128, d=F32), vm(L, D, d=F32), vm(L, D), vm(L, D), vm(4, L, D), vm(4, L, D), vm(L, D, d=F32),
               vm(L, D), vm(12, rs, D), vm(nb + 2, 16, D, d=F32), vm(nb + 2, 16, D, d=F32)]
    scratch += [vm(*((12,) + (2,) * (nb - k) + (rs, D))) for k in range(1, nb + 1)]
    scratch += [dma((6,)), dma((4,)), dma((4, 3)), dma((4, 3)), dma((nb, 12)), dma((nb, 12)), dma((3, 12)), dma((3, 12)), dma((nb + 3,)), dma((nb + 3,))]
    pos = jax.ShapeDtypeStruct((4, L // 4, D), BF)
    outs = [pos, pos, jax.ShapeDtypeStruct((12, rs, D), BF), jax.ShapeDtypeStruct((16, D), F32)]
    v, s, h = (pl.BlockSpec(memory_space=m) for m in (pltpu.VMEM, pltpu.SMEM, pl.ANY))
    return pl.pallas_call(
        functools.partial(fused_kernel, n_dp), out_shape=outs, in_specs=[h, h, s, s, h, h, h, h, v], out_specs=[h, h, v, v],
        scratch_shapes=scratch,
        compiler_params=pltpu.CompilerParams(collective_id=0, has_side_effects=True, vmem_limit_bytes=64 * 1024 * 1024 - 65536))(*args)


def on_device(n_dp, tokens, lengths, ranges, qkv_weight, qv_bias, out_weight, out_bias, norm_gains, norm_shifts, ffn_in, ffn_in_bias,
              ffn_out, ffn_out_bias, cotangent):
    small = jnp.concatenate([qv_bias, out_bias[None], norm_gains, norm_shifts, ffn_out_bias[None], ffn_in_bias.reshape(4, D)]).astype(F32)
    out, gx, gw, vec = fused(n_dp, tokens.transpose(1, 0, 2), cotangent.transpose(1, 0, 2), lengths, ranges, qkv_weight, out_weight,
                             ffn_in, ffn_out, small)
    rs = D // n_dp
    i = lax.axis_index("dp")
    gw = gw.astype(F32)

    def mine(v):
        return lax.dynamic_slice_in_dim(v, i * rs, rs, axis=-1)
    fib = lax.dynamic_slice(vec[8:12].reshape(-1), (i * 4 * rs,), (4 * rs,))
    return (out.transpose(1, 0, 2), gx.transpose(1, 0, 2).astype(F32), gw[9:12], mine(vec[0:2]), gw[8], mine(vec[2]), mine(vec[3:5]),
            mine(vec[5:7]), gw[7:3:-1].transpose(1, 0, 2).reshape(rs, F), fib, gw[0:4].reshape(4 * rs, D), mine(vec[7]))


def local_kernel(x_ref, ct_ref, len_ref, rng_ref, w_ref, sm, gx_ref, g_ref, vec_ref, w, qi_ref, q_ref, k_ref, v_ref, qt_ref, kt_ref, vt_ref,
                 p_ref, ctxt_ref, qct_ref, slc_ref, n1_ref, r1_ref, hid_ref, slh_ref, qh_ref, act_ref, dfac_ref, acc_ref, gb_ref, stage,
                 wsem, gsem):
    def fetch(slot, i):
        cp = pltpu.make_async_copy(w_ref.at[i], w.at[slot], wsem)
        cp.start()
        cp.wait()

    def put(i, v):
        stage[...] = v.astype(BF)
        cp = pltpu.make_async_copy(stage, g_ref.at[i], gsem)
        cp.start()
        cp.wait()

    b = [jnp.full((1, 1), rng_ref[i], jnp.int32).astype(F32) * (1 / 16.0) for i in range(4)]
    iv = [1.0 / t for t in b]
    vec_ref[...] = jnp.zeros_like(vec_ref)
    for m in range(4):
        fetch(m, 8 + (m + 1) % 4 if m < 3 else 8)
    for r in range(0, L, 256):
        qkv(x_ref, qi_ref, w, sm, q_ref, k_ref, v_ref, qt_ref, kt_ref, vt_ref, b[0], iv[0], slice(r, r + 256))
    attn_fwd(qt_ref, k_ref, vt_ref, p_ref, ctxt_ref, len_ref[0])
    out_proj(ctxt_ref, x_ref, w.at[3], sm, qct_ref, slc_ref, n1_ref, r1_ref, hid_ref, slh_ref, qh_ref, acc_ref, b[1], iv[1], b[2], iv[2])

    def before(c):
        fetch(4, c)
        fetch(5, 4 + c)
        return 4

    ffn_fwd(qh_ref, w, sm, act_ref, dfac_ref, acc_ref, b[3], iv[3], before, lambda c: None)
    ln2(acc_ref, hid_ref, ct_ref, sm, gb_ref, vec_ref)
    qht = vt_ref.reshape(D, L)
    ffn_bwd_out(gb_ref, qh_ref, act_ref, qht, lambda c, v: put(4 + c, v))
    acc_ref[...] = jnp.zeros_like(acc_ref)
    for c in range(4):
        before(c)
        ffn_bwd_in(c, gb_ref, w.at[4], w.at[5], dfac_ref, acc_ref, qht, functools.partial(put, c), vec_ref)
    ln1_bwd(acc_ref, hid_ref, slh_ref, n1_ref, r1_ref, sm, gb_ref, vec_ref)
    dc = LaneSlots(act_ref)
    out_bwd(gb_ref, w.at[3], qct_ref, slc_ref, dc, vt_ref, functools.partial(put, 8))
    attn_bwd(q_ref, kt_ref, v_ref, dc, vt_ref, p_ref, q_ref, k_ref, v_ref, lambda p: None)
    qkv_bwd(qi_ref, qct_ref, x_ref, w, q_ref, k_ref, v_ref, hid_ref, acc_ref, lambda m, v: put(9 + m, v), vec_ref, b[0], iv[0])
    gx_ref[...] = x_ref[...]


def local(x, ct, length, ranges, weights, small):
    def vm(*s, d=BF):
        return pltpu.VMEM(s, d)
    scratch = [vm(6, D, D), vm(L, D), vm(6, L, 128), vm(6, L, 128), vm(6, L, 128), vm(6, 128, L),
               vm(6, 128, L), vm(6, 128, L), vm(12, L, L), vm(6, 128, L), vm(D, L), vm(L, D),
               vm(L, D, d=F32), vm(L, 128, d=F32), vm(L, D, d=F32), vm(L, D), vm(L, D), vm(4, L, D), vm(4, L, D), vm(L, D, d=F32),
               vm(L, D), vm(D, D), pltpu.SemaphoreType.DMA, pltpu.SemaphoreType.DMA]
    outs = [jax.ShapeDtypeStruct((L, D), BF), jax.ShapeDtypeStruct((L, D), BF), jax.ShapeDtypeStruct((12, D, D), BF),
            jax.ShapeDtypeStruct((16, D), F32)]
    v, s, h = (pl.BlockSpec(memory_space=m) for m in (pltpu.VMEM, pltpu.SMEM, pl.ANY))

    def body(x_in, ct_in, len_ref, rng_ref, w_ref, sm, out_ref, gx_ref, g_ref, vec_ref, x_ref, *rest):
        x_ref[...] = x_in[...]
        out_ref[...] = ct_in[...]
        local_kernel(x_ref, out_ref, len_ref, rng_ref, w_ref, sm, gx_ref, g_ref, vec_ref, *rest)

    return pl.pallas_call(
        body, out_shape=outs, in_specs=[v, v, s, s, h, v], out_specs=[v, v, h, v], scratch_shapes=[vm(L, D)] + scratch,
        compiler_params=pltpu.CompilerParams(vmem_limit_bytes=60 * 1024 * 1024))(x, ct, length, ranges, weights, small)


def on_device_local(n_dp, tokens, lengths, ranges, qkv_weight, qv_bias, out_weight, out_bias, norm_gains, norm_shifts, ffn_in, ffn_in_bias,
                    ffn_out, ffn_out_bias, cotangent):
    def to_seq(a):
        return lax.all_to_all(a.transpose(1, 0, 2), "head", split_axis=0, concat_axis=1, tiled=True)[0]

    def to_pos(a):
        return lax.all_to_all(a[None], "head", split_axis=1, concat_axis=0, tiled=True).transpose(1, 0, 2)

    small = jnp.concatenate([qv_bias, out_bias[None], norm_gains, norm_shifts, ffn_out_bias[None], ffn_in_bias.reshape(4, D)]).astype(F32)
    weights = jnp.concatenate([ffn_in.reshape(D, 4, D).transpose(1, 0, 2), ffn_out.reshape(4, D, D), out_weight[None], qkv_weight])
    length = lax.dynamic_slice(lengths, (lax.axis_index("head"),), (1,))
    out, gx, g, vec = local(to_seq(tokens), to_seq(cotangent), length, ranges, weights, small)
    rs = D // n_dp
    wout = lax.psum_scatter(g[4:8].reshape(4 * D, D), "dp", scatter_dimension=0, tiled=True)
    rest = lax.psum_scatter(jnp.concatenate([g[0:4], g[8:12]]), "dp", scatter_dimension=1, tiled=True)
    both = lax.psum(jnp.concatenate([wout, rest.reshape(8 * rs, D)]), "head").astype(F32)
    wout, rest = both[:4 * rs], both[4 * rs:].reshape(8, rs, D)
    vec = lax.psum(vec, ("dp", "head"))
    i = lax.axis_index("dp")

    def mine(v):
        return lax.dynamic_slice_in_dim(v, i * rs, rs, axis=-1)
    fib = lax.dynamic_slice(vec[8:12].reshape(-1), (i * 4 * rs,), (4 * rs,))
    return (to_pos(out), to_pos(gx).astype(F32), rest[5:8], mine(vec[0:2]), rest[4], mine(vec[2]), mine(vec[3:5]), mine(vec[5:7]),
            rest[0:4].transpose(1, 0, 2).reshape(rs, F), fib, wout, mine(vec[7]))


def solution(mesh):
    n_dp = mesh.shape["dp"]
    tok = P("head", "dp", None)
    body = on_device if D // n_dp % 16 == 0 else on_device_local
    return jax.shard_map(
        functools.partial(body, n_dp),
        mesh=mesh,
        in_specs=(tok, P("dp")) + (P(),) * 11 + (tok,),
        out_specs=(tok, tok, P(None, "dp", None), P(None, "dp"), P("dp", None), P("dp"), P(None, "dp"), P(None, "dp"),
                   P("dp", None), P("dp"), P("dp", None), P("dp")),
        check_vma=False,
    )
```

```python
import functools
import jax
import jax.numpy as jnp
from jax import lax
from jax.experimental import pallas as pl
from jax.experimental.pallas import tpu as pltpu
from jax.sharding import PartitionSpec as P

F32, BF = jnp.float32, jnp.bfloat16
L, D, F, NP = 512, 768, 3072, 6
GC0, GC1 = 0.7978845608028654, 0.044715


def nn(a, b):
    return lax.dot_general(a, b, (((1,), (0,)), ((), ())), preferred_element_type=F32)


def nt(a, b):
    return lax.dot_general(a, b, (((1,), (1,)), ((), ())), preferred_element_type=F32)


def tn(a, b):
    return lax.dot_general(a, b, (((0,), (0,)), ((), ())), preferred_element_type=F32)


def rows_loop(n, step, f):
    def it(r, c):
        f(pl.multiple_of(r * step, step))
        return c
    lax.fori_loop(0, n // step, it, 0)


def mean(v):
    return jnp.sum(v, axis=-1, keepdims=True) * (1.0 / D)


class LaneSlots:
    def __init__(self, ref):
        self.ref = ref

    def __getitem__(self, p):
        return self.ref[0, :, pl.ds(pl.multiple_of(p * 128, 128), 128)]

    def __setitem__(self, p, value):
        self.ref[0, :, pl.ds(pl.multiple_of(p * 128, 128), 128)] = value


def qkv(x_ref, qit_ref, w_ref, sm, q_ref, k_ref, v_ref, qt_ref, kt_ref, vt_ref, b0, r0, rows):
    xb = x_ref[rows, :].astype(F32)
    qi = (b0 * jnp.tanh(xb * r0)).astype(BF)
    for p in range(NP):
        qit_ref[p * 128:(p + 1) * 128, rows] = qi[:, p * 128:(p + 1) * 128].T
    for m, (dst, tdst) in enumerate(((q_ref, qt_ref), (k_ref, kt_ref), (v_ref, vt_ref))):
        y = nn(qi, w_ref[m])
        if m == 0:
            y = (y + sm[0:1, :]).astype(BF).astype(F32) * 0.125
        if m == 2:
            y = y + sm[1:2, :]
        for p in range(NP):
            yp = y[:, p * 128:(p + 1) * 128].astype(BF)
            dst[p, rows, :] = yp
            tdst[p, :, rows] = yp.T


def attn_fwd(q_t, k_ref, v_t, p_ref, ctxt_ref, length):
    live = lax.broadcasted_iota(jnp.int32, (L, L), 0) < length
    low = lax.broadcasted_iota(jnp.int32, (128, L), 0) < 64

    def pair(p, c):
        kp, qt, vt = k_ref[p], q_t[p], v_t[p]
        for t in range(2):
            qm = jnp.where(low if t == 0 else ~low, qt, jnp.zeros_like(qt))
            s = jnp.where(live, nn(kp, qm), -1e9)
            e = jnp.exp(s - jnp.max(s, axis=0, keepdims=True))
            pr = (e * (1.0 / jnp.sum(e, axis=0, keepdims=True))).astype(BF)
            p_ref[2 * p + t] = pr
            ctxt_ref[p, 64 * t:64 * t + 64, :] = nn(vt[64 * t:64 * t + 64, :], pr).astype(BF)
        return c
    lax.fori_loop(0, NP, pair, 0)


def out_proj(ctxt_ref, x_ref, wo_ref, sm, qct_ref, slc_ref, n1_ref, r1_ref, hid_ref, slh_ref, qh_ref, acc_ref, b1, i1, b2, i2):
    for p in range(NP):
        th = jnp.tanh(ctxt_ref[p].astype(F32) * i1)
        qct_ref[p * 128:(p + 1) * 128, :] = (b1 * th).astype(BF)
        slc_ref[:, p * 128:(p + 1) * 128] = (1.0 - th * th).astype(BF).T
    hid_ref[...] = tn(qct_ref[...], wo_ref[...])

    def f(r):
        rows = pl.ds(r, 64)
        v = hid_ref[rows, :] + sm[2:3, :] + x_ref[rows, :].astype(F32)
        c = v - mean(v)
        rr = lax.rsqrt(mean(c * c) + 1e-5)
        n = c * rr
        n1_ref[rows, :] = n
        r1_ref[rows, :] = jnp.broadcast_to(rr, (64, 128))
        h = n * sm[3:4, :] + sm[5:6, :]
        hid_ref[rows, :] = h
        th = jnp.tanh(h * i2)
        qh_ref[rows, :] = (b2 * th).astype(BF)
        slh_ref[rows, :] = (1.0 - th * th).astype(BF)
    rows_loop(L, 64, f)
    acc_ref[...] = jnp.zeros_like(acc_ref)


def ffn_fwd(qh_ref, w, sm, act_ref, dfac_ref, acc_ref, b3, i3, before, after):
    def chunk(c, _):
        s = before(c)
        bias = sm[pl.ds(8 + c, 1), :]
        for r in range(0, L, 256):
            rows = slice(r, r + 256)
            t = nn(qh_ref[rows, :], w[s]) + bias
            t2 = t * t
            th = jnp.tanh(t * (GC0 + (GC0 * GC1) * t2))
            hp = 0.5 + 0.5 * th
            u = t * hp
            cl = jnp.tanh(u * i3)
            act = (b3 * cl).astype(BF)
            d = hp + u * (1.0 - th) * (GC0 + (3 * GC0 * GC1) * t2)
            act_ref[c, rows, :] = act
            dfac_ref[c, rows, :] = (d * (1.0 - cl * cl)).astype(BF)
            acc_ref[rows, :] += nn(act, w[s + 1])
        after(c)
        return _
    lax.fori_loop(0, 4, chunk, 0)


def colsum(vec, row, val):
    vec[row:row + 1, :] += jnp.sum(val, axis=0, keepdims=True)


def ln2(acc_ref, hid_ref, ct_ref, sm, gb_ref, vec):
    def f(r):
        rows = pl.ds(r, 64)
        v = acc_ref[rows, :] + sm[7:8, :] + hid_ref[rows, :]
        c = v - mean(v)
        rr = lax.rsqrt(mean(c * c) + 1e-5)
        n = c * rr
        ct = ct_ref[rows, :].astype(F32)
        ct_ref[rows, :] = (n * sm[4:5, :] + sm[6:7, :]).astype(BF)
        colsum(vec, 4, ct * n)
        colsum(vec, 6, ct)
        q = ct * sm[4:5, :]
        gs = rr * (q - mean(q) - n * mean(q * n))
        hid_ref[rows, :] = gs
        gb = gs.astype(BF)
        gb_ref[rows, :] = gb
        colsum(vec, 7, gb.astype(F32))
    rows_loop(L, 64, f)


def ffn_bwd_out(gb_ref, act_ref, put):
    def chunk(c, _):
        put(c, tn(act_ref[c], gb_ref[...]))
        return _
    lax.fori_loop(0, 4, chunk, 0)


def ffn_bwd_in(c, gb_ref, win, wout, dfac_ref, acc_ref, qht_ref, put, vec):
    for r in range(0, L, 256):
        rows = slice(r, r + 256)
        gp = (nt(gb_ref[rows, :], wout[...]) * dfac_ref[c, rows, :].astype(F32)).astype(BF)
        dfac_ref[c, rows, :] = gp
        vec[pl.ds(8 + c, 1), :] += jnp.sum(gp.astype(F32), axis=0, keepdims=True)
        acc_ref[rows, :] += nt(gp, win[...])
    put(nn(qht_ref[...], dfac_ref[c]))


def ln1_bwd(acc_ref, gs_ref, slh_ref, n1_ref, r1_ref, sm, gat_ref, vec):
    def f(r):
        rows = pl.ds(r, 64)
        gh = gs_ref[rows, :] + acc_ref[rows, :] * slh_ref[rows, :].astype(F32)
        n = n1_ref[rows, :]
        colsum(vec, 3, gh * n)
        colsum(vec, 5, gh)
        q = gh * sm[3:4, :]
        gs = r1_ref[rows, 0:1] * (q - mean(q) - n * mean(q * n))
        gs_ref[rows, :] = gs
        gat = gs.astype(BF)
        gat_ref[rows, :] = gat
        colsum(vec, 2, gat.astype(F32))
    rows_loop(L, 64, f)


def out_bwd(gat_ref, wo_ref, qct_ref, slc_ref, dc_ref, dct_ref, put):
    put(nn(qct_ref[...], gat_ref[...]))
    g = nt(gat_ref[...], wo_ref[...])
    for p in range(NP):
        cols = slice(p * 128, (p + 1) * 128)
        d = (g[:, cols] * slc_ref[:, cols].astype(F32)).astype(BF)
        dc_ref[p] = d
        dct_ref[p] = d.T


def attn_bwd(q_ref, k_t, v_ref, dc_ref, dc_t, p_ref, dq_ref, dk_ref, dv_ref, service):
    low = lax.broadcasted_iota(jnp.int32, (128, L), 0) < 64
    lane_low = lax.broadcasted_iota(jnp.int32, (L, 128), 1) < 64

    def pair(p, c):
        qp, kt, vp, dc, dct = q_ref[p], k_t[p], v_ref[p], dc_ref[p], dc_t[p]
        res = []
        for t in range(2):
            dm = jnp.where(low if t == 0 else ~low, dct, jnp.zeros_like(dct))
            dp = nn(vp, dm)
            pr = p_ref[2 * p + t]
            prf = pr.astype(F32)
            delta = jnp.sum(dp * prf, axis=0, keepdims=True)
            ds = (prf * (dp - delta)).astype(BF)
            res.append((nn(pr, dc), nn(ds, qp), nn(kt[64 * t:64 * t + 64, :], ds) * 0.125))
        dv_ref[p] = jnp.where(lane_low, res[0][0], res[1][0]).astype(BF)
        dk_ref[p] = jnp.where(lane_low, res[0][1], res[1][1]).astype(BF)
        dq_ref[p] = jnp.concatenate([res[0][2], res[1][2]], axis=0).astype(BF).T
        service(p)
        return c
    lax.fori_loop(0, NP, pair, 0)


def lanes(ref):
    return jnp.concatenate([ref[p] for p in range(NP)], axis=1)


def qkv_bwd_x(x_ref, w_ref, dq_ref, dk_ref, dv_ref, gs_ref, acc_ref, vec, i0):
    for m, ref in enumerate((dq_ref, dk_ref, dv_ref)):
        d = lanes(ref)
        if m != 1:
            colsum(vec, m // 2, d.astype(F32))
        if m == 0:
            acc_ref[...] = nt(d, w_ref[m])
        else:
            acc_ref[...] += nt(d, w_ref[m])

    def f(r):
        rows = pl.ds(r, 64)
        th = jnp.tanh(x_ref[rows, :].astype(F32) * i0)
        x_ref[rows, :] = (gs_ref[rows, :] + acc_ref[rows, :] * (1.0 - th * th)).astype(BF)
    rows_loop(L, 64, f)


MESH = pl.DeviceIdType.MESH
SCHEDULE = {
    "f0": [(0, 0)],
    "f1": [(0, 1)],
    "f2": [(0, 4)],
    "ln": [(1, 0), (0, 5)],
    "a0": [(1, 1)],
    "a1": [(2, 0), (0, 7), (0, 3), (0, 6)],
    "a3": [(2, 1)],
    "a5": [(3, 0), (1, 5)],
    "x": [(9, 1), (0, 2), (4, 0)],
    "q0": [(9, 2), (1, 4), (2, 5), (0, 9), (1, 7)],
    "q1": [(0, 8), (3, 5), (1, 2), (9, 0), (3, 1), (1, 3)],
    "q2": [(2, 7), (4, 5), (0, 11), (1, 9)],
    "drain": [(3, 7), (2, 4), (4, 1), (2, 2), (0, 10), (2, 3), (3, 4), (2, 9), (4, 7), (3, 2), (1, 6), (4, 4), (3, 3), (1, 8),
        (1, 11), (4, 2), (1, 10), (3, 9), (2, 6), (4, 3), (2, 11), (3, 6), (4, 9), (3, 11), (2, 10), (2, 8), (4, 6), (3, 10), (4, 11),
        (3, 8), (4, 10), (4, 8)],
}
V_WITH = 9


def fused_kernel(n_dp, tok, cot, len_ref, rng_ref, wqkv, wo, win, wout, sm,
                 outp, gxp, gw, vout,
                 w, g, x_ref, ct_ref, qit_ref, q_ref, k_ref, v_ref, qt_ref, kt_ref, vt_ref, p_ref, ctxt_ref, qct_ref, slc_ref,
                 n1_ref, r1_ref, hid_ref, slh_ref, qh_ref, act_ref, dfac_ref, acc_ref, gb_ref, za, vec, vrecv, *rest):
    nb = n_dp.bit_length() - 1
    bufs, (wsem, locsem, a2s, a2r, gs_sem, gr_sem, zs_sem, zr_sem, vs_sem, vr_sem) = rest[:nb], rest[nb:]
    rs, nz, SEG = D // n_dp, 4, L // 4
    dp, z = lax.axis_index("dp"), lax.axis_index("head")
    bit = [(dp // (1 << b)) % 2 for b in range(nb)]
    buddy = [dp + (1 - 2 * bit[b]) * (1 << b) for b in range(nb)]
    z_near, z_cross, z_far = z + 1 - 2 * (z % 2), 3 - z, (z + 2) % 4
    peers = (z_near, z_far, z_cross)
    inner = (z + 1) // 2 == 1

    def at(dpi, zi):
        return {"dp": dpi, "head": zi}

    def load_w(slot, src):
        return pltpu.make_async_copy(src, w.at[slot], wsem.at[slot])

    def win_c(c):
        return win.at[:, pl.ds(pl.multiple_of(c * D, D), D)]

    def wout_c(c):
        return wout.at[pl.ds(pl.multiple_of(c * D, D), D), :]

    def seg(i):
        return pl.ds(pl.multiple_of(i * SEG, SEG), SEG)

    def to_seq(n, src, dst, j):
        return pltpu.make_async_remote_copy(src.at[peers[j]], dst.at[seg(z), :], a2s.at[n, j], a2r.at[n, j], device_id=at(dp, peers[j]),
                                            device_id_type=MESH)

    def to_seq_in(n, src, dst, j):
        return pltpu.make_async_remote_copy(src.at[peers[j]], dst.at[seg(peers[j]), :], a2s.at[n, j], a2r.at[n, j],
                                            device_id=at(dp, peers[j]), device_id_type=MESH)

    def to_pos(n, src, dst, j):
        return pltpu.make_async_remote_copy(src.at[seg(peers[j]), :], dst.at[z], a2s.at[n, j], a2r.at[n, j], device_id=at(dp, peers[j]),
                                            device_id_type=MESH)

    def to_pos_in(n, src, dst, j):
        return pltpu.make_async_remote_copy(src.at[seg(peers[j]), :], dst.at[peers[j]], a2s.at[n, j], a2r.at[n, j],
                                            device_id=at(dp, peers[j]), device_id_type=MESH)

    full = [g.reshape(*((8,) + (2,) * nb + (rs, D)))] + list(bufs)

    def order(i):
        up = list(range(1, nb))
        return [0] + (up if i % 2 == 0 else up[::-1])

    def slot(i, k):
        return i % 8 if k < 1 else i

    def pick(i, k, **vals):
        left = sorted(set(range(nb)) - set(order(i)[:k]), reverse=True)
        return (slot(i, k),) + tuple(vals.get(f"b{b}", slice(None)) for b in left)

    def red(i, k):
        b = order(i)[k]
        return pltpu.make_async_remote_copy(full[k].at[pick(i, k, **{f"b{b}": 1 - bit[b]})], full[k + 1].at[slot(i, k + 1)], gs_sem.at[k, i],
                                            gr_sem.at[k, i], device_id=at(buddy[b], z), device_id_type=MESH)

    def red_add(i, k):
        b = order(i)[k]
        red(i, k).wait_recv()
        if k + 1 < nb:
            n = order(i)[k + 1]
            for val in (1 - bit[n], bit[n]):
                d = pick(i, k + 1, **{f"b{n}": val})
                s = pick(i, k, **{f"b{b}": bit[b], f"b{n}": val})
                full[k + 1][d] = full[k + 1][d] + full[k][s]
                if val is not bit[n]:
                    red(i, k + 1).start()
        else:
            full[nb][i] = full[nb][i] + full[k][pick(i, k, **{f"b{b}": bit[b]})]
            pl.when(jnp.logical_not(inner))(zcopy(i, 0).start)

    def zcopy(i, k):
        src, dst, to = ((bufs[nb - 1], za, z_near), (za, gw, z_cross), (gw, gw, z_near))[k]
        return pltpu.make_async_remote_copy(src.at[i], dst.at[i], zs_sem.at[k, i], zr_sem.at[k, i], device_id=at(dp, to), device_id_type=MESH)

    def z_add(i, k):
        @pl.when(inner)
        def _():
            zcopy(i, k).wait_recv()
            if k == 0:
                za[i] = za[i] + bufs[nb - 1][i]
                zcopy(i, 1).start()
            else:
                gw[i] = gw[i] + za[i]
                zcopy(i, 2).start()

    def z_end(i):
        @pl.when(inner)
        def _():
            zcopy(i, 1).wait_send()
            zcopy(i, 2).wait_send()

        @pl.when(jnp.logical_not(inner))
        def _():
            zcopy(i, 2).wait_recv()
            zcopy(i, 0).wait_send()

    def vcopy(k):
        if k < nb:
            src, dst, to = vec.at[k], vrecv.at[k], at(buddy[order(V_WITH)[k]], z)
        else:
            src, dst, to = ((vec.at[nb], vrecv.at[nb], at(dp, z_near)), (vec.at[nb + 1], vrecv.at[nb + 1], at(dp, z_cross)),
                            (vout, vout, at(dp, z_near)))[k - nb]
        return pltpu.make_async_remote_copy(src, dst, vs_sem.at[k], vr_sem.at[k], device_id=to, device_id_type=MESH)

    def v_add(k):
        if k < nb:
            vcopy(k).wait_recv()
            vec[k + 1] = vec[k] + vrecv[k]
            if k + 1 < nb:
                vcopy(k + 1).start()
            else:
                pl.when(jnp.logical_not(inner))(vcopy(nb).start)
        else:
            @pl.when(inner)
            def _():
                vcopy(k).wait_recv()
                if k == nb:
                    vec[nb + 1] = vec[nb] + vrecv[nb]
                    vcopy(nb + 1).start()
                else:
                    vout[...] = vec[nb + 1] + vrecv[nb + 1]
                    vcopy(nb + 2).start()

    def v_end():
        for k in range(nb):
            vcopy(k).wait_send()

        @pl.when(inner)
        def _():
            vcopy(nb + 1).wait_send()
            vcopy(nb + 2).wait_send()

        @pl.when(jnp.logical_not(inner))
        def _():
            vcopy(nb).wait_send()
            vcopy(nb + 2).wait_recv()

    for m in range(3):
        load_w(m, wqkv.at[m]).start()
    own_tok = pltpu.make_async_copy(tok.at[z], x_ref.at[seg(z), :], locsem.at[0])
    own_tok.start()
    load_w(3, wo).start()
    load_w(4, win_c(0)).start()
    load_w(5, wout_c(0)).start()
    barrier = pltpu.get_barrier_semaphore()
    others = [at(buddy[b], z) for b in range(nb)] + [at(dp, p) for p in peers]
    for o in others:
        pl.semaphore_signal(barrier, inc=1, device_id=o, device_id_type=MESH)
    pl.semaphore_wait(barrier, len(others))
    for j in (1, 2, 0):
        to_seq(0, tok, x_ref, j).start()
    b = [jnp.full((1, 1), rng_ref[i], jnp.int32).astype(F32) * (1 / 16.0) for i in range(4)]
    iv = [1.0 / t for t in b]
    vec[0] = jnp.zeros_like(vec[0])
    v0 = vec.at[0]

    own_tok.wait()
    for m in range(3):
        load_w(m, wqkv.at[m]).wait()
    for j in range(4):
        if j:
            to_seq_in(0, tok, x_ref, j - 1).wait_recv()
        qkv(x_ref, qit_ref, w, sm, q_ref, k_ref, v_ref, qt_ref, kt_ref, vt_ref, b[0], iv[0], seg(peers[j - 1] if j else z))
    own_cot = pltpu.make_async_copy(cot.at[z], ct_ref.at[seg(z), :], locsem.at[1])
    own_cot.start()
    for j in (1, 2, 0):
        to_seq(1, cot, ct_ref, j).start()
    load_w(0, win_c(1)).start()
    load_w(1, wout_c(1)).start()
    attn_fwd(qt_ref, k_ref, vt_ref, p_ref, ctxt_ref, len_ref[z])
    load_w(3, wo).wait()
    out_proj(ctxt_ref, x_ref, w.at[3], sm, qct_ref, slc_ref, n1_ref, r1_ref, hid_ref, slh_ref, qh_ref, acc_ref, b[1], iv[1], b[2], iv[2])

    def w_slot(c):
        return 4 * (1 - c % 2)

    def fwd_wait(c):
        load_w(w_slot(c), win_c(c)).wait()
        load_w(w_slot(c) + 1, wout_c(c)).wait()
        return w_slot(c)

    def fwd_done(c):
        @pl.when(c < 2)
        def _():
            load_w(w_slot(c), win_c(c + 2)).start()
            load_w(w_slot(c) + 1, wout_c(c + 2)).start()

    ffn_fwd(qh_ref, w, sm, act_ref, dfac_ref, acc_ref, b[3], iv[3], fwd_wait, fwd_done)
    own_cot.wait()
    for j in range(3):
        to_seq_in(1, cot, ct_ref, j).wait_recv()
    ln2(acc_ref, hid_ref, ct_ref, sm, gb_ref, v0)
    own_out = pltpu.make_async_copy(ct_ref.at[seg(z), :], outp.at[z], locsem.at[2])
    own_out.start()
    for j in (1, 2, 0):
        to_pos(2, ct_ref, outp, j).start()

    def put_out(c, v):
        fr = 4 * rs
        for h in range(D // fr):
            for j in range(4):
                g[j, c * (D // fr) + h] = v[h * fr + j * rs:h * fr + (j + 1) * rs].astype(BF)

    def put(i, v):
        g[i % 8] = v.astype(BF).reshape(n_dp, rs, D)

    def at_point(point):
        for k, i in SCHEDULE.get(point, ()):
            if k == 9:
                to_pos(3, x_ref, gxp, i).start()
            elif k < nb:
                red_add(i, k)
            else:
                z_add(i, k - nb)
            if i == V_WITH and k != 9:
                v_add(k)

    ffn_bwd_out(gb_ref, act_ref, put_out)
    for i in range(4):
        red(i, 0).start()
    acc_ref[...] = jnp.zeros_like(acc_ref)
    qht = vt_ref.reshape(D, L)
    for p in range(NP):
        qht[p * 128:(p + 1) * 128, :] = qh_ref[:, p * 128:(p + 1) * 128].T
    at_point("fo")
    for j in range(4):
        c = 3 - j
        s = w_slot(c)
        if j >= 2:
            fwd_wait(c)
        ffn_bwd_in(c, gb_ref, w.at[s], w.at[s + 1], dfac_ref, acc_ref, qht, functools.partial(put, 4 + j), v0)
        red(4 + j, 0).start()
        if j < 2:
            load_w(s, win_c(c - 2)).start()
            load_w(s + 1, wout_c(c - 2)).start()
        if j == 2:
            load_w(0, wqkv.at[0]).start()
            load_w(1, wqkv.at[1]).start()
        at_point(f"f{j}")
    ln1_bwd(acc_ref, hid_ref, slh_ref, n1_ref, r1_ref, sm, gb_ref, v0)
    at_point("ln")
    dc = LaneSlots(act_ref)
    red(0, 0).wait_send()
    out_bwd(gb_ref, w.at[3], qct_ref, slc_ref, dc, vt_ref, functools.partial(put, 8))
    red(8, 0).start()
    at_point("ob")

    def service(p):
        for at_p in range(NP):
            if f"a{at_p}" in SCHEDULE:
                @pl.when(p == at_p)
                def _():
                    at_point(f"a{at_p}")

    attn_bwd(q_ref, kt_ref, v_ref, dc, vt_ref, p_ref, q_ref, k_ref, v_ref, service)
    for m in (0, 1):
        load_w(m, wqkv.at[m]).wait()
    qkv_bwd_x(x_ref, w, q_ref, k_ref, v_ref, hid_ref, acc_ref, v0, iv[0])
    vcopy(0).start()
    own_gx = pltpu.make_async_copy(x_ref.at[seg(z), :], gxp.at[z], locsem.at[3])
    own_gx.start()
    at_point("x")
    for m, ref in enumerate((q_ref, k_ref, v_ref)):
        red(1 + m, 0).wait_send()
        put(9 + m, nn(qit_ref[...], lanes(ref)))
        red(9 + m, 0).start()
        at_point(f"q{m}")
    at_point("drain")
    for i in range(12):
        z_end(i)
        for k in range(nb):
            if (k, i) not in ((0, 0), (0, 1), (0, 2), (0, 3)):
                red(i, k).wait_send()
    v_end()
    own_out.wait()
    own_gx.wait()
    for j in range(3):
        to_seq(0, tok, x_ref, j).wait_send()
        to_seq(1, cot, ct_ref, j).wait_send()
        to_pos(2, ct_ref, outp, j).wait_send()
        to_pos_in(2, ct_ref, outp, j).wait_recv()
        to_pos(3, x_ref, gxp, j).wait_send()
        to_pos_in(3, x_ref, gxp, j).wait_recv()


def fused(n_dp, *args):
    nb, rs = n_dp.bit_length() - 1, D // n_dp

    def vm(*s, d=BF):
        return pltpu.VMEM(s, d)
    dma = pltpu.SemaphoreType.DMA
    scratch = [vm(6, D, D), vm(8, n_dp, rs, D), vm(L, D), vm(L, D), vm(D, L), vm(6, L, 128), vm(6, L, 128), vm(6, L, 128), vm(6, 128, L),
               vm(6, 128, L), vm(6, 128, L), vm(12, L, L), vm(6, 128, L), vm(D, L), vm(L, D),
               vm(L, D, d=F32), vm(L, 128, d=F32), vm(L, D, d=F32), vm(L, D), vm(L, D), vm(4, L, D), vm(4, L, D), vm(L, D, d=F32),
               vm(L, D), vm(12, rs, D), vm(nb + 2, 16, D, d=F32), vm(nb + 2, 16, D, d=F32)]
    scratch += [vm(*((12,) + (2,) * (nb - k) + (rs, D))) for k in range(1, nb + 1)]
    scratch += [dma((6,)), dma((4,)), dma((4, 3)), dma((4, 3)), dma((nb, 12)), dma((nb, 12)), dma((3, 12)), dma((3, 12)), dma((nb + 3,)), dma((nb + 3,))]
    pos = jax.ShapeDtypeStruct((4, L // 4, D), BF)
    outs = [pos, pos, jax.ShapeDtypeStruct((12, rs, D), BF), jax.ShapeDtypeStruct((16, D), F32)]
    v, s, h = (pl.BlockSpec(memory_space=m) for m in (pltpu.VMEM, pltpu.SMEM, pl.ANY))
    return pl.pallas_call(
        functools.partial(fused_kernel, n_dp), out_shape=outs, in_specs=[h, h, s, s, h, h, h, h, v], out_specs=[h, h, v, v],
        scratch_shapes=scratch,
        compiler_params=pltpu.CompilerParams(collective_id=0, has_side_effects=True, vmem_limit_bytes=64 * 1024 * 1024 - 65536))(*args)


def on_device(n_dp, tokens, lengths, ranges, qkv_weight, qv_bias, out_weight, out_bias, norm_gains, norm_shifts, ffn_in, ffn_in_bias,
              ffn_out, ffn_out_bias, cotangent):
    small = jnp.concatenate([qv_bias, out_bias[None], norm_gains, norm_shifts, ffn_out_bias[None], ffn_in_bias.reshape(4, D)]).astype(F32)
    out, gx, gw, vec = fused(n_dp, tokens.transpose(1, 0, 2), cotangent.transpose(1, 0, 2), lengths, ranges, qkv_weight, out_weight,
                             ffn_in, ffn_out, small)
    rs = D // n_dp
    i = lax.axis_index("dp")
    gw = gw.astype(F32)

    def mine(v):
        return lax.dynamic_slice_in_dim(v, i * rs, rs, axis=-1)
    fib = lax.dynamic_slice(vec[8:12].reshape(-1), (i * 4 * rs,), (4 * rs,))
    return (out.transpose(1, 0, 2), gx.transpose(1, 0, 2).astype(F32), gw[9:12], mine(vec[0:2]), gw[8], mine(vec[2]), mine(vec[3:5]),
            mine(vec[5:7]), gw[7:3:-1].transpose(1, 0, 2).reshape(rs, F), fib, gw[0:4].reshape(4 * rs, D), mine(vec[7]))


def local_kernel(x_ref, ct_ref, len_ref, rng_ref, w_ref, sm, gx_ref, g_ref, vec_ref, w, qit_ref, q_ref, k_ref, v_ref, qt_ref, kt_ref, vt_ref,
                 p_ref, ctxt_ref, qct_ref, slc_ref, n1_ref, r1_ref, hid_ref, slh_ref, qh_ref, act_ref, dfac_ref, acc_ref, gb_ref, stage,
                 wsem, gsem):
    def fetch(slot, i):
        cp = pltpu.make_async_copy(w_ref.at[i], w.at[slot], wsem)
        cp.start()
        cp.wait()

    def put(i, v):
        stage[...] = v.astype(BF)
        cp = pltpu.make_async_copy(stage, g_ref.at[i], gsem)
        cp.start()
        cp.wait()

    b = [jnp.full((1, 1), rng_ref[i], jnp.int32).astype(F32) * (1 / 16.0) for i in range(4)]
    iv = [1.0 / t for t in b]
    vec_ref[...] = jnp.zeros_like(vec_ref)
    for m in range(4):
        fetch(m, 8 + (m + 1) % 4 if m < 3 else 8)
    for r in range(0, L, 256):
        qkv(x_ref, qit_ref, w, sm, q_ref, k_ref, v_ref, qt_ref, kt_ref, vt_ref, b[0], iv[0], slice(r, r + 256))
    attn_fwd(qt_ref, k_ref, vt_ref, p_ref, ctxt_ref, len_ref[0])
    out_proj(ctxt_ref, x_ref, w.at[3], sm, qct_ref, slc_ref, n1_ref, r1_ref, hid_ref, slh_ref, qh_ref, acc_ref, b[1], iv[1], b[2], iv[2])

    def before(c):
        fetch(4, c)
        fetch(5, 4 + c)
        return 4

    ffn_fwd(qh_ref, w, sm, act_ref, dfac_ref, acc_ref, b[3], iv[3], before, lambda c: None)
    ln2(acc_ref, hid_ref, ct_ref, sm, gb_ref, vec_ref)
    qht = vt_ref.reshape(D, L)
    for p in range(NP):
        qht[p * 128:(p + 1) * 128, :] = qh_ref[:, p * 128:(p + 1) * 128].T
    ffn_bwd_out(gb_ref, act_ref, lambda c, v: put(4 + c, v))
    acc_ref[...] = jnp.zeros_like(acc_ref)
    for c in range(4):
        before(c)
        ffn_bwd_in(c, gb_ref, w.at[4], w.at[5], dfac_ref, acc_ref, qht, functools.partial(put, c), vec_ref)
    ln1_bwd(acc_ref, hid_ref, slh_ref, n1_ref, r1_ref, sm, gb_ref, vec_ref)
    dc = LaneSlots(act_ref)
    out_bwd(gb_ref, w.at[3], qct_ref, slc_ref, dc, vt_ref, functools.partial(put, 8))
    attn_bwd(q_ref, kt_ref, v_ref, dc, vt_ref, p_ref, q_ref, k_ref, v_ref, lambda p: None)
    qkv_bwd_x(x_ref, w, q_ref, k_ref, v_ref, hid_ref, acc_ref, vec_ref, iv[0])
    for m, ref in enumerate((q_ref, k_ref, v_ref)):
        put(9 + m, nn(qit_ref[...], lanes(ref)))
    gx_ref[...] = x_ref[...]


def local(x, ct, length, ranges, weights, small):
    def vm(*s, d=BF):
        return pltpu.VMEM(s, d)
    scratch = [vm(6, D, D), vm(D, L), vm(6, L, 128), vm(6, L, 128), vm(6, L, 128), vm(6, 128, L),
               vm(6, 128, L), vm(6, 128, L), vm(12, L, L), vm(6, 128, L), vm(D, L), vm(L, D),
               vm(L, D, d=F32), vm(L, 128, d=F32), vm(L, D, d=F32), vm(L, D), vm(L, D), vm(4, L, D), vm(4, L, D), vm(L, D, d=F32),
               vm(L, D), vm(D, D), pltpu.SemaphoreType.DMA, pltpu.SemaphoreType.DMA]
    outs = [jax.ShapeDtypeStruct((L, D), BF), jax.ShapeDtypeStruct((L, D), BF), jax.ShapeDtypeStruct((12, D, D), BF),
            jax.ShapeDtypeStruct((16, D), F32)]
    v, s, h = (pl.BlockSpec(memory_space=m) for m in (pltpu.VMEM, pltpu.SMEM, pl.ANY))

    def body(x_in, ct_in, len_ref, rng_ref, w_ref, sm, out_ref, gx_ref, g_ref, vec_ref, x_ref, *rest):
        x_ref[...] = x_in[...]
        out_ref[...] = ct_in[...]
        local_kernel(x_ref, out_ref, len_ref, rng_ref, w_ref, sm, gx_ref, g_ref, vec_ref, *rest)

    return pl.pallas_call(
        body, out_shape=outs, in_specs=[v, v, s, s, h, v], out_specs=[v, v, h, v], scratch_shapes=[vm(L, D)] + scratch,
        compiler_params=pltpu.CompilerParams(vmem_limit_bytes=60 * 1024 * 1024))(x, ct, length, ranges, weights, small)


def on_device_local(n_dp, tokens, lengths, ranges, qkv_weight, qv_bias, out_weight, out_bias, norm_gains, norm_shifts, ffn_in, ffn_in_bias,
                    ffn_out, ffn_out_bias, cotangent):
    def to_seq(a):
        return lax.all_to_all(a.transpose(1, 0, 2), "head", split_axis=0, concat_axis=1, tiled=True)[0]

    def to_pos(a):
        return lax.all_to_all(a[None], "head", split_axis=1, concat_axis=0, tiled=True).transpose(1, 0, 2)

    small = jnp.concatenate([qv_bias, out_bias[None], norm_gains, norm_shifts, ffn_out_bias[None], ffn_in_bias.reshape(4, D)]).astype(F32)
    weights = jnp.concatenate([ffn_in.reshape(D, 4, D).transpose(1, 0, 2), ffn_out.reshape(4, D, D), out_weight[None], qkv_weight])
    length = lax.dynamic_slice(lengths, (lax.axis_index("head"),), (1,))
    out, gx, g, vec = local(to_seq(tokens), to_seq(cotangent), length, ranges, weights, small)
    rs = D // n_dp
    wout = lax.psum_scatter(g[4:8].reshape(4 * D, D), "dp", scatter_dimension=0, tiled=True)
    rest = lax.psum_scatter(jnp.concatenate([g[0:4], g[8:12]]), "dp", scatter_dimension=1, tiled=True)
    both = lax.psum(jnp.concatenate([wout, rest.reshape(8 * rs, D)]), "head").astype(F32)
    wout, rest = both[:4 * rs], both[4 * rs:].reshape(8, rs, D)
    vec = lax.psum(vec, ("dp", "head"))
    i = lax.axis_index("dp")

    def mine(v):
        return lax.dynamic_slice_in_dim(v, i * rs, rs, axis=-1)
    fib = lax.dynamic_slice(vec[8:12].reshape(-1), (i * 4 * rs,), (4 * rs,))
    return (to_pos(out), to_pos(gx).astype(F32), rest[5:8], mine(vec[0:2]), rest[4], mine(vec[2]), mine(vec[3:5]), mine(vec[5:7]),
            rest[0:4].transpose(1, 0, 2).reshape(rs, F), fib, wout, mine(vec[7]))


def solution(mesh):
    n_dp = mesh.shape["dp"]
    tok = P("head", "dp", None)
    body = on_device if D // n_dp % 16 == 0 else on_device_local
    return jax.shard_map(
        functools.partial(body, n_dp),
        mesh=mesh,
        in_specs=(tok, P("dp")) + (P(),) * 11 + (tok,),
        out_specs=(tok, tok, P(None, "dp", None), P(None, "dp"), P("dp", None), P("dp"), P(None, "dp"), P(None, "dp"),
                   P("dp", None), P("dp"), P("dp", None), P("dp")),
        check_vma=False,
    )
```

```python
import functools
import jax
import jax.numpy as jnp
from jax import lax
from jax.experimental import pallas as pl
from jax.experimental.pallas import tpu as pltpu
from jax.sharding import PartitionSpec as P

F32, BF = jnp.float32, jnp.bfloat16
L, D, F, NP = 512, 768, 3072, 6
GC0, GC1 = 0.7978845608028654, 0.044715


def nn(a, b):
    return lax.dot_general(a, b, (((1,), (0,)), ((), ())), preferred_element_type=F32)


def nt(a, b):
    return lax.dot_general(a, b, (((1,), (1,)), ((), ())), preferred_element_type=F32)


def tn(a, b):
    return lax.dot_general(a, b, (((0,), (0,)), ((), ())), preferred_element_type=F32)


def rows_loop(n, step, f):
    def it(r, c):
        f(pl.multiple_of(r * step, step))
        return c
    lax.fori_loop(0, n // step, it, 0, unroll=2)


def mean(v):
    return jnp.sum(v, axis=-1, keepdims=True) * (1.0 / D)


class LaneSlots:
    def __init__(self, ref):
        self.ref = ref

    def __getitem__(self, p):
        return self.ref[0, :, pl.ds(pl.multiple_of(p * 128, 128), 128)]

    def __setitem__(self, p, value):
        self.ref[0, :, pl.ds(pl.multiple_of(p * 128, 128), 128)] = value


def qkv(x_ref, qit_ref, w_ref, sm, q_ref, k_ref, v_ref, qt_ref, kt_ref, vt_ref, b0, r0, rows):
    xb = x_ref[rows, :].astype(F32)
    qi = (b0 * jnp.tanh(xb * r0)).astype(BF)
    for p in range(NP):
        qit_ref[p * 128:(p + 1) * 128, rows] = qi[:, p * 128:(p + 1) * 128].T
    for m, (dst, tdst) in enumerate(((q_ref, qt_ref), (k_ref, kt_ref), (v_ref, vt_ref))):
        y = nn(qi, w_ref[m])
        if m == 0:
            y = (y + sm[0:1, :]).astype(BF).astype(F32) * 0.125
        if m == 2:
            y = y + sm[1:2, :]
        for p in range(NP):
            yp = y[:, p * 128:(p + 1) * 128].astype(BF)
            dst[p, rows, :] = yp
            tdst[p, :, rows] = yp.T


def attn_fwd(q_t, k_ref, v_t, p_ref, ctxt_ref, length):
    dead = (lax.broadcasted_iota(jnp.int32, (L, 128), 0) >= length) & (lax.broadcasted_iota(jnp.int32, (L, 128), 1) == 0)
    dead = jnp.where(dead, -1e9, 0.0).astype(BF)
    one = (lax.broadcasted_iota(jnp.int32, (128, L), 0) == 0).astype(F32).astype(BF)
    low = lax.broadcasted_iota(jnp.int32, (128, L), 0) < 64

    def pair(p, c):
        kp, qt, vt = jnp.concatenate([k_ref[p], dead], axis=1), q_t[p], v_t[p]
        for t in range(2):
            qm = jnp.where(low if t == 0 else ~low, qt, jnp.zeros_like(qt))
            s = nn(kp, jnp.concatenate([qm, one], axis=0))
            e = jnp.exp(s - jnp.max(s, axis=0, keepdims=True))
            pr = (e * (1.0 / jnp.sum(e, axis=0, keepdims=True))).astype(BF)
            p_ref[2 * p + t] = pr
            ctxt_ref[p, 64 * t:64 * t + 64, :] = nn(vt[64 * t:64 * t + 64, :], pr).astype(BF)
        return c
    lax.fori_loop(0, NP, pair, 0)


def out_proj(ctxt_ref, x_ref, wo_ref, sm, qct_ref, slc_ref, n1_ref, r1_ref, hid_ref, slh_ref, qh_ref, acc_ref, b1, i1, b2, i2):
    for p in range(NP):
        th = jnp.tanh(ctxt_ref[p].astype(F32) * i1)
        qct_ref[p * 128:(p + 1) * 128, :] = (b1 * th).astype(BF)
        slc_ref[:, p * 128:(p + 1) * 128] = (1.0 - th * th).astype(BF).T
    hid_ref[...] = tn(qct_ref[...], wo_ref[...])

    def f(r):
        rows = pl.ds(r, 64)
        v = hid_ref[rows, :] + sm[2:3, :] + x_ref[rows, :].astype(F32)
        c = v - mean(v)
        rr = lax.rsqrt(mean(c * c) + 1e-5)
        n = c * rr
        n1_ref[rows, :] = n
        r1_ref[rows, :] = jnp.broadcast_to(rr, (64, 128))
        h = n * sm[3:4, :] + sm[5:6, :]
        hid_ref[rows, :] = h
        th = jnp.tanh(h * i2)
        qh_ref[rows, :] = (b2 * th).astype(BF)
        slh_ref[rows, :] = (1.0 - th * th).astype(BF)
    rows_loop(L, 64, f)
    acc_ref[...] = jnp.zeros_like(acc_ref)


def ffn_fwd(qh_ref, w, sm, act_ref, dfac_ref, acc_ref, b3, i3, before, after):
    def chunk(c, _):
        s = before(c)
        bias = sm[pl.ds(8 + c, 1), :]
        for r in range(0, L, 256):
            rows = slice(r, r + 256)
            t = nn(qh_ref[rows, :], w[s]) + bias
            t2 = t * t
            th = jnp.tanh(t * (GC0 + (GC0 * GC1) * t2))
            hp = 0.5 + 0.5 * th
            u = t * hp
            cl = jnp.tanh(u * i3)
            act = (b3 * cl).astype(BF)
            d = hp + u * (1.0 - th) * (GC0 + (3 * GC0 * GC1) * t2)
            act_ref[c, rows, :] = act
            dfac_ref[c, rows, :] = (d * (1.0 - cl * cl)).astype(BF)
            acc_ref[rows, :] += nn(act, w[s + 1])
        after(c)
        return _
    lax.fori_loop(0, 4, chunk, 0)


def colsum(vec, row, val):
    vec[row:row + 1, :] += jnp.sum(val, axis=0, keepdims=True)


def ln2(acc_ref, hid_ref, ct_ref, sm, gb_ref, vec):
    def f(r):
        rows = pl.ds(r, 64)
        v = acc_ref[rows, :] + sm[7:8, :] + hid_ref[rows, :]
        c = v - mean(v)
        rr = lax.rsqrt(mean(c * c) + 1e-5)
        n = c * rr
        ct = ct_ref[rows, :].astype(F32)
        ct_ref[rows, :] = (n * sm[4:5, :] + sm[6:7, :]).astype(BF)
        colsum(vec, 4, ct * n)
        colsum(vec, 6, ct)
        q = ct * sm[4:5, :]
        gs = rr * (q - mean(q) - n * mean(q * n))
        hid_ref[rows, :] = gs
        gb = gs.astype(BF)
        gb_ref[rows, :] = gb
        colsum(vec, 7, gb.astype(F32))
    rows_loop(L, 64, f)


def ffn_bwd_out(gb_ref, act_ref, put):
    def chunk(c, _):
        put(c, tn(act_ref[c], gb_ref[...]))
        return _
    lax.fori_loop(0, 4, chunk, 0)


def ffn_bwd_in(c, gb_ref, win, wout, dfac_ref, acc_ref, qht_ref, put, vec):
    for r in range(0, L, 256):
        rows = slice(r, r + 256)
        gp = (nt(gb_ref[rows, :], wout[...]) * dfac_ref[c, rows, :].astype(F32)).astype(BF)
        dfac_ref[c, rows, :] = gp
        vec[pl.ds(8 + c, 1), :] += jnp.sum(gp.astype(F32), axis=0, keepdims=True)
        acc_ref[rows, :] += nt(gp, win[...])
    put(nn(qht_ref[...], dfac_ref[c]))


def ln1_bwd(acc_ref, gs_ref, slh_ref, n1_ref, r1_ref, sm, gat_ref, vec):
    def f(r):
        rows = pl.ds(r, 64)
        gh = gs_ref[rows, :] + acc_ref[rows, :] * slh_ref[rows, :].astype(F32)
        n = n1_ref[rows, :]
        colsum(vec, 3, gh * n)
        colsum(vec, 5, gh)
        q = gh * sm[3:4, :]
        gs = r1_ref[rows, 0:1] * (q - mean(q) - n * mean(q * n))
        gs_ref[rows, :] = gs
        gat = gs.astype(BF)
        gat_ref[rows, :] = gat
        colsum(vec, 2, gat.astype(F32))
    rows_loop(L, 64, f)


def out_bwd(gat_ref, wo_ref, qct_ref, slc_ref, dc_ref, dct_ref, put):
    put(nn(qct_ref[...], gat_ref[...]))
    g = nt(gat_ref[...], wo_ref[...])
    for p in range(NP):
        cols = slice(p * 128, (p + 1) * 128)
        d = (g[:, cols] * slc_ref[:, cols].astype(F32)).astype(BF)
        dc_ref[p] = d
        dct_ref[p] = d.T


def attn_bwd(q_ref, k_t, v_ref, dc_ref, dc_t, p_ref, dq_ref, dk_ref, dv_ref, service):
    low = lax.broadcasted_iota(jnp.int32, (128, L), 0) < 64
    lane_low = lax.broadcasted_iota(jnp.int32, (L, 128), 1) < 64

    def pair(p, c):
        qp, kt, vp, dc, dct = q_ref[p], k_t[p], v_ref[p], dc_ref[p], dc_t[p]
        res = []
        for t in range(2):
            dm = jnp.where(low if t == 0 else ~low, dct, jnp.zeros_like(dct))
            dp = nn(vp, dm)
            pr = p_ref[2 * p + t]
            prf = pr.astype(F32)
            delta = jnp.sum(dp * prf, axis=0, keepdims=True)
            ds = (prf * (dp - delta)).astype(BF)
            res.append((nn(pr, dc), nn(ds, qp), nn(kt[64 * t:64 * t + 64, :], ds) * 0.125))
        dv_ref[p] = jnp.where(lane_low, res[0][0], res[1][0]).astype(BF)
        dk_ref[p] = jnp.where(lane_low, res[0][1], res[1][1]).astype(BF)
        dq_ref[p] = jnp.concatenate([res[0][2], res[1][2]], axis=0).astype(BF).T
        service(p)
        return c
    lax.fori_loop(0, NP, pair, 0)


def lanes(ref):
    return jnp.concatenate([ref[p] for p in range(NP)], axis=1)


def qkv_bwd_x(x_ref, w_ref, dq_ref, dk_ref, dv_ref, gs_ref, acc_ref, vec, i0):
    for m, ref in enumerate((dq_ref, dk_ref, dv_ref)):
        d = lanes(ref)
        if m != 1:
            colsum(vec, m // 2, d.astype(F32))
        if m == 0:
            acc_ref[...] = nt(d, w_ref[m])
        else:
            acc_ref[...] += nt(d, w_ref[m])

    def f(r):
        rows = pl.ds(r, 64)
        th = jnp.tanh(x_ref[rows, :].astype(F32) * i0)
        x_ref[rows, :] = (gs_ref[rows, :] + acc_ref[rows, :] * (1.0 - th * th)).astype(BF)
    rows_loop(L, 64, f)


MESH = pl.DeviceIdType.MESH
SCHEDULE = {
    "f0": [(0, 0)],
    "f1": [(0, 1)],
    "f2": [(0, 4)],
    "ln": [(1, 0), (0, 5)],
    "a0": [(1, 1)],
    "a1": [(2, 0), (0, 7), (0, 3), (0, 6)],
    "a3": [(2, 1)],
    "a5": [(3, 0), (1, 5)],
    "x": [(9, 1), (0, 2), (4, 0)],
    "q0": [(9, 2), (1, 4), (2, 5), (0, 9), (1, 7)],
    "q1": [(0, 8), (3, 5), (1, 2), (9, 0), (3, 1), (1, 3)],
    "q2": [(2, 7), (4, 5), (0, 11), (1, 9)],
    "drain": [(3, 7), (2, 4), (4, 1), (2, 2), (0, 10), (2, 3), (3, 4), (2, 9), (4, 7), (3, 2), (1, 6), (4, 4), (3, 3), (1, 8),
        (1, 11), (4, 2), (1, 10), (3, 9), (2, 6), (4, 3), (2, 11), (3, 6), (4, 9), (3, 11), (2, 10), (2, 8), (4, 6), (3, 10), (4, 11),
        (3, 8), (4, 10), (4, 8)],
}
V_WITH = 9


def fused_kernel(n_dp, tok, cot, len_ref, rng_ref, wqkv, wo, win, wout, qvb, ob, gains, shifts, fib, fob,
                 outp, gxp, gw, vout,
                 sm, w, g, x_ref, ct_ref, qit_ref, q_ref, k_ref, v_ref, qt_ref, kt_ref, vt_ref, p_ref, ctxt_ref, qct_ref, slc_ref,
                 n1_ref, r1_ref, hid_ref, slh_ref, qh_ref, act_ref, dfac_ref, acc_ref, gb_ref, za, vec, vrecv, *rest):
    nb = n_dp.bit_length() - 1
    bufs, (wsem, locsem, a2s, a2r, gs_sem, gr_sem, zs_sem, zr_sem, vs_sem, vr_sem) = rest[:nb], rest[nb:]
    rs, nz, SEG = D // n_dp, 4, L // 4
    dp, z = lax.axis_index("dp"), lax.axis_index("head")
    bit = [(dp // (1 << b)) % 2 for b in range(nb)]
    buddy = [dp + (1 - 2 * bit[b]) * (1 << b) for b in range(nb)]
    z_near, z_cross, z_far = z + 1 - 2 * (z % 2), 3 - z, (z + 2) % 4
    peers = (z_near, z_far, z_cross)
    inner = (z + 1) // 2 == 1

    def at(dpi, zi):
        return {"dp": dpi, "head": zi}

    def load_w(slot, src):
        return pltpu.make_async_copy(src, w.at[slot], wsem.at[slot])

    def win_c(c):
        return win.at[:, pl.ds(pl.multiple_of(c * D, D), D)]

    def wout_c(c):
        return wout.at[pl.ds(pl.multiple_of(c * D, D), D), :]

    def seg(i):
        return pl.ds(pl.multiple_of(i * SEG, SEG), SEG)

    def to_seq(n, src, dst, j):
        return pltpu.make_async_remote_copy(src.at[peers[j]], dst.at[seg(z), :], a2s.at[n, j], a2r.at[n, j], device_id=at(dp, peers[j]),
                                            device_id_type=MESH)

    def to_seq_in(n, src, dst, j):
        return pltpu.make_async_remote_copy(src.at[peers[j]], dst.at[seg(peers[j]), :], a2s.at[n, j], a2r.at[n, j],
                                            device_id=at(dp, peers[j]), device_id_type=MESH)

    def to_pos(n, src, dst, j):
        return pltpu.make_async_remote_copy(src.at[seg(peers[j]), :], dst.at[z], a2s.at[n, j], a2r.at[n, j], device_id=at(dp, peers[j]),
                                            device_id_type=MESH)

    def to_pos_in(n, src, dst, j):
        return pltpu.make_async_remote_copy(src.at[seg(peers[j]), :], dst.at[peers[j]], a2s.at[n, j], a2r.at[n, j],
                                            device_id=at(dp, peers[j]), device_id_type=MESH)

    full = [g.reshape(*((8,) + (2,) * nb + (rs, D)))] + list(bufs)

    def order(i):
        up = list(range(1, nb))
        return [0] + (up if i % 2 == 0 else up[::-1])

    def slot(i, k):
        return i % 8 if k < 1 else i

    def pick(i, k, **vals):
        left = sorted(set(range(nb)) - set(order(i)[:k]), reverse=True)
        return (slot(i, k),) + tuple(vals.get(f"b{b}", slice(None)) for b in left)

    def red(i, k):
        b = order(i)[k]
        return pltpu.make_async_remote_copy(full[k].at[pick(i, k, **{f"b{b}": 1 - bit[b]})], full[k + 1].at[slot(i, k + 1)], gs_sem.at[k, i],
                                            gr_sem.at[k, i], device_id=at(buddy[b], z), device_id_type=MESH)

    def red_add(i, k):
        b = order(i)[k]
        red(i, k).wait_recv()
        if k + 1 < nb:
            n = order(i)[k + 1]
            for val in (1 - bit[n], bit[n]):
                d = pick(i, k + 1, **{f"b{n}": val})
                s = pick(i, k, **{f"b{b}": bit[b], f"b{n}": val})
                full[k + 1][d] = full[k + 1][d] + full[k][s]
                if val is not bit[n]:
                    red(i, k + 1).start()
        else:
            full[nb][i] = full[nb][i] + full[k][pick(i, k, **{f"b{b}": bit[b]})]
            pl.when(jnp.logical_not(inner))(zcopy(i, 0).start)

    def zcopy(i, k):
        src, dst, to = ((bufs[nb - 1], za, z_near), (za, gw, z_cross), (gw, gw, z_near))[k]
        return pltpu.make_async_remote_copy(src.at[i], dst.at[i], zs_sem.at[k, i], zr_sem.at[k, i], device_id=at(dp, to), device_id_type=MESH)

    def z_add(i, k):
        @pl.when(inner)
        def _():
            zcopy(i, k).wait_recv()
            if k == 0:
                za[i] = za[i] + bufs[nb - 1][i]
                zcopy(i, 1).start()
            else:
                gw[i] = gw[i] + za[i]
                zcopy(i, 2).start()

    def z_end(i):
        @pl.when(inner)
        def _():
            zcopy(i, 1).wait_send()
            zcopy(i, 2).wait_send()

        @pl.when(jnp.logical_not(inner))
        def _():
            zcopy(i, 2).wait_recv()
            zcopy(i, 0).wait_send()

    def vcopy(k):
        if k < nb:
            src, dst, to = vec.at[k], vrecv.at[k], at(buddy[order(V_WITH)[k]], z)
        else:
            src, dst, to = ((vec.at[nb], vrecv.at[nb], at(dp, z_near)), (vec.at[nb + 1], vrecv.at[nb + 1], at(dp, z_cross)),
                            (vout, vout, at(dp, z_near)))[k - nb]
        return pltpu.make_async_remote_copy(src, dst, vs_sem.at[k], vr_sem.at[k], device_id=to, device_id_type=MESH)

    def v_add(k):
        if k < nb:
            vcopy(k).wait_recv()
            vec[k + 1] = vec[k] + vrecv[k]
            if k + 1 < nb:
                vcopy(k + 1).start()
            else:
                pl.when(jnp.logical_not(inner))(vcopy(nb).start)
        else:
            @pl.when(inner)
            def _():
                vcopy(k).wait_recv()
                if k == nb:
                    vec[nb + 1] = vec[nb] + vrecv[nb]
                    vcopy(nb + 1).start()
                else:
                    vout[...] = vec[nb + 1] + vrecv[nb + 1]
                    vcopy(nb + 2).start()

    def v_end():
        for k in range(nb):
            vcopy(k).wait_send()

        @pl.when(inner)
        def _():
            vcopy(nb + 1).wait_send()
            vcopy(nb + 2).wait_send()

        @pl.when(jnp.logical_not(inner))
        def _():
            vcopy(nb).wait_send()
            vcopy(nb + 2).wait_recv()

    for m in range(3):
        load_w(m, wqkv.at[m]).start()
    own_tok = pltpu.make_async_copy(tok.at[z], x_ref.at[seg(z), :], locsem.at[0])
    own_tok.start()
    load_w(3, wo).start()
    load_w(4, win_c(0)).start()
    load_w(5, wout_c(0)).start()
    barrier = pltpu.get_barrier_semaphore()
    others = [at(buddy[b], z) for b in range(nb)] + [at(dp, p) for p in peers]
    for o in others:
        pl.semaphore_signal(barrier, inc=1, device_id=o, device_id_type=MESH)
    pl.semaphore_wait(barrier, len(others))
    for j in (1, 2, 0):
        to_seq(0, tok, x_ref, j).start()
    b = [jnp.full((1, 1), rng_ref[i], jnp.int32).astype(F32) * (1 / 16.0) for i in range(4)]
    iv = [1.0 / t for t in b]
    vec[0] = jnp.zeros_like(vec[0])
    sm[0:2, :] = qvb[...].astype(F32)
    sm[2:3, :] = ob[...].astype(F32).reshape(1, D)
    sm[3:5, :] = gains[...].astype(F32)
    sm[5:7, :] = shifts[...].astype(F32)
    sm[7:8, :] = fob[...].astype(F32).reshape(1, D)
    ffb = fib[...].astype(F32).reshape(1, F)
    for c in range(4):
        sm[8 + c:9 + c, :] = ffb[:, c * D:(c + 1) * D]
    v0 = vec.at[0]

    own_tok.wait()
    for m in range(3):
        load_w(m, wqkv.at[m]).wait()
    for j in range(4):
        if j:
            to_seq_in(0, tok, x_ref, j - 1).wait_recv()
        qkv(x_ref, qit_ref, w, sm, q_ref, k_ref, v_ref, qt_ref, kt_ref, vt_ref, b[0], iv[0], seg(peers[j - 1] if j else z))
    load_w(0, win_c(1)).start()
    load_w(1, wout_c(1)).start()
    own_cot = pltpu.make_async_copy(cot.at[z], ct_ref.at[seg(z), :], locsem.at[1])
    own_cot.start()
    for j in (1, 2, 0):
        to_seq(1, cot, ct_ref, j).start()
    attn_fwd(qt_ref, k_ref, vt_ref, p_ref, ctxt_ref, len_ref[z])
    load_w(3, wo).wait()
    out_proj(ctxt_ref, x_ref, w.at[3], sm, qct_ref, slc_ref, n1_ref, r1_ref, hid_ref, slh_ref, qh_ref, acc_ref, b[1], iv[1], b[2], iv[2])

    def w_slot(c):
        return 4 * (1 - c % 2)

    def fwd_wait(c):
        load_w(w_slot(c), win_c(c)).wait()
        load_w(w_slot(c) + 1, wout_c(c)).wait()
        return w_slot(c)

    def fwd_done(c):
        @pl.when(c < 2)
        def _():
            load_w(w_slot(c), win_c(c + 2)).start()
            load_w(w_slot(c) + 1, wout_c(c + 2)).start()

    ffn_fwd(qh_ref, w, sm, act_ref, dfac_ref, acc_ref, b[3], iv[3], fwd_wait, fwd_done)
    own_cot.wait()
    for j in range(3):
        to_seq_in(1, cot, ct_ref, j).wait_recv()
    ln2(acc_ref, hid_ref, ct_ref, sm, gb_ref, v0)
    own_out = pltpu.make_async_copy(ct_ref.at[seg(z), :], outp.at[z], locsem.at[2])
    own_out.start()
    for j in (1, 2, 0):
        to_pos(2, ct_ref, outp, j).start()

    def put_out(c, v):
        fr = 4 * rs
        for h in range(D // fr):
            for j in range(4):
                g[j, c * (D // fr) + h] = v[h * fr + j * rs:h * fr + (j + 1) * rs].astype(BF)

    def put(i, v):
        g[i % 8] = v.astype(BF).reshape(n_dp, rs, D)

    def at_point(point):
        for k, i in SCHEDULE.get(point, ()):
            if k == 9:
                to_pos(3, x_ref, gxp, i).start()
            elif k < nb:
                red_add(i, k)
            else:
                z_add(i, k - nb)
            if i == V_WITH and k != 9:
                v_add(k)

    ffn_bwd_out(gb_ref, act_ref, put_out)
    for i in range(4):
        red(i, 0).start()
    acc_ref[...] = jnp.zeros_like(acc_ref)
    qht = vt_ref.reshape(D, L)
    for p in range(NP):
        qht[p * 128:(p + 1) * 128, :] = qh_ref[:, p * 128:(p + 1) * 128].T
    at_point("fo")
    for j in range(4):
        c = 3 - j
        s = w_slot(c)
        if j >= 2:
            fwd_wait(c)
        ffn_bwd_in(c, gb_ref, w.at[s], w.at[s + 1], dfac_ref, acc_ref, qht, functools.partial(put, 4 + j), v0)
        red(4 + j, 0).start()
        if j < 2:
            load_w(s, win_c(c - 2)).start()
            load_w(s + 1, wout_c(c - 2)).start()
        if j == 2:
            load_w(0, wqkv.at[0]).start()
            load_w(1, wqkv.at[1]).start()
        at_point(f"f{j}")
    ln1_bwd(acc_ref, hid_ref, slh_ref, n1_ref, r1_ref, sm, gb_ref, v0)
    at_point("ln")
    dc = LaneSlots(act_ref)
    red(0, 0).wait_send()
    out_bwd(gb_ref, w.at[3], qct_ref, slc_ref, dc, vt_ref, functools.partial(put, 8))
    red(8, 0).start()
    at_point("ob")

    def service(p):
        for at_p in range(NP):
            if f"a{at_p}" in SCHEDULE:
                @pl.when(p == at_p)
                def _():
                    at_point(f"a{at_p}")

    attn_bwd(q_ref, kt_ref, v_ref, dc, vt_ref, p_ref, q_ref, k_ref, v_ref, service)
    for m in (0, 1):
        load_w(m, wqkv.at[m]).wait()
    qkv_bwd_x(x_ref, w, q_ref, k_ref, v_ref, hid_ref, acc_ref, v0, iv[0])
    vcopy(0).start()
    own_gx = pltpu.make_async_copy(x_ref.at[seg(z), :], gxp.at[z], locsem.at[3])
    own_gx.start()
    at_point("x")
    for m, ref in enumerate((q_ref, k_ref, v_ref)):
        red(1 + m, 0).wait_send()
        put(9 + m, nn(qit_ref[...], lanes(ref)))
        red(9 + m, 0).start()
        at_point(f"q{m}")
    at_point("drain")
    for i in range(12):
        z_end(i)
        for k in range(nb):
            if (k, i) not in ((0, 0), (0, 1), (0, 2), (0, 3)):
                red(i, k).wait_send()
    v_end()
    own_out.wait()
    own_gx.wait()
    for j in range(3):
        to_seq(0, tok, x_ref, j).wait_send()
        to_seq(1, cot, ct_ref, j).wait_send()
        to_pos(2, ct_ref, outp, j).wait_send()
        to_pos_in(2, ct_ref, outp, j).wait_recv()
        to_pos(3, x_ref, gxp, j).wait_send()
        to_pos_in(3, x_ref, gxp, j).wait_recv()


def fused(n_dp, *args):
    nb, rs = n_dp.bit_length() - 1, D // n_dp

    def vm(*s, d=BF):
        return pltpu.VMEM(s, d)
    dma = pltpu.SemaphoreType.DMA
    scratch = [vm(12, D, d=F32), vm(6, D, D), vm(8, n_dp, rs, D), vm(L, D), vm(L, D), vm(D, L), vm(6, L, 128), vm(6, L, 128), vm(6, L, 128), vm(6, 128, L),
               vm(6, 128, L), vm(6, 128, L), vm(12, L, L), vm(6, 128, L), vm(D, L), vm(L, D),
               vm(L, D, d=F32), vm(L, 128, d=F32), vm(L, D, d=F32), vm(L, D), vm(L, D), vm(4, L, D), vm(4, L, D), vm(L, D, d=F32),
               vm(L, D), vm(12, rs, D), vm(nb + 2, 16, D, d=F32), vm(nb + 2, 16, D, d=F32)]
    scratch += [vm(*((12,) + (2,) * (nb - k) + (rs, D))) for k in range(1, nb + 1)]
    scratch += [dma((6,)), dma((4,)), dma((4, 3)), dma((4, 3)), dma((nb, 12)), dma((nb, 12)), dma((3, 12)), dma((3, 12)), dma((nb + 3,)), dma((nb + 3,))]
    pos = jax.ShapeDtypeStruct((4, L // 4, D), BF)
    outs = [pos, pos, jax.ShapeDtypeStruct((12, rs, D), BF), jax.ShapeDtypeStruct((16, D), F32)]
    v, s, h = (pl.BlockSpec(memory_space=m) for m in (pltpu.VMEM, pltpu.SMEM, pl.ANY))
    return pl.pallas_call(
        functools.partial(fused_kernel, n_dp), out_shape=outs, in_specs=[h, h, s, s, h, h, h, h] + [v] * 6, out_specs=[h, h, v, v],
        scratch_shapes=scratch,
        compiler_params=pltpu.CompilerParams(collective_id=0, has_side_effects=True, vmem_limit_bytes=64 * 1024 * 1024 - 65536))(*args)


def finish_kernel(n_dp, outp, gxp, gw, vec, out, gx, gqkv, gqvb, gwo, gob, gains, shifts, gwin, gfib, gwout, gfob,
                  seq_in, gw_in, tmp, seq_out, gx_out, gw_out, isem, osem):
    rs = D // n_dp
    i = lax.axis_index("dp")
    ins = [pltpu.make_async_copy(outp, seq_in.at[0], isem.at[0]), pltpu.make_async_copy(gw, gw_in, isem.at[1]),
           pltpu.make_async_copy(gxp, seq_in.at[1], isem.at[2])]
    for c in ins:
        c.start()
    outs = []

    def send(src, dst):
        c = pltpu.make_async_copy(src, dst, osem.at[len(outs)])
        c.start()
        outs.append(c)

    v, fib = vec[0:8, :], vec[8:12, :]
    mine, f = jnp.zeros((8, rs), F32), jnp.zeros((1, 4 * rs), F32)
    per = D // (4 * rs)
    for k in range(n_dp):
        mine = jnp.where(i == k, v[:, k * rs:(k + 1) * rs], mine)
        f = jnp.where(i == k, fib[k // per:k // per + 1, (k % per) * 4 * rs:(k % per + 1) * 4 * rs], f)
    gqvb[...] = mine[0:2]
    gob[...] = mine[2:3]
    gains[...] = mine[3:5]
    shifts[...] = mine[5:7]
    gfob[...] = mine[7:8]
    gfib[...] = f.reshape(4 * rs)
    ins[0].wait()
    for s in range(4):
        tmp[:, s, :] = seq_in[0, s].astype(F32)
    seq_out[...] = tmp[...].astype(BF)
    send(seq_out, out)
    ins[1].wait()
    for k in range(12):
        gw_out[k] = gw_in[k].astype(F32)
        if k < 4:
            send(gw_out.at[k], gwout.at[pl.ds(k * rs, rs), :])
        elif k < 8:
            send(gw_out.at[k], gwin.at[:, pl.ds((7 - k) * D, D)])
        elif k == 8:
            send(gw_out.at[k], gwo)
        else:
            send(gw_out.at[k], gqkv.at[k - 9])
    ins[2].wait()
    for s in range(4):
        gx_out[:, s, :] = seq_in[1, s].astype(F32)
    send(gx_out, gx)
    for c in outs:
        c.wait()


def finish(n_dp, *args):
    rs, seg = D // n_dp, L // 4
    shapes = [((seg, 4, D), BF), ((seg, 4, D), F32)]
    shapes += [(s, F32) for s in ((3, rs, D), (2, rs), (rs, D), (1, rs), (2, rs), (2, rs), (rs, F), (4 * rs,), (4 * rs, D), (1, rs))]
    v, h = pl.BlockSpec(memory_space=pltpu.VMEM), pl.BlockSpec(memory_space=pl.ANY)
    vm, dma = pltpu.VMEM, pltpu.SemaphoreType.DMA
    return pl.pallas_call(
        functools.partial(finish_kernel, n_dp), out_shape=[jax.ShapeDtypeStruct(s, d) for s, d in shapes], in_specs=[h, h, h, v],
        out_specs=[h, h, h, v, h, v, v, v, h, v, h, v],
        scratch_shapes=[vm((2, 4, seg, D), BF), vm((12, rs, D), BF), vm((seg, 4, D), F32), vm((seg, 4, D), BF), vm((seg, 4, D), F32),
                        vm((12, rs, D), F32), dma((3,)), dma((14,))],
        compiler_params=pltpu.CompilerParams(vmem_limit_bytes=60 * 1024 * 1024))(*args)


def on_device(n_dp, tokens, lengths, ranges, qkv_weight, qv_bias, out_weight, out_bias, norm_gains, norm_shifts, ffn_in, ffn_in_bias,
              ffn_out, ffn_out_bias, cotangent):
    res = finish(n_dp, *fused(n_dp, tokens.transpose(1, 0, 2), cotangent.transpose(1, 0, 2), lengths, ranges, qkv_weight, out_weight,
                              ffn_in, ffn_out, qv_bias, out_bias, norm_gains, norm_shifts, ffn_in_bias, ffn_out_bias))
    return tuple(r[0] if n in (5, 11) else r for n, r in enumerate(res))


def local_kernel(x_ref, ct_ref, len_ref, rng_ref, w_ref, sm, gx_ref, g_ref, vec_ref, w, qit_ref, q_ref, k_ref, v_ref, qt_ref, kt_ref, vt_ref,
                 p_ref, ctxt_ref, qct_ref, slc_ref, n1_ref, r1_ref, hid_ref, slh_ref, qh_ref, act_ref, dfac_ref, acc_ref, gb_ref, stage,
                 wsem, gsem):
    def fetch(slot, i):
        cp = pltpu.make_async_copy(w_ref.at[i], w.at[slot], wsem)
        cp.start()
        cp.wait()

    def put(i, v):
        stage[...] = v.astype(BF)
        cp = pltpu.make_async_copy(stage, g_ref.at[i], gsem)
        cp.start()
        cp.wait()

    b = [jnp.full((1, 1), rng_ref[i], jnp.int32).astype(F32) * (1 / 16.0) for i in range(4)]
    iv = [1.0 / t for t in b]
    vec_ref[...] = jnp.zeros_like(vec_ref)
    for m in range(4):
        fetch(m, 8 + (m + 1) % 4 if m < 3 else 8)
    for r in range(0, L, 256):
        qkv(x_ref, qit_ref, w, sm, q_ref, k_ref, v_ref, qt_ref, kt_ref, vt_ref, b[0], iv[0], slice(r, r + 256))
    attn_fwd(qt_ref, k_ref, vt_ref, p_ref, ctxt_ref, len_ref[0])
    out_proj(ctxt_ref, x_ref, w.at[3], sm, qct_ref, slc_ref, n1_ref, r1_ref, hid_ref, slh_ref, qh_ref, acc_ref, b[1], iv[1], b[2], iv[2])

    def before(c):
        fetch(4, c)
        fetch(5, 4 + c)
        return 4

    ffn_fwd(qh_ref, w, sm, act_ref, dfac_ref, acc_ref, b[3], iv[3], before, lambda c: None)
    ln2(acc_ref, hid_ref, ct_ref, sm, gb_ref, vec_ref)
    qht = vt_ref.reshape(D, L)
    for p in range(NP):
        qht[p * 128:(p + 1) * 128, :] = qh_ref[:, p * 128:(p + 1) * 128].T
    ffn_bwd_out(gb_ref, act_ref, lambda c, v: put(4 + c, v))
    acc_ref[...] = jnp.zeros_like(acc_ref)
    for c in range(4):
        before(c)
        ffn_bwd_in(c, gb_ref, w.at[4], w.at[5], dfac_ref, acc_ref, qht, functools.partial(put, c), vec_ref)
    ln1_bwd(acc_ref, hid_ref, slh_ref, n1_ref, r1_ref, sm, gb_ref, vec_ref)
    dc = LaneSlots(act_ref)
    out_bwd(gb_ref, w.at[3], qct_ref, slc_ref, dc, vt_ref, functools.partial(put, 8))
    attn_bwd(q_ref, kt_ref, v_ref, dc, vt_ref, p_ref, q_ref, k_ref, v_ref, lambda p: None)
    qkv_bwd_x(x_ref, w, q_ref, k_ref, v_ref, hid_ref, acc_ref, vec_ref, iv[0])
    for m, ref in enumerate((q_ref, k_ref, v_ref)):
        put(9 + m, nn(qit_ref[...], lanes(ref)))
    gx_ref[...] = x_ref[...]


def local(x, ct, length, ranges, weights, small):
    def vm(*s, d=BF):
        return pltpu.VMEM(s, d)
    scratch = [vm(6, D, D), vm(D, L), vm(6, L, 128), vm(6, L, 128), vm(6, L, 128), vm(6, 128, L),
               vm(6, 128, L), vm(6, 128, L), vm(12, L, L), vm(6, 128, L), vm(D, L), vm(L, D),
               vm(L, D, d=F32), vm(L, 128, d=F32), vm(L, D, d=F32), vm(L, D), vm(L, D), vm(4, L, D), vm(4, L, D), vm(L, D, d=F32),
               vm(L, D), vm(D, D), pltpu.SemaphoreType.DMA, pltpu.SemaphoreType.DMA]
    outs = [jax.ShapeDtypeStruct((L, D), BF), jax.ShapeDtypeStruct((L, D), BF), jax.ShapeDtypeStruct((12, D, D), BF),
            jax.ShapeDtypeStruct((16, D), F32)]
    v, s, h = (pl.BlockSpec(memory_space=m) for m in (pltpu.VMEM, pltpu.SMEM, pl.ANY))

    def body(x_in, ct_in, len_ref, rng_ref, w_ref, sm, out_ref, gx_ref, g_ref, vec_ref, x_ref, *rest):
        x_ref[...] = x_in[...]
        out_ref[...] = ct_in[...]
        local_kernel(x_ref, out_ref, len_ref, rng_ref, w_ref, sm, gx_ref, g_ref, vec_ref, *rest)

    return pl.pallas_call(
        body, out_shape=outs, in_specs=[v, v, s, s, h, v], out_specs=[v, v, h, v], scratch_shapes=[vm(L, D)] + scratch,
        compiler_params=pltpu.CompilerParams(vmem_limit_bytes=60 * 1024 * 1024))(x, ct, length, ranges, weights, small)


def on_device_local(n_dp, tokens, lengths, ranges, qkv_weight, qv_bias, out_weight, out_bias, norm_gains, norm_shifts, ffn_in, ffn_in_bias,
                    ffn_out, ffn_out_bias, cotangent):
    def to_seq(a):
        return lax.all_to_all(a.transpose(1, 0, 2), "head", split_axis=0, concat_axis=1, tiled=True)[0]

    def to_pos(a):
        return lax.all_to_all(a[None], "head", split_axis=1, concat_axis=0, tiled=True).transpose(1, 0, 2)

    small = jnp.concatenate([qv_bias, out_bias[None], norm_gains, norm_shifts, ffn_out_bias[None], ffn_in_bias.reshape(4, D)]).astype(F32)
    weights = jnp.concatenate([ffn_in.reshape(D, 4, D).transpose(1, 0, 2), ffn_out.reshape(4, D, D), out_weight[None], qkv_weight])
    length = lax.dynamic_slice(lengths, (lax.axis_index("head"),), (1,))
    out, gx, g, vec = local(to_seq(tokens), to_seq(cotangent), length, ranges, weights, small)
    rs = D // n_dp
    wout = lax.psum_scatter(g[4:8].reshape(4 * D, D), "dp", scatter_dimension=0, tiled=True)
    rest = lax.psum_scatter(jnp.concatenate([g[0:4], g[8:12]]), "dp", scatter_dimension=1, tiled=True)
    both = lax.psum(jnp.concatenate([wout, rest.reshape(8 * rs, D)]), "head").astype(F32)
    wout, rest = both[:4 * rs], both[4 * rs:].reshape(8, rs, D)
    vec = lax.psum(vec, ("dp", "head"))
    i = lax.axis_index("dp")

    def mine(v):
        return lax.dynamic_slice_in_dim(v, i * rs, rs, axis=-1)
    fib = lax.dynamic_slice(vec[8:12].reshape(-1), (i * 4 * rs,), (4 * rs,))
    return (to_pos(out), to_pos(gx).astype(F32), rest[5:8], mine(vec[0:2]), rest[4], mine(vec[2]), mine(vec[3:5]), mine(vec[5:7]),
            rest[0:4].transpose(1, 0, 2).reshape(rs, F), fib, wout, mine(vec[7]))


def solution(mesh):
    n_dp = mesh.shape["dp"]
    tok = P("head", "dp", None)
    body = on_device if D // n_dp % 16 == 0 else on_device_local
    return jax.shard_map(
        functools.partial(body, n_dp),
        mesh=mesh,
        in_specs=(tok, P("dp")) + (P(),) * 11 + (tok,),
        out_specs=(tok, tok, P(None, "dp", None), P(None, "dp"), P("dp", None), P("dp"), P(None, "dp"), P(None, "dp"),
                   P("dp", None), P("dp"), P("dp", None), P("dp")),
        check_vma=False,
    )
```

```python
import functools
import jax
import jax.numpy as jnp
from jax import lax
from jax.experimental import pallas as pl
from jax.experimental.pallas import tpu as pltpu
from jax.sharding import PartitionSpec as P

F32, BF = jnp.float32, jnp.bfloat16
L, D, F, NP = 512, 768, 3072, 6
GC0, GC1 = 0.7978845608028654, 0.044715


def nn(a, b):
    return lax.dot_general(a, b, (((1,), (0,)), ((), ())), preferred_element_type=F32)


def nt(a, b):
    return lax.dot_general(a, b, (((1,), (1,)), ((), ())), preferred_element_type=F32)


def tn(a, b):
    return lax.dot_general(a, b, (((0,), (0,)), ((), ())), preferred_element_type=F32)


def rows_loop(n, step, f):
    def it(r, c):
        f(pl.multiple_of(r * step, step))
        return c
    lax.fori_loop(0, n // step, it, 0, unroll=2)


def mean(v):
    return jnp.sum(v, axis=-1, keepdims=True) * (1.0 / D)


class LaneSlots:
    def __init__(self, ref):
        self.ref = ref

    def __getitem__(self, p):
        return self.ref[0, :, pl.ds(pl.multiple_of(p * 128, 128), 128)]

    def __setitem__(self, p, value):
        self.ref[0, :, pl.ds(pl.multiple_of(p * 128, 128), 128)] = value


def qkv(x_ref, qit_ref, w_ref, sm, q_ref, k_ref, v_ref, qt_ref, kt_ref, vt_ref, b0, r0, rows):
    xb = x_ref[rows, :].astype(F32)
    qi = (b0 * jnp.tanh(xb * r0)).astype(BF)
    for p in range(NP):
        qit_ref[p * 128:(p + 1) * 128, rows] = qi[:, p * 128:(p + 1) * 128].T
    for m, (dst, tdst) in enumerate(((q_ref, qt_ref), (k_ref, kt_ref), (v_ref, vt_ref))):
        y = nn(qi, w_ref[m])
        if m == 0:
            y = (y + sm[0:1, :]).astype(BF).astype(F32) * 0.125
        if m == 2:
            y = y + sm[1:2, :]
        for p in range(NP):
            yp = y[:, p * 128:(p + 1) * 128].astype(BF)
            dst[p, rows, :] = yp
            tdst[p, :, rows] = yp.T


def attn_fwd(q_t, k_ref, v_t, p_ref, ctxt_ref, length):
    dead = (lax.broadcasted_iota(jnp.int32, (L, 128), 0) >= length) & (lax.broadcasted_iota(jnp.int32, (L, 128), 1) == 0)
    dead = jnp.where(dead, -1e9, 0.0).astype(BF)
    one = (lax.broadcasted_iota(jnp.int32, (128, L), 0) == 0).astype(F32).astype(BF)
    low = lax.broadcasted_iota(jnp.int32, (128, L), 0) < 64

    def pair(p, c):
        kp, qt, vt = jnp.concatenate([k_ref[p], dead], axis=1), q_t[p], v_t[p]
        for t in range(2):
            qm = jnp.where(low if t == 0 else ~low, qt, jnp.zeros_like(qt))
            s = nn(kp, jnp.concatenate([qm, one], axis=0))
            e = jnp.exp(s - jnp.max(s, axis=0, keepdims=True))
            pr = (e * (1.0 / jnp.sum(e, axis=0, keepdims=True))).astype(BF)
            p_ref[2 * p + t] = pr
            ctxt_ref[p, 64 * t:64 * t + 64, :] = nn(vt[64 * t:64 * t + 64, :], pr).astype(BF)
        return c
    lax.fori_loop(0, NP, pair, 0)


def out_proj(ctxt_ref, x_ref, wo_ref, sm, qct_ref, slc_ref, n1_ref, r1_ref, hid_ref, slh_ref, qh_ref, acc_ref, b1, i1, b2, i2):
    for p in range(NP):
        th = jnp.tanh(ctxt_ref[p].astype(F32) * i1)
        qct_ref[p * 128:(p + 1) * 128, :] = (b1 * th).astype(BF)
        slc_ref[:, p * 128:(p + 1) * 128] = (1.0 - th * th).astype(BF).T
    hid_ref[...] = tn(qct_ref[...], wo_ref[...])

    def f(r):
        rows = pl.ds(r, 64)
        v = hid_ref[rows, :] + sm[2:3, :] + x_ref[rows, :].astype(F32)
        c = v - mean(v)
        rr = lax.rsqrt(mean(c * c) + 1e-5)
        n = c * rr
        n1_ref[rows, :] = n
        r1_ref[rows, :] = jnp.broadcast_to(rr, (64, 128))
        h = n * sm[3:4, :] + sm[5:6, :]
        hid_ref[rows, :] = h
        th = jnp.tanh(h * i2)
        qh_ref[rows, :] = (b2 * th).astype(BF)
        slh_ref[rows, :] = (1.0 - th * th).astype(BF)
    rows_loop(L, 64, f)
    acc_ref[...] = jnp.zeros_like(acc_ref)


def ffn_fwd(qh_ref, w, sm, act_ref, dfac_ref, acc_ref, b3, i3, before, after):
    def chunk(c, _):
        s = before(c)
        bias = sm[pl.ds(8 + c, 1), :]
        for r in range(0, L, 256):
            rows = slice(r, r + 256)
            t = nn(qh_ref[rows, :], w[s]) + bias
            t2 = t * t
            th = jnp.tanh(t * (GC0 + (GC0 * GC1) * t2))
            hp = 0.5 + 0.5 * th
            u = t * hp
            cl = jnp.tanh(u * i3)
            act = (b3 * cl).astype(BF)
            d = hp + u * (1.0 - th) * (GC0 + (3 * GC0 * GC1) * t2)
            act_ref[c, rows, :] = act
            dfac_ref[c, rows, :] = (d * (1.0 - cl * cl)).astype(BF)
            acc_ref[rows, :] += nn(act, w[s + 1])
        after(c)
        return _
    lax.fori_loop(0, 4, chunk, 0)


def colsum(vec, row, val):
    vec[row:row + 1, :] += jnp.sum(val, axis=0, keepdims=True)


def ln2(acc_ref, hid_ref, ct_ref, sm, gb_ref, vec):
    def f(r):
        rows = pl.ds(r, 64)
        v = acc_ref[rows, :] + sm[7:8, :] + hid_ref[rows, :]
        c = v - mean(v)
        rr = lax.rsqrt(mean(c * c) + 1e-5)
        n = c * rr
        ct = ct_ref[rows, :].astype(F32)
        ct_ref[rows, :] = (n * sm[4:5, :] + sm[6:7, :]).astype(BF)
        colsum(vec, 4, ct * n)
        colsum(vec, 6, ct)
        q = ct * sm[4:5, :]
        gs = rr * (q - mean(q) - n * mean(q * n))
        hid_ref[rows, :] = gs
        gb = gs.astype(BF)
        gb_ref[rows, :] = gb
        colsum(vec, 7, gb.astype(F32))
    rows_loop(L, 64, f)


def ffn_bwd_out(gb_ref, act_ref, put):
    def chunk(c, _):
        put(c, tn(act_ref[c], gb_ref[...]))
        return _
    lax.fori_loop(0, 4, chunk, 0)


def ffn_bwd_in(c, gb_ref, win, wout, dfac_ref, acc_ref, qht_ref, put, vec):
    for r in range(0, L, 256):
        rows = slice(r, r + 256)
        gp = (nt(gb_ref[rows, :], wout[...]) * dfac_ref[c, rows, :].astype(F32)).astype(BF)
        dfac_ref[c, rows, :] = gp
        vec[pl.ds(8 + c, 1), :] += jnp.sum(gp.astype(F32), axis=0, keepdims=True)
        acc_ref[rows, :] += nt(gp, win[...])
    put(nn(qht_ref[...], dfac_ref[c]))


def ln1_bwd(acc_ref, gs_ref, slh_ref, n1_ref, r1_ref, sm, gat_ref, vec):
    def f(r):
        rows = pl.ds(r, 64)
        gh = gs_ref[rows, :] + acc_ref[rows, :] * slh_ref[rows, :].astype(F32)
        n = n1_ref[rows, :]
        colsum(vec, 3, gh * n)
        colsum(vec, 5, gh)
        q = gh * sm[3:4, :]
        gs = r1_ref[rows, 0:1] * (q - mean(q) - n * mean(q * n))
        gs_ref[rows, :] = gs
        gat = gs.astype(BF)
        gat_ref[rows, :] = gat
        colsum(vec, 2, gat.astype(F32))
    rows_loop(L, 64, f)


def out_bwd(gat_ref, wo_ref, qct_ref, slc_ref, dc_ref, dct_ref, put):
    put(nn(qct_ref[...], gat_ref[...]))
    g = nt(gat_ref[...], wo_ref[...])
    for p in range(NP):
        cols = slice(p * 128, (p + 1) * 128)
        d = (g[:, cols] * slc_ref[:, cols].astype(F32)).astype(BF)
        dc_ref[p] = d
        dct_ref[p] = d.T


def attn_bwd(q_ref, k_t, v_ref, dc_ref, dc_t, p_ref, dq_ref, dk_ref, dv_ref, service):
    low = lax.broadcasted_iota(jnp.int32, (128, L), 0) < 64
    lane_low = lax.broadcasted_iota(jnp.int32, (L, 128), 1) < 64

    def pair(p, c):
        qp, kt, vp, dc, dct = q_ref[p], k_t[p], v_ref[p], dc_ref[p], dc_t[p]
        res = []
        for t in range(2):
            dm = jnp.where(low if t == 0 else ~low, dct, jnp.zeros_like(dct))
            dp = nn(vp, dm)
            pr = p_ref[2 * p + t]
            prf = pr.astype(F32)
            delta = jnp.sum(dp * prf, axis=0, keepdims=True)
            ds = (prf * (dp - delta)).astype(BF)
            res.append((nn(pr, dc), nn(ds, qp), nn(kt[64 * t:64 * t + 64, :], ds) * 0.125))
        dv_ref[p] = jnp.where(lane_low, res[0][0], res[1][0]).astype(BF)
        dk_ref[p] = jnp.where(lane_low, res[0][1], res[1][1]).astype(BF)
        dq_ref[p] = jnp.concatenate([res[0][2], res[1][2]], axis=0).astype(BF).T
        service(p)
        return c
    lax.fori_loop(0, NP, pair, 0)


def lanes(ref):
    return jnp.concatenate([ref[p] for p in range(NP)], axis=1)


def qkv_bwd_x(x_ref, w_ref, dq_ref, dk_ref, dv_ref, gs_ref, acc_ref, vec, i0):
    for m, ref in enumerate((dq_ref, dk_ref, dv_ref)):
        d = lanes(ref)
        if m != 1:
            colsum(vec, m // 2, d.astype(F32))
        if m == 0:
            acc_ref[...] = nt(d, w_ref[m])
        else:
            acc_ref[...] += nt(d, w_ref[m])

    def f(r):
        rows = pl.ds(r, 64)
        th = jnp.tanh(x_ref[rows, :].astype(F32) * i0)
        x_ref[rows, :] = (gs_ref[rows, :] + acc_ref[rows, :] * (1.0 - th * th)).astype(BF)
    rows_loop(L, 64, f)


MESH = pl.DeviceIdType.MESH
SCHEDULE = {
    "f0": [(0, 0)],
    "f1": [(0, 1)],
    "f2": [(0, 4)],
    "ln": [(1, 0), (0, 5)],
    "a0": [(1, 1)],
    "a1": [(2, 0), (0, 7), (0, 3), (0, 6)],
    "a3": [(2, 1)],
    "a5": [(3, 0), (1, 5)],
    "x": [(9, 1), (0, 2), (4, 0)],
    "q0": [(9, 2), (1, 4), (2, 5), (0, 9), (1, 7)],
    "q1": [(0, 8), (3, 5), (1, 2), (9, 0), (3, 1), (1, 3)],
    "q2": [(2, 7), (4, 5), (0, 11), (1, 9)],
    "drain": [(3, 7), (2, 4), (4, 1), (2, 2), (0, 10), (2, 3), (3, 4), (2, 9), (4, 7), (3, 2), (1, 6), (4, 4), (3, 3), (1, 8),
        (1, 11), (4, 2), (1, 10), (3, 9), (2, 6), (4, 3), (2, 11), (3, 6), (4, 9), (3, 11), (2, 10), (2, 8), (4, 6), (3, 10), (4, 11),
        (3, 8), (4, 10), (4, 8)],
}
V_WITH = 9


def fused_kernel(n_dp, tok, cot, len_ref, rng_ref, wqkv, wo, win, wout, qvb, ob, gains, shifts, fib, fob,
                 outp, gxp, gw, vout,
                 sm, w, g, x_ref, ct_ref, qit_ref, q_ref, k_ref, v_ref, qt_ref, kt_ref, vt_ref, p_ref, ctxt_ref, qct_ref, slc_ref,
                 n1_ref, r1_ref, hid_ref, slh_ref, qh_ref, act_ref, dfac_ref, acc_ref, gb_ref, za, vec, vrecv, *rest):
    nb = n_dp.bit_length() - 1
    bufs, (wsem, locsem, a2s, a2r, gs_sem, gr_sem, zs_sem, zr_sem, vs_sem, vr_sem) = rest[:nb], rest[nb:]
    rs, nz, SEG = D // n_dp, 4, L // 4
    dp, z = lax.axis_index("dp"), lax.axis_index("head")
    bit = [(dp // (1 << b)) % 2 for b in range(nb)]
    buddy = [dp + (1 - 2 * bit[b]) * (1 << b) for b in range(nb)]
    z_near, z_cross, z_far = z + 1 - 2 * (z % 2), 3 - z, (z + 2) % 4
    peers = (z_near, z_far, z_cross)
    inner = (z + 1) // 2 == 1

    def at(dpi, zi):
        return {"dp": dpi, "head": zi}

    def load_w(slot, src):
        return pltpu.make_async_copy(src, w.at[slot], wsem.at[slot])

    def win_c(c):
        return win.at[:, pl.ds(pl.multiple_of(c * D, D), D)]

    def wout_c(c):
        return wout.at[pl.ds(pl.multiple_of(c * D, D), D), :]

    def seg(i):
        return pl.ds(pl.multiple_of(i * SEG, SEG), SEG)

    def to_seq(n, src, dst, j):
        return pltpu.make_async_remote_copy(src.at[peers[j]], dst.at[seg(z), :], a2s.at[n, j], a2r.at[n, j], device_id=at(dp, peers[j]),
                                            device_id_type=MESH)

    def to_seq_in(n, src, dst, j):
        return pltpu.make_async_remote_copy(src.at[peers[j]], dst.at[seg(peers[j]), :], a2s.at[n, j], a2r.at[n, j],
                                            device_id=at(dp, peers[j]), device_id_type=MESH)

    def to_pos(n, src, dst, j):
        return pltpu.make_async_remote_copy(src.at[seg(peers[j]), :], dst.at[z], a2s.at[n, j], a2r.at[n, j], device_id=at(dp, peers[j]),
                                            device_id_type=MESH)

    def to_pos_in(n, src, dst, j):
        return pltpu.make_async_remote_copy(src.at[seg(peers[j]), :], dst.at[peers[j]], a2s.at[n, j], a2r.at[n, j],
                                            device_id=at(dp, peers[j]), device_id_type=MESH)

    full = [g.reshape(*((8,) + (2,) * nb + (rs, D)))] + list(bufs)

    def order(i):
        up = list(range(1, nb))
        return [0] + (up if i % 2 == 0 else up[::-1])

    def slot(i, k):
        return i % 8 if k < 1 else i

    def pick(i, k, **vals):
        left = sorted(set(range(nb)) - set(order(i)[:k]), reverse=True)
        return (slot(i, k),) + tuple(vals.get(f"b{b}", slice(None)) for b in left)

    def red(i, k):
        b = order(i)[k]
        return pltpu.make_async_remote_copy(full[k].at[pick(i, k, **{f"b{b}": 1 - bit[b]})], full[k + 1].at[slot(i, k + 1)], gs_sem.at[k, i],
                                            gr_sem.at[k, i], device_id=at(buddy[b], z), device_id_type=MESH)

    def red_add(i, k):
        b = order(i)[k]
        red(i, k).wait_recv()
        if k + 1 < nb:
            n = order(i)[k + 1]
            for val in (1 - bit[n], bit[n]):
                d = pick(i, k + 1, **{f"b{n}": val})
                s = pick(i, k, **{f"b{b}": bit[b], f"b{n}": val})
                full[k + 1][d] = full[k + 1][d] + full[k][s]
                if val is not bit[n]:
                    red(i, k + 1).start()
        else:
            full[nb][i] = full[nb][i] + full[k][pick(i, k, **{f"b{b}": bit[b]})]
            pl.when(jnp.logical_not(inner))(zcopy(i, 0).start)

    def zcopy(i, k):
        src, dst, to = ((bufs[nb - 1], za, z_near), (za, gw, z_cross), (gw, gw, z_near))[k]
        return pltpu.make_async_remote_copy(src.at[i], dst.at[i], zs_sem.at[k, i], zr_sem.at[k, i], device_id=at(dp, to), device_id_type=MESH)

    def z_add(i, k):
        @pl.when(inner)
        def _():
            zcopy(i, k).wait_recv()
            if k == 0:
                za[i] = za[i] + bufs[nb - 1][i]
                zcopy(i, 1).start()
            else:
                gw[i] = gw[i] + za[i]
                zcopy(i, 2).start()

    def z_end(i):
        @pl.when(inner)
        def _():
            zcopy(i, 1).wait_send()
            zcopy(i, 2).wait_send()

        @pl.when(jnp.logical_not(inner))
        def _():
            zcopy(i, 2).wait_recv()
            zcopy(i, 0).wait_send()

    def vcopy(k):
        if k < nb:
            src, dst, to = vec.at[k], vrecv.at[k], at(buddy[order(V_WITH)[k]], z)
        else:
            src, dst, to = ((vec.at[nb], vrecv.at[nb], at(dp, z_near)), (vec.at[nb + 1], vrecv.at[nb + 1], at(dp, z_cross)),
                            (vout, vout, at(dp, z_near)))[k - nb]
        return pltpu.make_async_remote_copy(src, dst, vs_sem.at[k], vr_sem.at[k], device_id=to, device_id_type=MESH)

    def v_add(k):
        if k < nb:
            vcopy(k).wait_recv()
            vec[k + 1] = vec[k] + vrecv[k]
            if k + 1 < nb:
                vcopy(k + 1).start()
            else:
                pl.when(jnp.logical_not(inner))(vcopy(nb).start)
        else:
            @pl.when(inner)
            def _():
                vcopy(k).wait_recv()
                if k == nb:
                    vec[nb + 1] = vec[nb] + vrecv[nb]
                    vcopy(nb + 1).start()
                else:
                    vout[...] = vec[nb + 1] + vrecv[nb + 1]
                    vcopy(nb + 2).start()

    def v_end():
        for k in range(nb):
            vcopy(k).wait_send()

        @pl.when(inner)
        def _():
            vcopy(nb + 1).wait_send()
            vcopy(nb + 2).wait_send()

        @pl.when(jnp.logical_not(inner))
        def _():
            vcopy(nb).wait_send()
            vcopy(nb + 2).wait_recv()

    for m in range(3):
        load_w(m, wqkv.at[m]).start(priority=1)
    own_tok = pltpu.make_async_copy(tok.at[z], x_ref.at[seg(z), :], locsem.at[0])
    own_tok.start()
    load_w(3, wo).start(priority=1)
    load_w(4, win_c(0)).start(priority=1)
    load_w(5, wout_c(0)).start(priority=1)
    barrier = pltpu.get_barrier_semaphore()
    others = [at(buddy[b], z) for b in range(nb)] + [at(dp, p) for p in peers]
    for o in others:
        pl.semaphore_signal(barrier, inc=1, device_id=o, device_id_type=MESH)
    pl.semaphore_wait(barrier, len(others))
    for j in (1, 2, 0):
        to_seq(0, tok, x_ref, j).start()
    b = [jnp.full((1, 1), rng_ref[i], jnp.int32).astype(F32) * (1 / 16.0) for i in range(4)]
    iv = [1.0 / t for t in b]
    vec[0] = jnp.zeros_like(vec[0])
    sm[0:2, :] = qvb[...].astype(F32)
    sm[2:3, :] = ob[...].astype(F32).reshape(1, D)
    sm[3:5, :] = gains[...].astype(F32)
    sm[5:7, :] = shifts[...].astype(F32)
    sm[7:8, :] = fob[...].astype(F32).reshape(1, D)
    ffb = fib[...].astype(F32).reshape(1, F)
    for c in range(4):
        sm[8 + c:9 + c, :] = ffb[:, c * D:(c + 1) * D]
    v0 = vec.at[0]

    own_tok.wait()
    for m in range(3):
        load_w(m, wqkv.at[m]).wait()
    for j in range(4):
        if j:
            to_seq_in(0, tok, x_ref, j - 1).wait_recv()
        qkv(x_ref, qit_ref, w, sm, q_ref, k_ref, v_ref, qt_ref, kt_ref, vt_ref, b[0], iv[0], seg(peers[j - 1] if j else z))
    load_w(0, win_c(1)).start(priority=1)
    load_w(1, wout_c(1)).start(priority=1)
    own_cot = pltpu.make_async_copy(cot.at[z], ct_ref.at[seg(z), :], locsem.at[1])
    own_cot.start()
    for j in (1, 2, 0):
        to_seq(1, cot, ct_ref, j).start()
    attn_fwd(qt_ref, k_ref, vt_ref, p_ref, ctxt_ref, len_ref[z])
    load_w(3, wo).wait()
    out_proj(ctxt_ref, x_ref, w.at[3], sm, qct_ref, slc_ref, n1_ref, r1_ref, hid_ref, slh_ref, qh_ref, acc_ref, b[1], iv[1], b[2], iv[2])

    def w_slot(c):
        return 4 * (1 - c % 2)

    def fwd_wait(c):
        load_w(w_slot(c), win_c(c)).wait()
        load_w(w_slot(c) + 1, wout_c(c)).wait()
        return w_slot(c)

    def fwd_done(c):
        @pl.when(c < 2)
        def _():
            load_w(w_slot(c), win_c(c + 2)).start(priority=1)
            load_w(w_slot(c) + 1, wout_c(c + 2)).start(priority=1)

    ffn_fwd(qh_ref, w, sm, act_ref, dfac_ref, acc_ref, b[3], iv[3], fwd_wait, fwd_done)
    own_cot.wait()
    for j in range(3):
        to_seq_in(1, cot, ct_ref, j).wait_recv()
    ln2(acc_ref, hid_ref, ct_ref, sm, gb_ref, v0)
    own_out = pltpu.make_async_copy(ct_ref.at[seg(z), :], outp.at[z], locsem.at[2])
    own_out.start()
    for j in (1, 2, 0):
        to_pos(2, ct_ref, outp, j).start()

    def put_out(c, v):
        fr = 4 * rs
        for h in range(D // fr):
            for j in range(4):
                g[j, c * (D // fr) + h] = v[h * fr + j * rs:h * fr + (j + 1) * rs].astype(BF)

    def put(i, v):
        g[i % 8] = v.astype(BF).reshape(n_dp, rs, D)

    def at_point(point):
        for k, i in SCHEDULE.get(point, ()):
            if k == 9:
                to_pos(3, x_ref, gxp, i).start()
            elif k < nb:
                red_add(i, k)
            else:
                z_add(i, k - nb)
            if i == V_WITH and k != 9:
                v_add(k)

    ffn_bwd_out(gb_ref, act_ref, put_out)
    for i in range(4):
        red(i, 0).start()
    acc_ref[...] = jnp.zeros_like(acc_ref)
    qht = vt_ref.reshape(D, L)
    for p in range(NP):
        qht[p * 128:(p + 1) * 128, :] = qh_ref[:, p * 128:(p + 1) * 128].T
    at_point("fo")
    for j in range(4):
        c = 3 - j
        s = w_slot(c)
        if j >= 2:
            fwd_wait(c)
        ffn_bwd_in(c, gb_ref, w.at[s], w.at[s + 1], dfac_ref, acc_ref, qht, functools.partial(put, 4 + j), v0)
        red(4 + j, 0).start()
        if j < 2:
            load_w(s, win_c(c - 2)).start(priority=1)
            load_w(s + 1, wout_c(c - 2)).start(priority=1)
        if j == 2:
            load_w(0, wqkv.at[0]).start(priority=1)
            load_w(1, wqkv.at[1]).start(priority=1)
        at_point(f"f{j}")
    ln1_bwd(acc_ref, hid_ref, slh_ref, n1_ref, r1_ref, sm, gb_ref, v0)
    at_point("ln")
    dc = LaneSlots(act_ref)
    red(0, 0).wait_send()
    out_bwd(gb_ref, w.at[3], qct_ref, slc_ref, dc, vt_ref, functools.partial(put, 8))
    red(8, 0).start()
    at_point("ob")

    def service(p):
        for at_p in range(NP):
            if f"a{at_p}" in SCHEDULE:
                @pl.when(p == at_p)
                def _():
                    at_point(f"a{at_p}")

    attn_bwd(q_ref, kt_ref, v_ref, dc, vt_ref, p_ref, q_ref, k_ref, v_ref, service)
    for m in (0, 1):
        load_w(m, wqkv.at[m]).wait()
    qkv_bwd_x(x_ref, w, q_ref, k_ref, v_ref, hid_ref, acc_ref, v0, iv[0])
    vcopy(0).start()
    own_gx = pltpu.make_async_copy(x_ref.at[seg(z), :], gxp.at[z], locsem.at[3])
    own_gx.start()
    at_point("x")
    for m, ref in enumerate((q_ref, k_ref, v_ref)):
        red(1 + m, 0).wait_send()
        put(9 + m, nn(qit_ref[...], lanes(ref)))
        red(9 + m, 0).start()
        at_point(f"q{m}")
    at_point("drain")
    for i in range(12):
        z_end(i)
        for k in range(nb):
            if (k, i) not in ((0, 0), (0, 1), (0, 2), (0, 3)):
                red(i, k).wait_send()
    v_end()
    own_out.wait()
    own_gx.wait()
    for j in range(3):
        to_seq(0, tok, x_ref, j).wait_send()
        to_seq(1, cot, ct_ref, j).wait_send()
        to_pos(2, ct_ref, outp, j).wait_send()
        to_pos_in(2, ct_ref, outp, j).wait_recv()
        to_pos(3, x_ref, gxp, j).wait_send()
        to_pos_in(3, x_ref, gxp, j).wait_recv()


def fused(n_dp, *args):
    nb, rs = n_dp.bit_length() - 1, D // n_dp

    def vm(*s, d=BF):
        return pltpu.VMEM(s, d)
    dma = pltpu.SemaphoreType.DMA
    scratch = [vm(12, D, d=F32), vm(6, D, D), vm(8, n_dp, rs, D), vm(L, D), vm(L, D), vm(D, L), vm(6, L, 128), vm(6, L, 128), vm(6, L, 128), vm(6, 128, L),
               vm(6, 128, L), vm(6, 128, L), vm(12, L, L), vm(6, 128, L), vm(D, L), vm(L, D),
               vm(L, D, d=F32), vm(L, 128, d=F32), vm(L, D, d=F32), vm(L, D), vm(L, D), vm(4, L, D), vm(4, L, D), vm(L, D, d=F32),
               vm(L, D), vm(12, rs, D), vm(nb + 2, 16, D, d=F32), vm(nb + 2, 16, D, d=F32)]
    scratch += [vm(*((12,) + (2,) * (nb - k) + (rs, D))) for k in range(1, nb + 1)]
    scratch += [dma((6,)), dma((4,)), dma((4, 3)), dma((4, 3)), dma((nb, 12)), dma((nb, 12)), dma((3, 12)), dma((3, 12)), dma((nb + 3,)), dma((nb + 3,))]
    pos = jax.ShapeDtypeStruct((4, L // 4, D), BF)
    outs = [pos, pos, jax.ShapeDtypeStruct((12, rs, D), BF), jax.ShapeDtypeStruct((16, D), F32)]
    v, s, h = (pl.BlockSpec(memory_space=m) for m in (pltpu.VMEM, pltpu.SMEM, pl.ANY))
    return pl.pallas_call(
        functools.partial(fused_kernel, n_dp), out_shape=outs, in_specs=[h, h, s, s, h, h, h, h] + [v] * 6, out_specs=[h, h, v, v],
        scratch_shapes=scratch,
        compiler_params=pltpu.CompilerParams(collective_id=0, has_side_effects=True, vmem_limit_bytes=64 * 1024 * 1024 - 65536))(*args)


def finish_kernel(n_dp, outp, gxp, gw, vec, out, gx, gqkv, gqvb, gwo, gob, gains, shifts, gwin, gfib, gwout, gfob,
                  seq_in, gw_in, tmp, seq_out, gx_out, gw_out, isem, osem):
    rs = D // n_dp
    i = lax.axis_index("dp")
    ins = [pltpu.make_async_copy(outp, seq_in.at[0], isem.at[0]), pltpu.make_async_copy(gw, gw_in, isem.at[1]),
           pltpu.make_async_copy(gxp, seq_in.at[1], isem.at[2])]
    for c in ins:
        c.start()
    outs = []

    def send(src, dst):
        c = pltpu.make_async_copy(src, dst, osem.at[len(outs)])
        c.start()
        outs.append(c)

    v, fib = vec[0:8, :], vec[8:12, :]
    mine, f = jnp.zeros((8, rs), F32), jnp.zeros((1, 4 * rs), F32)
    per = D // (4 * rs)
    for k in range(n_dp):
        mine = jnp.where(i == k, v[:, k * rs:(k + 1) * rs], mine)
        f = jnp.where(i == k, fib[k // per:k // per + 1, (k % per) * 4 * rs:(k % per + 1) * 4 * rs], f)
    gqvb[...] = mine[0:2]
    gob[...] = mine[2:3]
    gains[...] = mine[3:5]
    shifts[...] = mine[5:7]
    gfob[...] = mine[7:8]
    gfib[...] = f.reshape(4 * rs)
    ins[0].wait()
    for s in range(4):
        tmp[:, s, :] = seq_in[0, s].astype(F32)
    seq_out[...] = tmp[...].astype(BF)
    send(seq_out, out)
    ins[1].wait()
    for k in range(12):
        gw_out[k] = gw_in[k].astype(F32)
        if k < 4:
            send(gw_out.at[k], gwout.at[pl.ds(k * rs, rs), :])
        elif k < 8:
            send(gw_out.at[k], gwin.at[:, pl.ds((7 - k) * D, D)])
        elif k == 8:
            send(gw_out.at[k], gwo)
        else:
            send(gw_out.at[k], gqkv.at[k - 9])
    ins[2].wait()
    for s in range(4):
        gx_out[:, s, :] = seq_in[1, s].astype(F32)
    send(gx_out, gx)
    for c in outs:
        c.wait()


def finish(n_dp, *args):
    rs, seg = D // n_dp, L // 4
    shapes = [((seg, 4, D), BF), ((seg, 4, D), F32)]
    shapes += [(s, F32) for s in ((3, rs, D), (2, rs), (rs, D), (1, rs), (2, rs), (2, rs), (rs, F), (4 * rs,), (4 * rs, D), (1, rs))]
    v, h = pl.BlockSpec(memory_space=pltpu.VMEM), pl.BlockSpec(memory_space=pl.ANY)
    vm, dma = pltpu.VMEM, pltpu.SemaphoreType.DMA
    return pl.pallas_call(
        functools.partial(finish_kernel, n_dp), out_shape=[jax.ShapeDtypeStruct(s, d) for s, d in shapes], in_specs=[h, h, h, v],
        out_specs=[h, h, h, v, h, v, v, v, h, v, h, v],
        scratch_shapes=[vm((2, 4, seg, D), BF), vm((12, rs, D), BF), vm((seg, 4, D), F32), vm((seg, 4, D), BF), vm((seg, 4, D), F32),
                        vm((12, rs, D), F32), dma((3,)), dma((14,))],
        compiler_params=pltpu.CompilerParams(vmem_limit_bytes=60 * 1024 * 1024))(*args)


def on_device(n_dp, tokens, lengths, ranges, qkv_weight, qv_bias, out_weight, out_bias, norm_gains, norm_shifts, ffn_in, ffn_in_bias,
              ffn_out, ffn_out_bias, cotangent):
    res = finish(n_dp, *fused(n_dp, tokens.transpose(1, 0, 2), cotangent.transpose(1, 0, 2), lengths, ranges, qkv_weight, out_weight,
                              ffn_in, ffn_out, qv_bias, out_bias, norm_gains, norm_shifts, ffn_in_bias, ffn_out_bias))
    return tuple(r[0] if n in (5, 11) else r for n, r in enumerate(res))


def local_kernel(x_ref, ct_ref, len_ref, rng_ref, w_ref, sm, gx_ref, g_ref, vec_ref, w, qit_ref, q_ref, k_ref, v_ref, qt_ref, kt_ref, vt_ref,
                 p_ref, ctxt_ref, qct_ref, slc_ref, n1_ref, r1_ref, hid_ref, slh_ref, qh_ref, act_ref, dfac_ref, acc_ref, gb_ref, stage,
                 wsem, gsem):
    def fetch(slot, i):
        cp = pltpu.make_async_copy(w_ref.at[i], w.at[slot], wsem)
        cp.start()
        cp.wait()

    def put(i, v):
        stage[...] = v.astype(BF)
        cp = pltpu.make_async_copy(stage, g_ref.at[i], gsem)
        cp.start()
        cp.wait()

    b = [jnp.full((1, 1), rng_ref[i], jnp.int32).astype(F32) * (1 / 16.0) for i in range(4)]
    iv = [1.0 / t for t in b]
    vec_ref[...] = jnp.zeros_like(vec_ref)
    for m in range(4):
        fetch(m, 8 + (m + 1) % 4 if m < 3 else 8)
    for r in range(0, L, 256):
        qkv(x_ref, qit_ref, w, sm, q_ref, k_ref, v_ref, qt_ref, kt_ref, vt_ref, b[0], iv[0], slice(r, r + 256))
    attn_fwd(qt_ref, k_ref, vt_ref, p_ref, ctxt_ref, len_ref[0])
    out_proj(ctxt_ref, x_ref, w.at[3], sm, qct_ref, slc_ref, n1_ref, r1_ref, hid_ref, slh_ref, qh_ref, acc_ref, b[1], iv[1], b[2], iv[2])

    def before(c):
        fetch(4, c)
        fetch(5, 4 + c)
        return 4

    ffn_fwd(qh_ref, w, sm, act_ref, dfac_ref, acc_ref, b[3], iv[3], before, lambda c: None)
    ln2(acc_ref, hid_ref, ct_ref, sm, gb_ref, vec_ref)
    qht = vt_ref.reshape(D, L)
    for p in range(NP):
        qht[p * 128:(p + 1) * 128, :] = qh_ref[:, p * 128:(p + 1) * 128].T
    ffn_bwd_out(gb_ref, act_ref, lambda c, v: put(4 + c, v))
    acc_ref[...] = jnp.zeros_like(acc_ref)
    for c in range(4):
        before(c)
        ffn_bwd_in(c, gb_ref, w.at[4], w.at[5], dfac_ref, acc_ref, qht, functools.partial(put, c), vec_ref)
    ln1_bwd(acc_ref, hid_ref, slh_ref, n1_ref, r1_ref, sm, gb_ref, vec_ref)
    dc = LaneSlots(act_ref)
    out_bwd(gb_ref, w.at[3], qct_ref, slc_ref, dc, vt_ref, functools.partial(put, 8))
    attn_bwd(q_ref, kt_ref, v_ref, dc, vt_ref, p_ref, q_ref, k_ref, v_ref, lambda p: None)
    qkv_bwd_x(x_ref, w, q_ref, k_ref, v_ref, hid_ref, acc_ref, vec_ref, iv[0])
    for m, ref in enumerate((q_ref, k_ref, v_ref)):
        put(9 + m, nn(qit_ref[...], lanes(ref)))
    gx_ref[...] = x_ref[...]


def local(x, ct, length, ranges, weights, small):
    def vm(*s, d=BF):
        return pltpu.VMEM(s, d)
    scratch = [vm(6, D, D), vm(D, L), vm(6, L, 128), vm(6, L, 128), vm(6, L, 128), vm(6, 128, L),
               vm(6, 128, L), vm(6, 128, L), vm(12, L, L), vm(6, 128, L), vm(D, L), vm(L, D),
               vm(L, D, d=F32), vm(L, 128, d=F32), vm(L, D, d=F32), vm(L, D), vm(L, D), vm(4, L, D), vm(4, L, D), vm(L, D, d=F32),
               vm(L, D), vm(D, D), pltpu.SemaphoreType.DMA, pltpu.SemaphoreType.DMA]
    outs = [jax.ShapeDtypeStruct((L, D), BF), jax.ShapeDtypeStruct((L, D), BF), jax.ShapeDtypeStruct((12, D, D), BF),
            jax.ShapeDtypeStruct((16, D), F32)]
    v, s, h = (pl.BlockSpec(memory_space=m) for m in (pltpu.VMEM, pltpu.SMEM, pl.ANY))

    def body(x_in, ct_in, len_ref, rng_ref, w_ref, sm, out_ref, gx_ref, g_ref, vec_ref, x_ref, *rest):
        x_ref[...] = x_in[...]
        out_ref[...] = ct_in[...]
        local_kernel(x_ref, out_ref, len_ref, rng_ref, w_ref, sm, gx_ref, g_ref, vec_ref, *rest)

    return pl.pallas_call(
        body, out_shape=outs, in_specs=[v, v, s, s, h, v], out_specs=[v, v, h, v], scratch_shapes=[vm(L, D)] + scratch,
        compiler_params=pltpu.CompilerParams(vmem_limit_bytes=60 * 1024 * 1024))(x, ct, length, ranges, weights, small)


def on_device_local(n_dp, tokens, lengths, ranges, qkv_weight, qv_bias, out_weight, out_bias, norm_gains, norm_shifts, ffn_in, ffn_in_bias,
                    ffn_out, ffn_out_bias, cotangent):
    def to_seq(a):
        return lax.all_to_all(a.transpose(1, 0, 2), "head", split_axis=0, concat_axis=1, tiled=True)[0]

    def to_pos(a):
        return lax.all_to_all(a[None], "head", split_axis=1, concat_axis=0, tiled=True).transpose(1, 0, 2)

    small = jnp.concatenate([qv_bias, out_bias[None], norm_gains, norm_shifts, ffn_out_bias[None], ffn_in_bias.reshape(4, D)]).astype(F32)
    weights = jnp.concatenate([ffn_in.reshape(D, 4, D).transpose(1, 0, 2), ffn_out.reshape(4, D, D), out_weight[None], qkv_weight])
    length = lax.dynamic_slice(lengths, (lax.axis_index("head"),), (1,))
    out, gx, g, vec = local(to_seq(tokens), to_seq(cotangent), length, ranges, weights, small)
    rs = D // n_dp
    wout = lax.psum_scatter(g[4:8].reshape(4 * D, D), "dp", scatter_dimension=0, tiled=True)
    rest = lax.psum_scatter(jnp.concatenate([g[0:4], g[8:12]]), "dp", scatter_dimension=1, tiled=True)
    both = lax.psum(jnp.concatenate([wout, rest.reshape(8 * rs, D)]), "head").astype(F32)
    wout, rest = both[:4 * rs], both[4 * rs:].reshape(8, rs, D)
    vec = lax.psum(vec, ("dp", "head"))
    i = lax.axis_index("dp")

    def mine(v):
        return lax.dynamic_slice_in_dim(v, i * rs, rs, axis=-1)
    fib = lax.dynamic_slice(vec[8:12].reshape(-1), (i * 4 * rs,), (4 * rs,))
    return (to_pos(out), to_pos(gx).astype(F32), rest[5:8], mine(vec[0:2]), rest[4], mine(vec[2]), mine(vec[3:5]), mine(vec[5:7]),
            rest[0:4].transpose(1, 0, 2).reshape(rs, F), fib, wout, mine(vec[7]))


def solution(mesh):
    n_dp = mesh.shape["dp"]
    tok = P("head", "dp", None)
    body = on_device if D // n_dp % 16 == 0 else on_device_local
    return jax.shard_map(
        functools.partial(body, n_dp),
        mesh=mesh,
        in_specs=(tok, P("dp")) + (P(),) * 11 + (tok,),
        out_specs=(tok, tok, P(None, "dp", None), P(None, "dp"), P("dp", None), P("dp"), P(None, "dp"), P(None, "dp"),
                   P("dp", None), P("dp"), P("dp", None), P("dp")),
        check_vma=False,
    )
```

```python
import functools
import jax
import jax.numpy as jnp
from jax import lax
from jax.experimental import pallas as pl
from jax.experimental.pallas import tpu as pltpu
from jax.sharding import PartitionSpec as P

F32, BF = jnp.float32, jnp.bfloat16
L, D, F, NP = 512, 768, 3072, 6
GC0, GC1 = 0.7978845608028654, 0.044715


def nn(a, b):
    return lax.dot_general(a, b, (((1,), (0,)), ((), ())), preferred_element_type=F32)


def nt(a, b):
    return lax.dot_general(a, b, (((1,), (1,)), ((), ())), preferred_element_type=F32)


def tn(a, b):
    return lax.dot_general(a, b, (((0,), (0,)), ((), ())), preferred_element_type=F32)


def rows_loop(n, step, f):
    def it(r, c):
        f(pl.multiple_of(r * step, step))
        return c
    lax.fori_loop(0, n // step, it, 0, unroll=2)


def mean(v):
    return jnp.sum(v, axis=-1, keepdims=True) * (1.0 / D)


class LaneSlots:
    def __init__(self, ref):
        self.ref = ref

    def __getitem__(self, p):
        return self.ref[0, :, pl.ds(pl.multiple_of(p * 128, 128), 128)]

    def __setitem__(self, p, value):
        self.ref[0, :, pl.ds(pl.multiple_of(p * 128, 128), 128)] = value


def qkv(x_ref, qit_ref, w_ref, sm, q_ref, k_ref, v_ref, qt_ref, kt_ref, vt_ref, b0, r0, rows):
    xb = x_ref[rows, :].astype(F32)
    qi = (b0 * jnp.tanh(xb * r0)).astype(BF)
    for p in range(NP):
        qit_ref[p * 128:(p + 1) * 128, rows] = qi[:, p * 128:(p + 1) * 128].T
    for m, (dst, tdst) in enumerate(((q_ref, qt_ref), (k_ref, kt_ref), (v_ref, vt_ref))):
        y = nn(qi, w_ref[m])
        if m == 0:
            y = (y + sm[0:1, :]).astype(BF).astype(F32) * 0.125
        if m == 2:
            y = y + sm[1:2, :]
        for p in range(NP):
            yp = y[:, p * 128:(p + 1) * 128].astype(BF)
            dst[p, rows, :] = yp
            tdst[p, :, rows] = yp.T


def attn_fwd(q_t, k_ref, v_t, p_ref, ctxt_ref, length):
    dead = (lax.broadcasted_iota(jnp.int32, (L, 128), 0) >= length) & (lax.broadcasted_iota(jnp.int32, (L, 128), 1) == 0)
    dead = jnp.where(dead, -1e9, 0.0).astype(BF)
    one = (lax.broadcasted_iota(jnp.int32, (128, L), 0) == 0).astype(F32).astype(BF)
    low = lax.broadcasted_iota(jnp.int32, (128, L), 0) < 64

    def pair(p, c):
        kp, qt, vt = jnp.concatenate([k_ref[p], dead], axis=1), q_t[p], v_t[p]
        for t in range(2):
            qm = jnp.where(low if t == 0 else ~low, qt, jnp.zeros_like(qt))
            s = nn(kp, jnp.concatenate([qm, one], axis=0))
            e = jnp.exp(s - jnp.max(s, axis=0, keepdims=True))
            pr = (e * (1.0 / jnp.sum(e, axis=0, keepdims=True))).astype(BF)
            p_ref[2 * p + t] = pr
            ctxt_ref[p, 64 * t:64 * t + 64, :] = nn(vt[64 * t:64 * t + 64, :], pr).astype(BF)
        return c
    lax.fori_loop(0, NP, pair, 0)


def out_proj(ctxt_ref, x_ref, wo_ref, sm, qct_ref, slc_ref, n1_ref, r1_ref, hid_ref, slh_ref, qh_ref, acc_ref, b1, i1, b2, i2):
    for p in range(NP):
        th = jnp.tanh(ctxt_ref[p].astype(F32) * i1)
        qct_ref[p * 128:(p + 1) * 128, :] = (b1 * th).astype(BF)
        slc_ref[:, p * 128:(p + 1) * 128] = (1.0 - th * th).astype(BF).T
    hid_ref[...] = tn(qct_ref[...], wo_ref[...])

    def f(r):
        rows = pl.ds(r, 64)
        v = hid_ref[rows, :] + sm[2:3, :] + x_ref[rows, :].astype(F32)
        c = v - mean(v)
        rr = lax.rsqrt(mean(c * c) + 1e-5)
        n = c * rr
        n1_ref[rows, :] = n
        r1_ref[rows, :] = jnp.broadcast_to(rr, (64, 128))
        h = n * sm[3:4, :] + sm[5:6, :]
        hid_ref[rows, :] = h
        th = jnp.tanh(h * i2)
        qh_ref[rows, :] = (b2 * th).astype(BF)
        slh_ref[rows, :] = (1.0 - th * th).astype(BF)
    rows_loop(L, 64, f)
    acc_ref[...] = jnp.zeros_like(acc_ref)


def ffn_fwd(qh_ref, w, sm, act_ref, dfac_ref, acc_ref, b3, i3, before, after):
    def chunk(c, _):
        s = before(c)
        bias = sm[pl.ds(8 + c, 1), :]
        for r in range(0, L, 256):
            rows = slice(r, r + 256)
            t = nn(qh_ref[rows, :], w[s]) + bias
            t2 = t * t
            th = jnp.tanh(t * (GC0 + (GC0 * GC1) * t2))
            hp = 0.5 + 0.5 * th
            u = t * hp
            cl = jnp.tanh(u * i3)
            act = (b3 * cl).astype(BF)
            d = hp + u * (1.0 - th) * (GC0 + (3 * GC0 * GC1) * t2)
            act_ref[c, rows, :] = act
            dfac_ref[c, rows, :] = (d * (1.0 - cl * cl)).astype(BF)
            acc_ref[rows, :] += nn(act, w[s + 1])
        after(c)
        return _
    lax.fori_loop(0, 4, chunk, 0)


def colsum(vec, row, val):
    vec[row:row + 1, :] += jnp.sum(val, axis=0, keepdims=True)


def ln2(acc_ref, hid_ref, ct_ref, sm, gb_ref, vec):
    def f(r):
        rows = pl.ds(r, 64)
        v = acc_ref[rows, :] + sm[7:8, :] + hid_ref[rows, :]
        c = v - mean(v)
        rr = lax.rsqrt(mean(c * c) + 1e-5)
        n = c * rr
        ct = ct_ref[rows, :].astype(F32)
        ct_ref[rows, :] = (n * sm[4:5, :] + sm[6:7, :]).astype(BF)
        colsum(vec, 4, ct * n)
        colsum(vec, 6, ct)
        q = ct * sm[4:5, :]
        gs = rr * (q - mean(q) - n * mean(q * n))
        hid_ref[rows, :] = gs
        gb = gs.astype(BF)
        gb_ref[rows, :] = gb
        colsum(vec, 7, gb.astype(F32))
    rows_loop(L, 64, f)


def ffn_bwd_out(gb_ref, act_ref, put):
    def chunk(c, _):
        put(c, tn(act_ref[c], gb_ref[...]))
        return _
    lax.fori_loop(0, 4, chunk, 0)


def ffn_bwd_in(c, gb_ref, win, wout, dfac_ref, acc_ref, qht_ref, put, vec):
    for r in range(0, L, 256):
        rows = slice(r, r + 256)
        gp = (nt(gb_ref[rows, :], wout[...]) * dfac_ref[c, rows, :].astype(F32)).astype(BF)
        dfac_ref[c, rows, :] = gp
        vec[pl.ds(8 + c, 1), :] += jnp.sum(gp.astype(F32), axis=0, keepdims=True)
        acc_ref[rows, :] += nt(gp, win[...])
    put(nn(qht_ref[...], dfac_ref[c]))


def ln1_bwd(acc_ref, gs_ref, slh_ref, n1_ref, r1_ref, sm, gat_ref, vec):
    def f(r):
        rows = pl.ds(r, 64)
        gh = gs_ref[rows, :] + acc_ref[rows, :] * slh_ref[rows, :].astype(F32)
        n = n1_ref[rows, :]
        colsum(vec, 3, gh * n)
        colsum(vec, 5, gh)
        q = gh * sm[3:4, :]
        gs = r1_ref[rows, 0:1] * (q - mean(q) - n * mean(q * n))
        gs_ref[rows, :] = gs
        gat = gs.astype(BF)
        gat_ref[rows, :] = gat
        colsum(vec, 2, gat.astype(F32))
    rows_loop(L, 64, f)


def out_bwd(gat_ref, wo_ref, qct_ref, slc_ref, dc_ref, dct_ref, put):
    put(nn(qct_ref[...], gat_ref[...]))
    g = nt(gat_ref[...], wo_ref[...])
    for p in range(NP):
        cols = slice(p * 128, (p + 1) * 128)
        d = (g[:, cols] * slc_ref[:, cols].astype(F32)).astype(BF)
        dc_ref[p] = d
        dct_ref[p] = d.T


def attn_bwd(q_ref, k_t, v_ref, dc_ref, dc_t, p_ref, dq_ref, dk_ref, dv_ref, service):
    low = lax.broadcasted_iota(jnp.int32, (128, L), 0) < 64
    lane_low = lax.broadcasted_iota(jnp.int32, (L, 128), 1) < 64

    def pair(p, c):
        qp, kt, vp, dc, dct = q_ref[p], k_t[p], v_ref[p], dc_ref[p], dc_t[p]
        res = []
        for t in range(2):
            dm = jnp.where(low if t == 0 else ~low, dct, jnp.zeros_like(dct))
            dp = nn(vp, dm)
            pr = p_ref[2 * p + t]
            prf = pr.astype(F32)
            delta = jnp.sum(dp * prf, axis=0, keepdims=True)
            ds = (prf * (dp - delta)).astype(BF)
            res.append((nn(pr, dc), nn(ds, qp), nn(kt[64 * t:64 * t + 64, :], ds) * 0.125))
        dv_ref[p] = jnp.where(lane_low, res[0][0], res[1][0]).astype(BF)
        dk_ref[p] = jnp.where(lane_low, res[0][1], res[1][1]).astype(BF)
        dq_ref[p] = jnp.concatenate([res[0][2], res[1][2]], axis=0).astype(BF).T
        service(p)
        return c
    lax.fori_loop(0, NP, pair, 0)


def lanes(ref):
    return jnp.concatenate([ref[p] for p in range(NP)], axis=1)


def qkv_bwd_x(x_ref, w_ref, dq_ref, dk_ref, dv_ref, gs_ref, acc_ref, vec, i0):
    for m, ref in enumerate((dq_ref, dk_ref, dv_ref)):
        d = lanes(ref)
        if m != 1:
            colsum(vec, m // 2, d.astype(F32))
        if m == 0:
            acc_ref[...] = nt(d, w_ref[m])
        else:
            acc_ref[...] += nt(d, w_ref[m])

    def f(r):
        rows = pl.ds(r, 64)
        th = jnp.tanh(x_ref[rows, :].astype(F32) * i0)
        x_ref[rows, :] = (gs_ref[rows, :] + acc_ref[rows, :] * (1.0 - th * th)).astype(BF)
    rows_loop(L, 64, f)


MESH = pl.DeviceIdType.MESH
SCHEDULE = {
    "fo": [(0, 0), (0, 1)],
    "f2": [(0, 4)],
    "ln": [(1, 0), (0, 5)],
    "a0": [(1, 1)],
    "a1": [(2, 0), (0, 7), (0, 3), (0, 6)],
    "a3": [(2, 1)],
    "a5": [(3, 0), (1, 5)],
    "x": [(9, 1), (0, 2), (4, 0)],
    "q0": [(9, 2), (1, 4), (2, 5), (0, 9), (1, 7)],
    "q1": [(0, 8), (3, 5), (1, 2), (9, 0), (3, 1), (1, 3)],
    "q2": [(2, 7), (4, 5), (0, 11), (1, 9)],
    "drain": [(3, 7), (2, 4), (4, 1), (2, 2), (0, 10), (2, 3), (3, 4), (2, 9), (4, 7), (3, 2), (1, 6), (4, 4), (3, 3), (1, 8),
        (1, 11), (4, 2), (1, 10), (3, 9), (2, 6), (4, 3), (2, 11), (3, 6), (4, 9), (3, 11), (2, 10), (2, 8), (4, 6), (3, 10), (4, 11),
        (3, 8), (4, 10), (4, 8)],
}
V_WITH = 9


def fused_kernel(n_dp, tok, cot, len_ref, rng_ref, wqkv, wo, win, wout, qvb, ob, gains, shifts, fib, fob,
                 outp, gxp, gw, vout,
                 sm, w, g, x_ref, ct_ref, qit_ref, q_ref, k_ref, v_ref, qt_ref, kt_ref, vt_ref, p_ref, ctxt_ref, qct_ref, slc_ref,
                 n1_ref, r1_ref, hid_ref, slh_ref, qh_ref, act_ref, dfac_ref, acc_ref, gb_ref, za, vec, vrecv, *rest):
    nb = n_dp.bit_length() - 1
    bufs, (wsem, locsem, a2s, a2r, gs_sem, gr_sem, zs_sem, zr_sem, vs_sem, vr_sem) = rest[:nb], rest[nb:]
    rs, nz, SEG = D // n_dp, 4, L // 4
    dp, z = lax.axis_index("dp"), lax.axis_index("head")
    bit = [(dp // (1 << b)) % 2 for b in range(nb)]
    buddy = [dp + (1 - 2 * bit[b]) * (1 << b) for b in range(nb)]
    z_near, z_cross, z_far = z + 1 - 2 * (z % 2), 3 - z, (z + 2) % 4
    peers = (z_near, z_far, z_cross)
    inner = (z + 1) // 2 == 1

    def at(dpi, zi):
        return {"dp": dpi, "head": zi}

    def load_w(slot, src):
        return pltpu.make_async_copy(src, w.at[slot], wsem.at[slot])

    def win_c(c):
        return win.at[:, pl.ds(pl.multiple_of(c * D, D), D)]

    def wout_c(c):
        return wout.at[pl.ds(pl.multiple_of(c * D, D), D), :]

    def seg(i):
        return pl.ds(pl.multiple_of(i * SEG, SEG), SEG)

    def to_seq(n, src, dst, j):
        return pltpu.make_async_remote_copy(src.at[peers[j]], dst.at[seg(z), :], a2s.at[n, j], a2r.at[n, j], device_id=at(dp, peers[j]),
                                            device_id_type=MESH)

    def to_seq_in(n, src, dst, j):
        return pltpu.make_async_remote_copy(src.at[peers[j]], dst.at[seg(peers[j]), :], a2s.at[n, j], a2r.at[n, j],
                                            device_id=at(dp, peers[j]), device_id_type=MESH)

    def to_pos(n, src, dst, j):
        return pltpu.make_async_remote_copy(src.at[seg(peers[j]), :], dst.at[z], a2s.at[n, j], a2r.at[n, j], device_id=at(dp, peers[j]),
                                            device_id_type=MESH)

    def to_pos_in(n, src, dst, j):
        return pltpu.make_async_remote_copy(src.at[seg(peers[j]), :], dst.at[peers[j]], a2s.at[n, j], a2r.at[n, j],
                                            device_id=at(dp, peers[j]), device_id_type=MESH)

    full = [g.reshape(*((8,) + (2,) * nb + (rs, D)))] + list(bufs)

    def order(i):
        up = list(range(1, nb))
        return [0] + (up if i % 2 == 0 else up[::-1])

    def slot(i, k):
        return i % 8 if k < 1 else i

    def pick(i, k, **vals):
        left = sorted(set(range(nb)) - set(order(i)[:k]), reverse=True)
        return (slot(i, k),) + tuple(vals.get(f"b{b}", slice(None)) for b in left)

    def red(i, k):
        b = order(i)[k]
        return pltpu.make_async_remote_copy(full[k].at[pick(i, k, **{f"b{b}": 1 - bit[b]})], full[k + 1].at[slot(i, k + 1)], gs_sem.at[k, i],
                                            gr_sem.at[k, i], device_id=at(buddy[b], z), device_id_type=MESH)

    def red_add(i, k):
        b = order(i)[k]
        red(i, k).wait_recv()
        if k + 1 < nb:
            n = order(i)[k + 1]
            for val in (1 - bit[n], bit[n]):
                d = pick(i, k + 1, **{f"b{n}": val})
                s = pick(i, k, **{f"b{b}": bit[b], f"b{n}": val})
                full[k + 1][d] = full[k + 1][d] + full[k][s]
                if val is not bit[n]:
                    red(i, k + 1).start()
        else:
            full[nb][i] = full[nb][i] + full[k][pick(i, k, **{f"b{b}": bit[b]})]
            pl.when(jnp.logical_not(inner))(zcopy(i, 0).start)

    def zcopy(i, k):
        src, dst, to = ((bufs[nb - 1], za, z_near), (za, gw, z_cross), (gw, gw, z_near))[k]
        return pltpu.make_async_remote_copy(src.at[i], dst.at[i], zs_sem.at[k, i], zr_sem.at[k, i], device_id=at(dp, to), device_id_type=MESH)

    def z_add(i, k):
        @pl.when(inner)
        def _():
            zcopy(i, k).wait_recv()
            if k == 0:
                za[i] = za[i] + bufs[nb - 1][i]
                zcopy(i, 1).start()
            else:
                gw[i] = gw[i] + za[i]
                zcopy(i, 2).start()

    def z_end(i):
        @pl.when(inner)
        def _():
            zcopy(i, 1).wait_send()
            zcopy(i, 2).wait_send()

        @pl.when(jnp.logical_not(inner))
        def _():
            zcopy(i, 2).wait_recv()
            zcopy(i, 0).wait_send()

    def vcopy(k):
        if k < nb:
            src, dst, to = vec.at[k], vrecv.at[k], at(buddy[order(V_WITH)[k]], z)
        else:
            src, dst, to = ((vec.at[nb], vrecv.at[nb], at(dp, z_near)), (vec.at[nb + 1], vrecv.at[nb + 1], at(dp, z_cross)),
                            (vout, vout, at(dp, z_near)))[k - nb]
        return pltpu.make_async_remote_copy(src, dst, vs_sem.at[k], vr_sem.at[k], device_id=to, device_id_type=MESH)

    def v_add(k):
        if k < nb:
            vcopy(k).wait_recv()
            vec[k + 1] = vec[k] + vrecv[k]
            if k + 1 < nb:
                vcopy(k + 1).start()
            else:
                pl.when(jnp.logical_not(inner))(vcopy(nb).start)
        else:
            @pl.when(inner)
            def _():
                vcopy(k).wait_recv()
                if k == nb:
                    vec[nb + 1] = vec[nb] + vrecv[nb]
                    vcopy(nb + 1).start()
                else:
                    vout[...] = vec[nb + 1] + vrecv[nb + 1]
                    vcopy(nb + 2).start()

    def v_end():
        for k in range(nb):
            vcopy(k).wait_send()

        @pl.when(inner)
        def _():
            vcopy(nb + 1).wait_send()
            vcopy(nb + 2).wait_send()

        @pl.when(jnp.logical_not(inner))
        def _():
            vcopy(nb).wait_send()
            vcopy(nb + 2).wait_recv()

    for m in range(3):
        load_w(m, wqkv.at[m]).start(priority=1)
    own_tok = pltpu.make_async_copy(tok.at[z], x_ref.at[seg(z), :], locsem.at[0])
    own_tok.start()
    load_w(3, wo).start(priority=1)
    load_w(4, win_c(0)).start(priority=1)
    load_w(5, wout_c(0)).start(priority=1)
    barrier = pltpu.get_barrier_semaphore()
    others = [at(buddy[b], z) for b in range(nb)] + [at(dp, p) for p in peers]
    for o in others:
        pl.semaphore_signal(barrier, inc=1, device_id=o, device_id_type=MESH)
    pl.semaphore_wait(barrier, len(others))
    for j in (1, 2, 0):
        to_seq(0, tok, x_ref, j).start()
    b = [jnp.full((1, 1), rng_ref[i], jnp.int32).astype(F32) * (1 / 16.0) for i in range(4)]
    iv = [1.0 / t for t in b]
    vec[0] = jnp.zeros_like(vec[0])
    sm[0:2, :] = qvb[...].astype(F32)
    sm[2:3, :] = ob[...].astype(F32).reshape(1, D)
    sm[3:5, :] = gains[...].astype(F32)
    sm[5:7, :] = shifts[...].astype(F32)
    sm[7:8, :] = fob[...].astype(F32).reshape(1, D)
    ffb = fib[...].astype(F32).reshape(1, F)
    for c in range(4):
        sm[8 + c:9 + c, :] = ffb[:, c * D:(c + 1) * D]
    v0 = vec.at[0]

    own_tok.wait()
    for m in range(3):
        load_w(m, wqkv.at[m]).wait()
    for j in range(4):
        if j:
            to_seq_in(0, tok, x_ref, j - 1).wait_recv()
        qkv(x_ref, qit_ref, w, sm, q_ref, k_ref, v_ref, qt_ref, kt_ref, vt_ref, b[0], iv[0], seg(peers[j - 1] if j else z))
    load_w(0, win_c(1)).start(priority=1)
    load_w(1, wout_c(1)).start(priority=1)
    own_cot = pltpu.make_async_copy(cot.at[z], ct_ref.at[seg(z), :], locsem.at[1])
    own_cot.start()
    for j in (1, 2, 0):
        to_seq(1, cot, ct_ref, j).start()
    attn_fwd(qt_ref, k_ref, vt_ref, p_ref, ctxt_ref, len_ref[z])
    load_w(3, wo).wait()
    out_proj(ctxt_ref, x_ref, w.at[3], sm, qct_ref, slc_ref, n1_ref, r1_ref, hid_ref, slh_ref, qh_ref, acc_ref, b[1], iv[1], b[2], iv[2])

    def w_slot(c):
        return 4 * (1 - c % 2)

    def fwd_wait(c):
        load_w(w_slot(c), win_c(c)).wait()
        load_w(w_slot(c) + 1, wout_c(c)).wait()
        return w_slot(c)

    def fwd_done(c):
        @pl.when(c < 2)
        def _():
            load_w(w_slot(c), win_c(c + 2)).start(priority=1)
            load_w(w_slot(c) + 1, wout_c(c + 2)).start(priority=1)

    ffn_fwd(qh_ref, w, sm, act_ref, dfac_ref, acc_ref, b[3], iv[3], fwd_wait, fwd_done)
    own_cot.wait()
    for j in range(3):
        to_seq_in(1, cot, ct_ref, j).wait_recv()
    ln2(acc_ref, hid_ref, ct_ref, sm, gb_ref, v0)
    own_out = pltpu.make_async_copy(ct_ref.at[seg(z), :], outp.at[z], locsem.at[2])
    own_out.start()
    for j in (1, 2, 0):
        to_pos(2, ct_ref, outp, j).start()

    def put_out(c, v):
        fr = 4 * rs
        for h in range(D // fr):
            for j in range(4):
                g[j, c * (D // fr) + h] = v[h * fr + j * rs:h * fr + (j + 1) * rs].astype(BF)

    def put(i, v):
        g[i % 8] = v.astype(BF).reshape(n_dp, rs, D)

    def at_point(point):
        for k, i in SCHEDULE.get(point, ()):
            if k == 9:
                to_pos(3, x_ref, gxp, i).start()
            elif k < nb:
                red_add(i, k)
            else:
                z_add(i, k - nb)
            if i == V_WITH and k != 9:
                v_add(k)

    ffn_bwd_out(gb_ref, act_ref, put_out)
    for i in range(4):
        red(i, 0).start()
    acc_ref[...] = jnp.zeros_like(acc_ref)
    qht = vt_ref.reshape(D, L)
    for p in range(NP):
        qht[p * 128:(p + 1) * 128, :] = qh_ref[:, p * 128:(p + 1) * 128].T
    at_point("fo")
    for j in range(4):
        c = 3 - j
        s = w_slot(c)
        if j >= 2:
            fwd_wait(c)
        ffn_bwd_in(c, gb_ref, w.at[s], w.at[s + 1], dfac_ref, acc_ref, qht, functools.partial(put, 4 + j), v0)
        red(4 + j, 0).start()
        if j < 2:
            load_w(s, win_c(c - 2)).start(priority=1)
            load_w(s + 1, wout_c(c - 2)).start(priority=1)
        if j == 2:
            load_w(0, wqkv.at[0]).start(priority=1)
            load_w(1, wqkv.at[1]).start(priority=1)
        at_point(f"f{j}")
    ln1_bwd(acc_ref, hid_ref, slh_ref, n1_ref, r1_ref, sm, gb_ref, v0)
    at_point("ln")
    dc = LaneSlots(act_ref)
    red(0, 0).wait_send()
    out_bwd(gb_ref, w.at[3], qct_ref, slc_ref, dc, vt_ref, functools.partial(put, 8))
    red(8, 0).start()
    at_point("ob")

    def service(p):
        for at_p in range(NP):
            if f"a{at_p}" in SCHEDULE:
                @pl.when(p == at_p)
                def _():
                    at_point(f"a{at_p}")

    attn_bwd(q_ref, kt_ref, v_ref, dc, vt_ref, p_ref, q_ref, k_ref, v_ref, service)
    for m in (0, 1):
        load_w(m, wqkv.at[m]).wait()
    qkv_bwd_x(x_ref, w, q_ref, k_ref, v_ref, hid_ref, acc_ref, v0, iv[0])
    vcopy(0).start()
    own_gx = pltpu.make_async_copy(x_ref.at[seg(z), :], gxp.at[z], locsem.at[3])
    own_gx.start()
    at_point("x")
    for m, ref in enumerate((q_ref, k_ref, v_ref)):
        red(1 + m, 0).wait_send()
        put(9 + m, nn(qit_ref[...], lanes(ref)))
        red(9 + m, 0).start()
        at_point(f"q{m}")
    at_point("drain")
    for i in range(12):
        z_end(i)
        for k in range(nb):
            if (k, i) not in ((0, 0), (0, 1), (0, 2), (0, 3)):
                red(i, k).wait_send()
    v_end()
    own_out.wait()
    own_gx.wait()
    for j in range(3):
        to_seq(0, tok, x_ref, j).wait_send()
        to_seq(1, cot, ct_ref, j).wait_send()
        to_pos(2, ct_ref, outp, j).wait_send()
        to_pos_in(2, ct_ref, outp, j).wait_recv()
        to_pos(3, x_ref, gxp, j).wait_send()
        to_pos_in(3, x_ref, gxp, j).wait_recv()


def fused(n_dp, *args):
    nb, rs = n_dp.bit_length() - 1, D // n_dp

    def vm(*s, d=BF):
        return pltpu.VMEM(s, d)
    dma = pltpu.SemaphoreType.DMA
    scratch = [vm(12, D, d=F32), vm(6, D, D), vm(8, n_dp, rs, D), vm(L, D), vm(L, D), vm(D, L), vm(6, L, 128), vm(6, L, 128), vm(6, L, 128), vm(6, 128, L),
               vm(6, 128, L), vm(6, 128, L), vm(12, L, L), vm(6, 128, L), vm(D, L), vm(L, D),
               vm(L, D, d=F32), vm(L, 128, d=F32), vm(L, D, d=F32), vm(L, D), vm(L, D), vm(4, L, D), vm(4, L, D), vm(L, D, d=F32),
               vm(L, D), vm(12, rs, D), vm(nb + 2, 16, D, d=F32), vm(nb + 2, 16, D, d=F32)]
    scratch += [vm(*((12,) + (2,) * (nb - k) + (rs, D))) for k in range(1, nb + 1)]
    scratch += [dma((6,)), dma((4,)), dma((4, 3)), dma((4, 3)), dma((nb, 12)), dma((nb, 12)), dma((3, 12)), dma((3, 12)), dma((nb + 3,)), dma((nb + 3,))]
    pos = jax.ShapeDtypeStruct((4, L // 4, D), BF)
    outs = [pos, pos, jax.ShapeDtypeStruct((12, rs, D), BF), jax.ShapeDtypeStruct((16, D), F32)]
    v, s, h = (pl.BlockSpec(memory_space=m) for m in (pltpu.VMEM, pltpu.SMEM, pl.ANY))
    return pl.pallas_call(
        functools.partial(fused_kernel, n_dp), out_shape=outs, in_specs=[h, h, s, s, h, h, h, h] + [v] * 6, out_specs=[h, h, v, v],
        scratch_shapes=scratch,
        compiler_params=pltpu.CompilerParams(collective_id=0, has_side_effects=True, vmem_limit_bytes=64 * 1024 * 1024 - 65536))(*args)


def finish_kernel(n_dp, outp, gxp, gw, vec, out, gx, gqkv, gqvb, gwo, gob, gains, shifts, gwin, gfib, gwout, gfob,
                  seq_in, gw_in, tmp, seq_out, gx_out, gw_out, isem, osem):
    rs = D // n_dp
    i = lax.axis_index("dp")
    ins = [pltpu.make_async_copy(outp, seq_in.at[0], isem.at[0]), pltpu.make_async_copy(gw, gw_in, isem.at[1]),
           pltpu.make_async_copy(gxp, seq_in.at[1], isem.at[2])]
    for c in ins:
        c.start()
    outs = []

    def send(src, dst):
        c = pltpu.make_async_copy(src, dst, osem.at[len(outs)])
        c.start()
        outs.append(c)

    v, fib = vec[0:8, :], vec[8:12, :]
    mine, f = jnp.zeros((8, rs), F32), jnp.zeros((1, 4 * rs), F32)
    per = D // (4 * rs)
    for k in range(n_dp):
        mine = jnp.where(i == k, v[:, k * rs:(k + 1) * rs], mine)
        f = jnp.where(i == k, fib[k // per:k // per + 1, (k % per) * 4 * rs:(k % per + 1) * 4 * rs], f)
    gqvb[...] = mine[0:2]
    gob[...] = mine[2:3]
    gains[...] = mine[3:5]
    shifts[...] = mine[5:7]
    gfob[...] = mine[7:8]
    gfib[...] = f.reshape(4 * rs)
    ins[0].wait()
    for s in range(4):
        tmp[:, s, :] = seq_in[0, s].astype(F32)
    seq_out[...] = tmp[...].astype(BF)
    send(seq_out, out)
    ins[1].wait()
    for k in range(12):
        gw_out[k] = gw_in[k].astype(F32)
        if k < 4:
            send(gw_out.at[k], gwout.at[pl.ds(k * rs, rs), :])
        elif k < 8:
            send(gw_out.at[k], gwin.at[:, pl.ds((7 - k) * D, D)])
        elif k == 8:
            send(gw_out.at[k], gwo)
        else:
            send(gw_out.at[k], gqkv.at[k - 9])
    ins[2].wait()
    for s in range(4):
        gx_out[:, s, :] = seq_in[1, s].astype(F32)
    send(gx_out, gx)
    for c in outs:
        c.wait()


def finish(n_dp, *args):
    rs, seg = D // n_dp, L // 4
    shapes = [((seg, 4, D), BF), ((seg, 4, D), F32)]
    shapes += [(s, F32) for s in ((3, rs, D), (2, rs), (rs, D), (1, rs), (2, rs), (2, rs), (rs, F), (4 * rs,), (4 * rs, D), (1, rs))]
    v, h = pl.BlockSpec(memory_space=pltpu.VMEM), pl.BlockSpec(memory_space=pl.ANY)
    vm, dma = pltpu.VMEM, pltpu.SemaphoreType.DMA
    return pl.pallas_call(
        functools.partial(finish_kernel, n_dp), out_shape=[jax.ShapeDtypeStruct(s, d) for s, d in shapes], in_specs=[h, h, h, v],
        out_specs=[h, h, h, v, h, v, v, v, h, v, h, v],
        scratch_shapes=[vm((2, 4, seg, D), BF), vm((12, rs, D), BF), vm((seg, 4, D), F32), vm((seg, 4, D), BF), vm((seg, 4, D), F32),
                        vm((12, rs, D), F32), dma((3,)), dma((14,))],
        compiler_params=pltpu.CompilerParams(vmem_limit_bytes=60 * 1024 * 1024))(*args)


def on_device(n_dp, tokens, lengths, ranges, qkv_weight, qv_bias, out_weight, out_bias, norm_gains, norm_shifts, ffn_in, ffn_in_bias,
              ffn_out, ffn_out_bias, cotangent):
    res = finish(n_dp, *fused(n_dp, tokens.transpose(1, 0, 2), cotangent.transpose(1, 0, 2), lengths, ranges, qkv_weight, out_weight,
                              ffn_in, ffn_out, qv_bias, out_bias, norm_gains, norm_shifts, ffn_in_bias, ffn_out_bias))
    return tuple(r[0] if n in (5, 11) else r for n, r in enumerate(res))


def local_kernel(x_ref, ct_ref, len_ref, rng_ref, w_ref, sm, gx_ref, g_ref, vec_ref, w, qit_ref, q_ref, k_ref, v_ref, qt_ref, kt_ref, vt_ref,
                 p_ref, ctxt_ref, qct_ref, slc_ref, n1_ref, r1_ref, hid_ref, slh_ref, qh_ref, act_ref, dfac_ref, acc_ref, gb_ref, stage,
                 wsem, gsem):
    def fetch(slot, i):
        cp = pltpu.make_async_copy(w_ref.at[i], w.at[slot], wsem)
        cp.start()
        cp.wait()

    def put(i, v):
        stage[...] = v.astype(BF)
        cp = pltpu.make_async_copy(stage, g_ref.at[i], gsem)
        cp.start()
        cp.wait()

    b = [jnp.full((1, 1), rng_ref[i], jnp.int32).astype(F32) * (1 / 16.0) for i in range(4)]
    iv = [1.0 / t for t in b]
    vec_ref[...] = jnp.zeros_like(vec_ref)
    for m in range(4):
        fetch(m, 8 + (m + 1) % 4 if m < 3 else 8)
    for r in range(0, L, 256):
        qkv(x_ref, qit_ref, w, sm, q_ref, k_ref, v_ref, qt_ref, kt_ref, vt_ref, b[0], iv[0], slice(r, r + 256))
    attn_fwd(qt_ref, k_ref, vt_ref, p_ref, ctxt_ref, len_ref[0])
    out_proj(ctxt_ref, x_ref, w.at[3], sm, qct_ref, slc_ref, n1_ref, r1_ref, hid_ref, slh_ref, qh_ref, acc_ref, b[1], iv[1], b[2], iv[2])

    def before(c):
        fetch(4, c)
        fetch(5, 4 + c)
        return 4

    ffn_fwd(qh_ref, w, sm, act_ref, dfac_ref, acc_ref, b[3], iv[3], before, lambda c: None)
    ln2(acc_ref, hid_ref, ct_ref, sm, gb_ref, vec_ref)
    qht = vt_ref.reshape(D, L)
    for p in range(NP):
        qht[p * 128:(p + 1) * 128, :] = qh_ref[:, p * 128:(p + 1) * 128].T
    ffn_bwd_out(gb_ref, act_ref, lambda c, v: put(4 + c, v))
    acc_ref[...] = jnp.zeros_like(acc_ref)
    for c in range(4):
        before(c)
        ffn_bwd_in(c, gb_ref, w.at[4], w.at[5], dfac_ref, acc_ref, qht, functools.partial(put, c), vec_ref)
    ln1_bwd(acc_ref, hid_ref, slh_ref, n1_ref, r1_ref, sm, gb_ref, vec_ref)
    dc = LaneSlots(act_ref)
    out_bwd(gb_ref, w.at[3], qct_ref, slc_ref, dc, vt_ref, functools.partial(put, 8))
    attn_bwd(q_ref, kt_ref, v_ref, dc, vt_ref, p_ref, q_ref, k_ref, v_ref, lambda p: None)
    qkv_bwd_x(x_ref, w, q_ref, k_ref, v_ref, hid_ref, acc_ref, vec_ref, iv[0])
    for m, ref in enumerate((q_ref, k_ref, v_ref)):
        put(9 + m, nn(qit_ref[...], lanes(ref)))
    gx_ref[...] = x_ref[...]


def local(x, ct, length, ranges, weights, small):
    def vm(*s, d=BF):
        return pltpu.VMEM(s, d)
    scratch = [vm(6, D, D), vm(D, L), vm(6, L, 128), vm(6, L, 128), vm(6, L, 128), vm(6, 128, L),
               vm(6, 128, L), vm(6, 128, L), vm(12, L, L), vm(6, 128, L), vm(D, L), vm(L, D),
               vm(L, D, d=F32), vm(L, 128, d=F32), vm(L, D, d=F32), vm(L, D), vm(L, D), vm(4, L, D), vm(4, L, D), vm(L, D, d=F32),
               vm(L, D), vm(D, D), pltpu.SemaphoreType.DMA, pltpu.SemaphoreType.DMA]
    outs = [jax.ShapeDtypeStruct((L, D), BF), jax.ShapeDtypeStruct((L, D), BF), jax.ShapeDtypeStruct((12, D, D), BF),
            jax.ShapeDtypeStruct((16, D), F32)]
    v, s, h = (pl.BlockSpec(memory_space=m) for m in (pltpu.VMEM, pltpu.SMEM, pl.ANY))

    def body(x_in, ct_in, len_ref, rng_ref, w_ref, sm, out_ref, gx_ref, g_ref, vec_ref, x_ref, *rest):
        x_ref[...] = x_in[...]
        out_ref[...] = ct_in[...]
        local_kernel(x_ref, out_ref, len_ref, rng_ref, w_ref, sm, gx_ref, g_ref, vec_ref, *rest)

    return pl.pallas_call(
        body, out_shape=outs, in_specs=[v, v, s, s, h, v], out_specs=[v, v, h, v], scratch_shapes=[vm(L, D)] + scratch,
        compiler_params=pltpu.CompilerParams(vmem_limit_bytes=60 * 1024 * 1024))(x, ct, length, ranges, weights, small)


def on_device_local(n_dp, tokens, lengths, ranges, qkv_weight, qv_bias, out_weight, out_bias, norm_gains, norm_shifts, ffn_in, ffn_in_bias,
                    ffn_out, ffn_out_bias, cotangent):
    def to_seq(a):
        return lax.all_to_all(a.transpose(1, 0, 2), "head", split_axis=0, concat_axis=1, tiled=True)[0]

    def to_pos(a):
        return lax.all_to_all(a[None], "head", split_axis=1, concat_axis=0, tiled=True).transpose(1, 0, 2)

    small = jnp.concatenate([qv_bias, out_bias[None], norm_gains, norm_shifts, ffn_out_bias[None], ffn_in_bias.reshape(4, D)]).astype(F32)
    weights = jnp.concatenate([ffn_in.reshape(D, 4, D).transpose(1, 0, 2), ffn_out.reshape(4, D, D), out_weight[None], qkv_weight])
    length = lax.dynamic_slice(lengths, (lax.axis_index("head"),), (1,))
    out, gx, g, vec = local(to_seq(tokens), to_seq(cotangent), length, ranges, weights, small)
    rs = D // n_dp
    wout = lax.psum_scatter(g[4:8].reshape(4 * D, D), "dp", scatter_dimension=0, tiled=True)
    rest = lax.psum_scatter(jnp.concatenate([g[0:4], g[8:12]]), "dp", scatter_dimension=1, tiled=True)
    both = lax.psum(jnp.concatenate([wout, rest.reshape(8 * rs, D)]), "head").astype(F32)
    wout, rest = both[:4 * rs], both[4 * rs:].reshape(8, rs, D)
    vec = lax.psum(vec, ("dp", "head"))
    i = lax.axis_index("dp")

    def mine(v):
        return lax.dynamic_slice_in_dim(v, i * rs, rs, axis=-1)
    fib = lax.dynamic_slice(vec[8:12].reshape(-1), (i * 4 * rs,), (4 * rs,))
    return (to_pos(out), to_pos(gx).astype(F32), rest[5:8], mine(vec[0:2]), rest[4], mine(vec[2]), mine(vec[3:5]), mine(vec[5:7]),
            rest[0:4].transpose(1, 0, 2).reshape(rs, F), fib, wout, mine(vec[7]))


def solution(mesh):
    n_dp = mesh.shape["dp"]
    tok = P("head", "dp", None)
    body = on_device if D // n_dp % 16 == 0 else on_device_local
    return jax.shard_map(
        functools.partial(body, n_dp),
        mesh=mesh,
        in_specs=(tok, P("dp")) + (P(),) * 11 + (tok,),
        out_specs=(tok, tok, P(None, "dp", None), P(None, "dp"), P("dp", None), P("dp"), P(None, "dp"), P(None, "dp"),
                   P("dp", None), P("dp"), P("dp", None), P("dp")),
        check_vma=False,
    )
```
